256 devices in a mesh: tm: 8 (over z), gx: 16 (over x, y_hi, core), gy: 2 (over y_lo).
Axes of the slice: x: 4, y: 4 (y_hi: 2, y_lo: 2; y = y_hi * 2 + y_lo), z: 8, core: 2. Of those that a mesh axis runs over, the one named last changes fastest.
Arguments:
- lagrange: float32 [16, 8, 1024, 256], P('tm', None, 'gx', 'gy'), may hold values from -6 to 6
- obs_lagrange: float32 [16, 16, 2, 1024], P('tm', 'gx', 'gy'), may hold values from -6 to 6
- increment: float32 [16, 8, 1024, 256], P('tm', None, 'gx', 'gy'), may hold values from -6 to 6
- forcing: float32 [16, 8, 1024, 256], P('tm', None, 'gx', 'gy'), may hold values from -6 to 6
- departures: float32 [16, 16, 2, 1024], P('tm', 'gx', 'gy'), may hold values from -6 to 6
- model_var: float32 [16, 8, 1024, 256], P('tm', None, 'gx', 'gy'), may hold values from 0.3 to 3
- obs_var: float32 [16, 16, 2, 1024], P('tm', 'gx', 'gy'), may hold values from 0.5 to 2
- wind_east: float32 [16, 8, 1024, 256], P('tm', None, 'gx', 'gy'), may hold values from -0.3 to 0.3
- wind_north: float32 [16, 8, 1024, 256], P('tm', None, 'gx', 'gy'), may hold values from -0.3 to 0.3
- obs_cells: int32 [16, 16, 2, 1024], P('tm', 'gx', 'gy'), may hold values from 0 to 65535
- step_count: int32 [16], P('tm'), may hold values from 1 to 4, as said below
Outputs:
- lagrange_next: float32 [16, 8, 1024, 256], P('tm', None, 'gx', 'gy')
- obs_lagrange_next: float32 [16, 16, 2, 1024], P('tm', 'gx', 'gy')
- increment_next: float32 [16, 8, 1024, 256], P('tm', None, 'gx', 'gy')
- residual_model: float32 [16, 8, 1024, 256], P('tm', None, 'gx', 'gy')
- residual_obs: float32 [16, 16, 2, 1024], P('tm', 'gx', 'gy')
- residual_increment: float32 [16, 8, 1024, 256], P('tm', None, 'gx', 'gy')
The draws below stay inside these ranges and needn't reach their ends.
Inputs may be any that keep to these rules, and one draw needn't show every extreme that they name: `step_count`: each sub-window's number of model steps; at least one sub-window takes 4.
All inputs are finite; a program needn't handle non-finite values.
Results may differ from the reference program's by a relative error of at most 0.0003.
Values sent between devices are 32-bit elements; how exact they have to be, the bound alone decides.
No kernel may reach another device: no remote copies, remote signals or barrier semaphores. Data moves between devices by JAX's collectives and lax.ppermute only.
A program may use at most 64 MiB of HBM per device.

```python
import math
import jax
import jax.numpy as jnp
from jax import lax

CX = 64
CY = 128
LEV = 8
MAXSTEP = 4
NOBS = 1024
NSUB = 16
NX = 1024
NY = 256
N_GX = 16
N_GY = 2


def draw_step_count(key, part):
    key = jax.random.fold_in(key, 11)
    counts = jax.random.randint(key, (NSUB,), 1, MAXSTEP + 1, dtype=jnp.int32)
    where_full = jax.random.randint(jax.random.fold_in(key, 12), (), 0, NSUB, dtype=jnp.int32)
    return counts.at[where_full].set(MAXSTEP)


def set_ends(drawn, rng, least, largest):
    index_at = [jax.random.randint(jax.random.fold_in(rng, axis), (), 0, length) for axis, length in enumerate(drawn.shape)]
    longest = drawn.shape.index(max(drawn.shape))
    neighbour = index_at[:longest] + [(index_at[longest] + 1) % drawn.shape[longest]] + index_at[longest + 1:]
    return drawn.at[tuple(index_at)].set(least).at[tuple(neighbour)].set(largest)


def block_levels(own_key, dims, pieces, low, high):
    factor_of, own = 1.0, jax.random.fold_in(own_key, 6)
    for axis_at, shards_of in pieces:
        steps = jnp.exp(jax.random.uniform(jax.random.fold_in(own, axis_at), (shards_of,), jnp.float32, low / len(pieces), high / len(pieces)))
        factor_of = factor_of * jnp.repeat(steps, dims[axis_at] // shards_of).reshape([-1 if axis == axis_at else 1 for axis in range(len(dims))])
    return factor_of


def gaussian(rng, dims, scale, bound, cuts=(), kind=jnp.bfloat16):
    result = jax.random.normal(rng, dims, jnp.float32) * scale
    if len(cuts) > 0:
        result = block_levels(rng, dims, cuts, -0.22, 0.18) * result
    return jnp.clip(result, min=-bound, max=bound).astype(kind)


def setup_inputs(seed: int = 0) -> dict:
    splits = jax.random.split(jax.random.key(seed), 12)
    lagrange = gaussian(splits[0], (NSUB, LEV, NX, NY), 1.0, 6.0, ((0, 8), (2, 16), (3, 2)), jnp.float32)
    obs_lagrange = gaussian(splits[1], (NSUB, N_GX, N_GY, NOBS), 1.0, 6.0, ((0, 8), (1, 16), (2, 2)), jnp.float32)
    increment = gaussian(splits[2], (NSUB, LEV, NX, NY), 1.0, 6.0, ((0, 8), (2, 16), (3, 2)), jnp.float32)
    forcing = gaussian(splits[3], (NSUB, LEV, NX, NY), 1.0, 6.0, ((0, 8), (2, 16), (3, 2)), jnp.float32)
    departures = gaussian(splits[4], (NSUB, N_GX, N_GY, NOBS), 1.0, 6.0, ((0, 8), (1, 16), (2, 2)), jnp.float32)
    model_var = jnp.clip(jnp.exp(math.log(3.0) - 2.3025851 * jax.random.uniform(splits[5], (NSUB, LEV, NX, NY), jnp.float32) ** block_levels(splits[5], (NSUB, LEV, NX, NY), ((0, 8), (2, 16), (3, 2)), -0.2, 0.2)), 0.3, 3.0)
    obs_var = jnp.clip(jnp.exp(math.log(2.0) - 1.3862944 * jax.random.uniform(splits[6], (NSUB, N_GX, N_GY, NOBS), jnp.float32) ** block_levels(splits[6], (NSUB, N_GX, N_GY, NOBS), ((0, 8), (1, 16), (2, 2)), -0.2, 0.2)), 0.5, 2.0)
    wind_east = jnp.clip(jax.random.uniform(splits[7], (NSUB, LEV, NX, NY), jnp.float32, -0.3, 0.3) * block_levels(splits[7], (NSUB, LEV, NX, NY), ((0, 8), (2, 16), (3, 2)), -0.4, 0.0), -0.3, 0.3)
    wind_north = jnp.clip(jax.random.uniform(splits[8], (NSUB, LEV, NX, NY), jnp.float32, -0.3, 0.3) * block_levels(splits[8], (NSUB, LEV, NX, NY), ((0, 8), (2, 16), (3, 2)), -0.4, 0.0), -0.3, 0.3)
    obs_cells = set_ends(jax.random.randint(splits[9], (NSUB, N_GX, N_GY, NOBS), 0, LEV * CX * CY), jax.random.fold_in(splits[9], 1), 0, (LEV * CX * CY) - 1).astype(jnp.int32)
    step_count = draw_step_count(jax.random.fold_in(splits[11], 71), 0)
    return {"lagrange": lagrange, "obs_lagrange": obs_lagrange, "increment": increment, "forcing": forcing, "departures": departures, "model_var": model_var, "obs_var": obs_var, "wind_east": wind_east, "wind_north": wind_north, "obs_cells": obs_cells, "step_count": step_count}


DIFFUSION = 0.18
VERTICAL = 0.1
CENTRE = 1.0 - 4.0 * DIFFUSION - 2.0 * VERTICAL


def coefficients(east_wind, north_wind):
    return (DIFFUSION - 0.5 * east_wind, DIFFUSION + 0.5 * east_wind,
            DIFFUSION - 0.5 * north_wind, DIFFUSION + 0.5 * north_wind)


def vertical_sum(field):
    padded = jnp.pad(field, ((1, 1), (0, 0), (0, 0)))
    return padded[2:] + padded[:-2]


def forward_step(field, coefs):
    east, west, north, south = coefs
    padded = jnp.pad(field, ((0, 0), (1, 1), (1, 1)))
    return (CENTRE * field + east * padded[:, 2:, 1:-1] + west * padded[:, :-2, 1:-1]
            + north * padded[:, 1:-1, 2:] + south * padded[:, 1:-1, :-2] + VERTICAL * vertical_sum(field))


def moved(term):
    return jnp.pad(term, ((0, 0), (1, 1), (1, 1)))


def adjoint_step(field, coefs):
    east, west, north, south = coefs
    return (CENTRE * field + moved(east * field)[:, :-2, 1:-1] + moved(west * field)[:, 2:, 1:-1]
            + moved(north * field)[:, 1:-1, :-2] + moved(south * field)[:, 1:-1, 2:] + VERTICAL * vertical_sum(field))


def sweep_one(packed, adjoint):
    field, east_wind, north_wind, count = packed
    coefs = coefficients(east_wind, north_wind)
    for step_index in range(MAXSTEP):
        stepped = adjoint_step(field, coefs) if adjoint else forward_step(field, coefs)
        field = jnp.where(step_index < count, stepped, field)
    return field


def sweep_all(fields, wind_east, wind_north, step_count, adjoint):
    return lax.map(lambda packed: sweep_one(packed, adjoint), (fields, wind_east, wind_north, step_count))


def to_tiles(field):
    shaped = field.reshape(NSUB, LEV, N_GX, CX, N_GY, CY).transpose(0, 2, 4, 1, 3, 5)
    return shaped.reshape(NSUB, N_GX, N_GY, LEV * CX * CY)


def from_tiles(tiles):
    shaped = tiles.reshape(NSUB, N_GX, N_GY, LEV, CX, CY).transpose(0, 3, 1, 4, 2, 5)
    return shaped.reshape(NSUB, LEV, N_GX * CX, N_GY * CY)


def observe(field, obs_cells):
    return jnp.take_along_axis(to_tiles(field), obs_cells, axis=3)


def spread(values, obs_cells):
    cells = LEV * CX * CY
    tile_ids = jnp.arange(NSUB * N_GX * N_GY, dtype=jnp.int32).reshape(NSUB, N_GX, N_GY, 1)
    flat = (tile_ids * cells + obs_cells).reshape(-1).astype(jnp.int32)
    summed = jnp.zeros((NSUB * N_GX * N_GY * cells,), jnp.float32).at[flat].add(values.reshape(-1))
    return from_tiles(summed.reshape(NSUB, N_GX, N_GY, cells))


def apply_operator(lagr, obs_lagr, incr, model_var, obs_var, wind_east, wind_north, obs_cells, step_count):
    forward = sweep_all(incr, wind_east, wind_north, step_count, False)
    previous = jnp.concatenate((jnp.zeros_like(forward[:1]), forward[:-1]), 0)
    following = jnp.concatenate((lagr[1:], jnp.zeros_like(lagr[:1])), 0)
    backward = sweep_all(following, wind_east, wind_north, step_count, True)
    model_part = model_var * lagr + (incr - previous)
    obs_part = obs_var * obs_lagr + observe(incr, obs_cells)
    incr_part = (lagr - backward) + spread(obs_lagr, obs_cells)
    return model_part, obs_part, incr_part


def reference(lagrange, obs_lagrange, increment, forcing, departures, model_var, obs_var,
              wind_east, wind_north, obs_cells, step_count):
    fixed = (model_var, obs_var, wind_east, wind_north, obs_cells, step_count)
    first = apply_operator(lagrange, obs_lagrange, increment, *fixed)
    resid = (forcing - first[0], departures - first[1], -first[2])
    image = apply_operator(resid[0], resid[1], resid[2], *fixed)
    cross = jnp.sum(resid[0] * image[0]) + jnp.sum(resid[1] * image[1]) + jnp.sum(resid[2] * image[2])
    square = jnp.sum(image[0] * image[0]) + jnp.sum(image[1] * image[1]) + jnp.sum(image[2] * image[2])
    alpha = cross / (square + 1e-6)
    return (lagrange + alpha * resid[0], obs_lagrange + alpha * resid[1], increment + alpha * resid[2],
            resid[0] - alpha * image[0], resid[1] - alpha * image[1], resid[2] - alpha * image[2])
```

```python
import functools

import jax
import jax.numpy as jnp
from jax import lax
from jax.experimental import pallas as pl
from jax.experimental.pallas import tpu as pltpu
from jax.sharding import PartitionSpec as P

DIFFUSION = 0.18
VERTICAL = 0.1
CENTRE = 1.0 - 4.0 * DIFFUSION - 2.0 * VERTICAL

LEV, CX, CY = 8, 64, 128
HALO = 8
EXT = CX + 2 * HALO
TOP = 8
BUF = EXT + 2 * TOP
VMEM_LIMIT = 48 * 1024 * 1024
NBLOCKS = 10 * LEV + 6
F32 = jnp.float32

VM = pl.BlockSpec(memory_space=pltpu.VMEM)
SM = pl.BlockSpec(memory_space=pltpu.SMEM)


def call(body, outs, ins, scratch=(), flops=0):
    shapes = [jax.ShapeDtypeStruct(s, F32) for s in outs]
    nbytes = 4 * sum(int(a.size) for a in ins) + 4 * sum(
        functools.reduce(lambda a, b: a * b, s, 1) for s in outs
    )
    in_specs = [SM if (a.dtype == jnp.int32 and a.size < 64) else VM for a in ins]
    return pl.pallas_call(
        body,
        out_shape=shapes,
        in_specs=in_specs,
        out_specs=[VM] * len(shapes),
        scratch_shapes=list(scratch),
        compiler_params=pltpu.CompilerParams(vmem_limit_bytes=VMEM_LIMIT),
        cost_estimate=pl.CostEstimate(flops=flops, bytes_accessed=nbytes, transcendentals=0),
    )(*ins)


def iota(shape, dim):
    return lax.broadcasted_iota(jnp.int32, shape, dim)


def split(x):
    high = x.astype(jnp.bfloat16)
    low = (x - high.astype(F32)).astype(jnp.bfloat16)
    return high, low


def one_hots(cells):
    n = cells.shape[1]
    rows = (iota((LEV * CX, n), 0) == (cells >> 7)).astype(jnp.bfloat16)
    lanes = iota((CY, n), 0) == (cells & 127)
    return rows, lanes


def scatter(rows, lanes, values):
    high, low = split(values)
    zero = jnp.zeros((), jnp.bfloat16)
    parts = jnp.concatenate(
        [jnp.where(lanes, high.astype(F32), 0.0), jnp.where(lanes, low.astype(F32), 0.0)], 0
    ).astype(jnp.bfloat16)
    both = lax.dot_general(
        rows, parts, (((1,), (1,)), ((), ())), preferred_element_type=F32
    )
    return both[:, :CY] + both[:, CY:]


def gather(rows, lanes, field):
    high, low = split(field)
    both = lax.dot_general(
        jnp.concatenate([high, low], 1), rows, (((0,), (0,)), ((), ())),
        preferred_element_type=F32,
    )
    picked = both[:CY] + both[CY:]
    return jnp.sum(jnp.where(lanes, picked, 0.0), 0, keepdims=True)


def swap_halves(x):
    inner = (iota(x.shape, x.ndim - 1) & 15) < 8
    axis = x.ndim - 1
    return jnp.where(inner, pltpu.roll(x, CY - 8, axis), pltpu.roll(x, 8, axis))


def own_half(shape, gy):
    lane = iota(shape, len(shape) - 1) & 15
    return jnp.where(gy == 0, lane, lane ^ 8) < 8


def pack_kernel(
    cells, m, v, l, f, mv, we, wn, b_out, a_out, strip_out, z_out, lh_out, g1_out, g_s
):
    core = lax.axis_index("gx") % 2
    gy = lax.axis_index("gy")
    lane = iota((CX, CY), 1)
    for s in range(2):
        rows, lanes = one_hots(cells[s : s + 1])
        h = scatter(rows, lanes, m[s : s + 1])
        lh_out[s] = l[s] + h.reshape(LEV, CX, CY)
        g_s[s] = f[s] - mv[s] * l[s] - v[s]
    g1_out[...] = g_s[1]
    for z in range(LEV):
        for i in range(CX // 8):
            z_out[z * 8 + i] = l[0, z, 8 * i : 8 * i + 8]
            z_out[64 + z * 8 + i] = g_s[0, z, 8 * i : 8 * i + 8]
            z_out[128 + z * 8 + i] = mv[0, z, 8 * i : 8 * i + 8]

    def own(get):
        packed = jnp.zeros((CX, CY), F32)
        for z in range(LEV):
            rolled = pltpu.roll(get(z), (16 * z + 8) % CY, 1)
            packed = jnp.where((lane >> 4) == z, rolled, packed)
        return packed

    half = own_half((CX, CY), gy)
    pairs = (
        ((v, 0), (v, 1)), ((l, 0), (g_s, 0)), ((l, 1), (g_s, 1)),
        ((lh_out, 0), (lh_out, 1)), ((we, 0), (wn, 0)), ((we, 1), (wn, 1)),
    )
    for p, (one, two) in enumerate(pairs):
        first = own(lambda z, one=one: one[0][one[1], z])
        second = own(lambda z, two=two: two[0][two[1], z])
        strip_out[p] = jnp.where(half, first, swap_halves(second))
    for i in range(CX // 8):
        z_out[192 + i] = strip_out[1, 8 * i : 8 * i + 8]

    sub = iota((8, CY), 0)
    for out, top in ((b_out, core == 0), (a_out, core != 0)):
        row = jnp.where(top, 0, CX - 8)
        row = pl.multiple_of(row, 8)
        edge = pl.ds(row, 8)
        for k, field in enumerate((v, l, we, wn)):
            for s in range(2):
                out[pl.ds((2 * k + s) * LEV, LEV)] = field[s, :, edge, :]
        keep = jnp.where(top, sub, 7 - sub) < 4
        for s in range(2):
            for z in range(LEV):
                lh_edge = lh_out[s, z, edge, :]
                g_edge = pltpu.roll(g_s[s, z, edge, :], 4, 0)
                out[(8 + s) * LEV + z] = jnp.where(keep, lh_edge, g_edge)
        out[pl.ds(10 * LEV, 6)] = strip_out[:, edge, :]


def obs_kernel(cells, m, v, dep, ov, rm_out, h2_out):
    for s in range(2):
        rows, lanes = one_hots(cells[s : s + 1])
        seen = gather(rows, lanes, v[s].reshape(LEV * CX, CY))
        rm = dep[s : s + 1] - (ov[s : s + 1] * m[s : s + 1] + seen)
        rm_out[s : s + 1] = rm
        h2_out[s] = scatter(rows, lanes, rm).reshape(LEV, CX, CY)


class Place:
    def __init__(self):
        gx = lax.axis_index("gx")
        self.gy = lax.axis_index("gy")
        core = gx % 2
        self.b_row = pl.multiple_of(jnp.where(core == 0, TOP, TOP + HALO + CX), 8)
        self.a_row = pl.multiple_of(jnp.where(core == 0, TOP + HALO + CX, TOP), 8)
        self.low = jnp.where(gx == 0, 0.0, 1.0)
        self.high = jnp.where(gx == lax.axis_size("gx") - 1, 0.0, 1.0)


def clear(ref, guard_levels):
    lead = ref.shape[:-2]
    zero = jnp.zeros(lead + (TOP, CY), F32)
    ref[..., 0:TOP, :] = zero
    ref[..., BUF - TOP : BUF, :] = zero
    if guard_levels:
        full = jnp.zeros((BUF, CY), F32)
        for i in range(lead[0]):
            ref[i, 0] = full
            ref[i, LEV + 1] = full


def fill(dst, base, place, tile, b_block, a_block):
    for z in range(LEV):
        dst[base + z, TOP + HALO : TOP + HALO + CX] = tile(z)
        dst[base + z, pl.ds(place.b_row, 8)] = b_block(z)
        dst[base + z, pl.ds(place.a_row, 8)] = a_block(z)


def unpack(place, own, received):
    half = own_half(own.shape, place.gy)
    return jnp.where(half, own, received), swap_halves(jnp.where(half, received, own))


def fill_strips(first, second, place, own, got, own_b, got_b, own_a, got_a):
    mid = pl.ds(TOP + HALO, CX)
    for where, a, b in (
        (mid, own, got),
        (pl.ds(place.b_row, 8), own_b, got_b),
        (pl.ds(place.a_row, 8), own_a, got_a),
    ):
        one, two = unpack(place, a, b)
        first[where] = one
        second[where] = two


ROWS = slice(TOP, TOP + EXT)
UP = slice(TOP + 1, TOP + EXT + 1)
DOWN = slice(TOP - 1, TOP + EXT - 1)


def injected(strip, gy):
    lane = iota((EXT, CY), 1) & 15
    moved = jnp.where(gy == 0, pltpu.roll(strip, 119, 1), pltpu.roll(strip, 121, 1))
    return jnp.where(lane == jnp.where(gy == 0, 15, 0), moved, 0.0)


def coefficients(place, wind, strip, coef, scoef, adjoint):
    lane = iota((EXT, CY), 1)
    if not adjoint:
        for z in range(LEV):
            east, north = 0.5 * wind[0, z, ROWS], 0.5 * wind[1, z, ROWS]
            coef[0, z] = DIFFUSION - east
            coef[1, z] = DIFFUSION + east
            coef[2, z] = DIFFUSION - north
            coef[3, z] = DIFFUSION + north
        east, north = 0.5 * strip[0, ROWS], 0.5 * strip[1, ROWS]
        scoef[0] = DIFFUSION - east
        scoef[1] = DIFFUSION + east
        scoef[2] = DIFFUSION - north
        scoef[3] = DIFFUSION + north
        return
    inj = injected(strip[1, ROWS], place.gy)
    for z in range(LEV):
        north = wind[1, z, ROWS]
        edge = pltpu.roll(inj, (CY - 16 * z) % CY, 1)
        after = jnp.where(lane == CY - 1, edge, pltpu.roll(north, CY - 1, 1))
        before = jnp.where(lane == 0, edge, pltpu.roll(north, 1, 1))
        coef[0, z] = DIFFUSION + 0.5 * wind[0, z, UP]
        coef[1, z] = DIFFUSION - 0.5 * wind[0, z, DOWN]
        coef[2, z] = DIFFUSION + 0.5 * after
        coef[3, z] = DIFFUSION - 0.5 * before
    scoef[0] = DIFFUSION + 0.5 * strip[0, UP]
    scoef[1] = DIFFUSION - 0.5 * strip[0, DOWN]
    scoef[2] = DIFFUSION + 0.5 * pltpu.roll(strip[1, ROWS], CY - 1, 1)
    scoef[3] = DIFFUSION - 0.5 * pltpu.roll(strip[1, ROWS], 1, 1)


def store(dst, z, out, place):
    dst[z, TOP : TOP + HALO] = out[:HALO] * place.low
    dst[z, TOP + HALO : TOP + HALO + CX] = out[HALO : HALO + CX]
    dst[z, TOP + HALO + CX : TOP + EXT] = out[HALO + CX :] * place.high


def sweep(place, state, strip, coef, scoef, count):
    lane = iota((EXT, CY), 1)

    def one(step, _):
        now = step & 1
        src, dst = state.at[now], state.at[1 - now]
        ssrc, sdst = strip.at[now], strip.at[1 - now]
        own = ssrc[0, ROWS]
        inj = injected(own, place.gy)
        for z in range(LEV):
            mid = src[z + 1, ROWS]
            edge = pltpu.roll(inj, (CY - 16 * z) % CY, 1)
            after = jnp.where(lane == CY - 1, edge, pltpu.roll(mid, CY - 1, 1))
            before = jnp.where(lane == 0, edge, pltpu.roll(mid, 1, 1))
            out = (
                CENTRE * mid
                + coef[0, z] * src[z + 1, UP]
                + coef[1, z] * src[z + 1, DOWN]
                + coef[2, z] * after
                + coef[3, z] * before
                + VERTICAL * (src[z + 2, ROWS] + src[z, ROWS])
            )
            store(dst, z + 1, out, place)
        above = jnp.where(lane < CY - 16, pltpu.roll(own, CY - 16, 1), 0.0)
        below = jnp.where(lane >= 16, pltpu.roll(own, 16, 1), 0.0)
        out = (
            CENTRE * own
            + scoef[0] * ssrc[0, UP]
            + scoef[1] * ssrc[0, DOWN]
            + scoef[2] * pltpu.roll(own, CY - 1, 1)
            + scoef[3] * pltpu.roll(own, 1, 1)
            + VERTICAL * (above + below)
        )
        store(sdst, 0, out, place)
        return 0

    lax.fori_loop(0, count, one, 0)


STATE = pltpu.VMEM((2, LEV + 2, BUF, CY), F32)
STRIP = pltpu.VMEM((2, 1, BUF, CY), F32)
COEF = pltpu.VMEM((4, LEV, EXT, CY), F32)
SCOEF = pltpu.VMEM((4, EXT, CY), F32)
WIND = pltpu.VMEM((2, LEV, BUF, CY), F32)
WSTRIP = pltpu.VMEM((2, BUF, CY), F32)


def fill_winds(place, s, we, wn, bg, ag, own, got, by, ay, wind, wstrip):
    for k, field in enumerate((we, wn)):
        fill(
            wind.at[k], 0, place, lambda z, field=field: field[s, z],
            lambda z, k=k: bg[(4 + 2 * k + s) * LEV + z],
            lambda z, k=k: ag[(4 + 2 * k + s) * LEV + z],
        )
    p = 4 + s
    fill_strips(
        wstrip.at[0], wstrip.at[1], place, own[p], got[p],
        bg[10 * LEV + p], by[p], ag[10 * LEV + p], ay[p],
    )


def first_kernel(
    counts, v, l, we, wn, lh, g1, own, got, bg, ag, by, ay,
    ext_out, rv_out, f1_out,
    x_f, x_b, s_f, s_b, coef, scoef, wind, wstrip, extra, estrip,
):
    place = Place()
    clear(x_f, True)
    clear(x_b, True)
    for ref in (s_f, s_b, wind, wstrip, extra, estrip):
        clear(ref, False)

    def strips(p, first, second):
        fill_strips(
            first, second, place, own[p], got[p],
            bg[10 * LEV + p], by[p], ag[10 * LEV + p], ay[p],
        )

    fill_winds(place, 0, we, wn, bg, ag, own, got, by, ay, wind, wstrip)
    fill(
        x_b.at[0], 1, place, lambda z: l[1, z],
        lambda z: bg[3 * LEV + z], lambda z: ag[3 * LEV + z],
    )
    strips(2, s_b.at[0, 0], estrip.at[1])
    coefficients(place, wind, wstrip, coef, scoef, True)
    sweep(place, x_b, s_b, coef, scoef, counts[0])
    end = counts[0] & 1
    fill(
        extra.at[0], 0, place, lambda z: lh[0, z],
        lambda z: bg[8 * LEV + z], lambda z: ag[8 * LEV + z],
    )
    fill(
        extra.at[1], 0, place, lambda z: g1[z],
        lambda z: pltpu.roll(bg[9 * LEV + z], 4, 0),
        lambda z: pltpu.roll(ag[9 * LEV + z], 4, 0),
    )
    for z in range(LEV):
        rv = x_b[end, z + 1, ROWS] - extra[0, z, ROWS]
        ext_out[0, z] = rv
        rv_out[z] = rv[HALO : HALO + CX]
    strips(3, estrip.at[0], s_f.at[0, 0])
    ext_out[0, LEV] = s_b[end, 0, ROWS] - estrip[0, ROWS]

    for s in range(2):
        if s == 1:
            fill_winds(place, 1, we, wn, bg, ag, own, got, by, ay, wind, wstrip)
        coefficients(place, wind, wstrip, coef, scoef, False)
        fill(
            x_f.at[0], 1, place, lambda z, s=s: v[s, z],
            lambda z, s=s: bg[s * LEV + z], lambda z, s=s: ag[s * LEV + z],
        )
        if s == 0:
            strips(0, s_f.at[0, 0], estrip.at[0])
        else:
            strips(0, estrip.at[0], s_f.at[0, 0])
        sweep(place, x_f, s_f, coef, scoef, counts[s])
        end = counts[s] & 1
        for z in range(LEV):
            out = x_f[end, z + 1, ROWS]
            if s == 0:
                ext_out[1, z] = out + extra[1, z, ROWS]
            else:
                ext_out[2, z] = out
                f1_out[z] = out[HALO : HALO + CX]
        out = s_f[end, 0, ROWS]
        ext_out[1 + s, LEV] = out + estrip[1, ROWS] if s == 0 else out


def lane_sum(x):
    return functools.reduce(
        lambda a, b: a + b, [x[:, i : i + CY] for i in range(0, x.shape[1], CY)]
    )


def second_kernel(
    counts, cells, ext, we, wn, lh, own, got, bg, ag, by, ay, zt, zh,
    mv, h2, rm, ov,
    rv1_out, rl1_out, rl2_out, f21_out, b20_out, ql1_out, qv1_out, qm_out, dots_out,
    x_f, x_b, s_f, s_b, coef, scoef, wind, wstrip, extra, estrip,
):
    place = Place()
    clear(x_f, True)
    clear(x_b, True)
    for ref in (s_f, s_b, wind, wstrip, extra, estrip):
        clear(ref, False)
    tile = slice(HALO, HALO + CX)
    follows = jnp.where(lax.axis_index("tm") == lax.axis_size("tm") - 1, 0.0, 1.0)

    fill_winds(place, 1, we, wn, bg, ag, own, got, by, ay, wind, wstrip)
    coefficients(place, wind, wstrip, coef, scoef, True)

    def z_tile(base):
        return lambda z: zt[base + 8 * z : base + 8 * z + 8].reshape(CX, CY)

    fill(x_b.at[0], 1, place, z_tile(0), lambda z: zh[z], lambda z: zh[16 + z])
    fill(
        extra.at[1], 0, place, z_tile(64),
        lambda z: pltpu.roll(zh[8 + z], 4, 0), lambda z: pltpu.roll(zh[24 + z], 4, 0),
    )
    fill_strips(
        s_b.at[0, 0], estrip.at[1], place,
        zt[192:200].reshape(CX, CY), zh[36:44].reshape(CX, CY),
        zh[32], zh[33], zh[34], zh[35],
    )
    sweep(place, x_b, s_b, coef, scoef, counts[1])
    end = counts[1] & 1

    fill(
        extra.at[0], 0, place, lambda z: lh[1, z],
        lambda z: bg[9 * LEV + z], lambda z: ag[9 * LEV + z],
    )
    fill_strips(
        s_f.at[0, 0], estrip.at[0], place, own[3], got[3],
        bg[10 * LEV + 3], by[3], ag[10 * LEV + 3], ay[3],
    )
    for z in range(LEV):
        rv = x_b[end, z + 1, ROWS] - extra[0, z, ROWS]
        x_f[0, z + 1, ROWS] = rv
        rv1_out[z] = rv[tile]
        rl = (extra[1, z, ROWS] + ext[2, z]) * follows
        x_b[0, z + 1, ROWS] = rl
        rl2_out[z] = rl[tile]
    s_f[0, 0, ROWS] = s_b[end, 0, ROWS] - estrip[0, ROWS]
    s_b[0, 0, ROWS] = (estrip[1, ROWS] + ext[2, LEV]) * follows

    sweep(place, x_b, s_b, coef, scoef, counts[1])
    cross = jnp.zeros((8, CY), F32)
    square = jnp.zeros((8, CY), F32)

    def dots(r, q):
        return jnp.sum((r * q).reshape(-1, 8, CY), 0), jnp.sum((q * q).reshape(-1, 8, CY), 0)

    for z in range(LEV):
        rl1 = ext[1, z, tile]
        rl1_out[z] = rl1
        qv = rl1 - x_b[end, z + 1, TOP + HALO : TOP + HALO + CX] + h2[1, z]
        qv1_out[z] = qv
        c, q = dots(rv1_out[z], qv)
        cross, square = cross + c, square + q
    coefficients(place, wind, wstrip, coef, scoef, False)
    sweep(place, x_f, s_f, coef, scoef, counts[1])
    for z in range(LEV):
        f21_out[z] = x_f[end, z + 1, TOP + HALO : TOP + HALO + CX]

    end = counts[0] & 1
    fill_winds(place, 0, we, wn, bg, ag, own, got, by, ay, wind, wstrip)
    coefficients(place, wind, wstrip, coef, scoef, False)
    for z in range(LEV):
        x_f[0, z + 1, ROWS] = ext[0, z]
        x_b[0, z + 1, ROWS] = ext[1, z]
    s_f[0, 0, ROWS] = ext[0, LEV]
    s_b[0, 0, ROWS] = ext[1, LEV]
    sweep(place, x_f, s_f, coef, scoef, counts[0])
    for z in range(LEV):
        rl1 = ext[1, z, tile]
        ql = mv[1, z] * rl1 + rv1_out[z] - x_f[end, z + 1, TOP + HALO : TOP + HALO + CX]
        ql1_out[z] = ql
        c, q = dots(rl1, ql)
        cross, square = cross + c, square + q
    coefficients(place, wind, wstrip, coef, scoef, True)
    sweep(place, x_b, s_b, coef, scoef, counts[0])
    for z in range(LEV):
        b20_out[z] = x_b[end, z + 1, TOP + HALO : TOP + HALO + CX]

    for s in range(2):
        rows, lanes = one_hots(cells[s : s + 1])
        if s == 0:
            field = ext[0, 0:LEV, tile].reshape(LEV * CX, CY)
        else:
            field = rv1_out[...].reshape(LEV * CX, CY)
        seen = gather(rows, lanes, field)
        r = rm[s : s + 1]
        q = ov[s : s + 1] * r + seen
        qm_out[s : s + 1] = q
        c, q = lane_sum(r * q), lane_sum(q * q)
        first = iota((8, CY), 0) == 0
        cross = cross + jnp.where(first, c, 0.0)
        square = square + jnp.where(first, q, 0.0)
    dots_out[0] = cross
    dots_out[1] = square


def dots_kernel(
    z_f, z_rv, zt, rl2, f21, b20, z_own, h2, rv0, mv, dots_in, rl0_out, qv0_out, send_out
):
    follows = jnp.where(lax.axis_index("tm") == lax.axis_size("tm") - 1, 0.0, 1.0)
    starts = jnp.where(lax.axis_index("tm") == 0, 1.0, 0.0)
    cross, square = dots_in[0], dots_in[1]

    def total(x):
        return jnp.sum(x.reshape(-1, 8, CY), 0)

    for z in range(LEV):
        rl0 = z_own[64 + 8 * z : 72 + 8 * z].reshape(CX, CY) + z_f[z]
        rv = rv0[z]
        qv = rl0 - b20[z] + h2[0, z]
        rl0_out[z] = rl0
        qv0_out[z] = qv
        ql = (mv[0, z] * rl0 + rv) * starts
        rl2z = rl2[z]
        q2 = (zt[128 + 8 * z : 136 + 8 * z].reshape(CX, CY) * rl2z + z_rv[z] - f21[z]) * follows
        cross += total(rv * qv) + total(rl0 * ql) + total(rl2z * q2)
        square += total(qv * qv) + total(ql * ql) + total(q2 * q2)
    cross = jnp.sum(jnp.sum(cross, 0, keepdims=True), 1, keepdims=True)
    square = jnp.sum(jnp.sum(square, 0, keepdims=True), 1, keepdims=True)
    n = send_out.shape[0]
    lane = iota((n, CY), 1)
    send_out[...] = jnp.where(lane == 0, cross, jnp.where(lane == 1, square, 0.0))


def last_kernel(
    sums, l, m, v, mv, rl0, rl1, rv0, rv1, rm, z_f2, ql1, qv0, qv1, qm,
    l_out, m_out, v_out, a_out, b_out, c_out,
):
    total = jnp.sum(sums[...], 0, keepdims=True)
    lane = iota((1, CY), 1)
    cross = jnp.sum(jnp.where(lane == 0, total, 0.0), 1, keepdims=True)
    square = jnp.sum(jnp.where(lane == 1, total, 0.0), 1, keepdims=True)
    alpha = cross / (square + 1e-06)
    m_out[...] = m[...] + alpha * rm[...]
    b_out[...] = rm[...] - alpha * qm[...]
    for z in range(LEV):
        ql0 = mv[0, z] * rl0[z] + rv0[z] - z_f2[z]
        l_out[0, z] = l[0, z] + alpha * rl0[z]
        l_out[1, z] = l[1, z] + alpha * rl1[z]
        v_out[0, z] = v[0, z] + alpha * rv0[z]
        v_out[1, z] = v[1, z] + alpha * rv1[z]
        a_out[0, z] = rl0[z] - alpha * ql0
        a_out[1, z] = rl1[z] - alpha * ql1[z]
        c_out[0, z] = rv0[z] - alpha * qv0[z]
        c_out[1, z] = rv1[z] - alpha * qv1[z]


def shards(sizes, l4, m4, v4, f4, d4, mv4, ov4, we4, wn4, cells4, counts):
    ntm, ngx, ngy = sizes
    tile = (LEV, CX, CY)
    flat = lambda x: x.reshape(2, -1)
    m, dep, ov, cells = flat(m4), flat(d4), flat(ov4), flat(cells4)
    nobs = m.shape[1]

    def pair_b(i):
        return i - 1 if i % 2 == 0 else i + 1

    def plane(move_x, move_y):
        pairs = []
        for x in range(ngx):
            for y in range(ngy):
                to = move_x(x)
                if 0 <= to < ngx:
                    pairs.append((x * ngy + y, to * ngy + (1 - y if move_y else y)))
        return pairs

    same = lambda i: i
    pair_a = lambda i: i ^ 1
    axes = ("gx", "gy")
    down = [(i + 1, i) for i in range(ntm - 1)]
    up = [(i, i + 1) for i in range(ntm - 1)]

    b_send, a_send, own, z_send, lh, g1 = call(
        pack_kernel,
        [(NBLOCKS, 8, CY)] * 2 + [(6, CX, CY), (200, 8, CY), (2,) + tile, tile],
        [cells, m, v4, l4, f4, mv4, we4, wn4],
        [pltpu.VMEM((2,) + tile, F32)],
    )
    zt = lax.ppermute(z_send, "tm", down)
    bg = lax.ppermute(b_send, axes, plane(pair_b, False))
    got = lax.ppermute(own, axes, plane(same, True))
    by = lax.ppermute(b_send[10 * LEV :], axes, plane(pair_b, True))
    ag = lax.ppermute(a_send, axes, plane(pair_a, False))
    ay = lax.ppermute(a_send[10 * LEV :], axes, plane(pair_a, True))
    rm, h2 = call(obs_kernel, [(2, nobs), (2,) + tile], [cells, m, v4, dep, ov])

    p = 10 * LEV + 1
    z_edges = jnp.concatenate(
        [
            bg[2 * LEV : 3 * LEV], bg[8 * LEV : 9 * LEV],
            ag[2 * LEV : 3 * LEV], ag[8 * LEV : 9 * LEV],
            bg[p : p + 1], by[1:2], ag[p : p + 1], ay[1:2],
            got[1].reshape(8, 8, CY),
        ],
        0,
    )
    zh = lax.ppermute(z_edges, "tm", down)
    scratch = [
        STATE, STATE, STRIP, STRIP, COEF, SCOEF, WIND, WSTRIP,
        pltpu.VMEM((2, LEV, BUF, CY), F32), pltpu.VMEM((2, BUF, CY), F32),
    ]
    ext, rv0, f1 = call(
        first_kernel,
        [(3, LEV + 1, EXT, CY), tile, tile],
        [counts, v4, l4, we4, wn4, lh, g1, own, got, bg, ag, by, ay],
        scratch,
    )
    z_rv = lax.ppermute(rv0, "tm", down)
    z_f = lax.ppermute(f1, "tm", up)
    rv1, rl1, rl2, f21, b20, ql1, qv1, qm, dots = call(
        second_kernel,
        [tile] * 7 + [(2, nobs), (2, 8, CY)],
        [counts, cells, ext, we4, wn4, lh, own, got, bg, ag, by, ay, zt, zh, mv4, h2, rm, ov],
        scratch,
    )
    z_f2 = lax.ppermute(f21, "tm", up)
    n = ntm * ngx * ngy
    rl0, qv0, send = call(
        dots_kernel,
        [tile, tile, (n, CY)],
        [z_f, z_rv, zt, rl2, f21, b20, z_send, h2, rv0, mv4, dots],
    )
    sums = lax.all_to_all(send, ("tm", "gx", "gy"), 0, 0, tiled=True)
    l_next, m_next, v_next, res_l, res_m, res_v = call(
        last_kernel,
        [l4.shape, (2, nobs), v4.shape, l4.shape, (2, nobs), v4.shape],
        [sums, l4, m, v4, mv4, rl0, rl1, rv0, rv1, rm, z_f2, ql1, qv0, qv1, qm],
    )
    return l_next, m_next.reshape(m4.shape), v_next, res_l, res_m.reshape(m4.shape), res_v


def solution(mesh):
    field = P("tm", None, "gx", "gy")
    obs = P("tm", "gx", "gy", None)
    sizes = tuple(mesh.shape[a] for a in ("tm", "gx", "gy"))
    return jax.shard_map(
        functools.partial(shards, sizes),
        mesh=mesh,
        in_specs=(field, obs, field, field, obs, field, obs, field, field, obs, P("tm")),
        out_specs=(field, obs, field, field, obs, field),
        check_vma=False,
    )
```

```python
import functools

import jax
import jax.numpy as jnp
from jax import lax
from jax.experimental import pallas as pl
from jax.experimental.pallas import tpu as pltpu
from jax.sharding import PartitionSpec as P

DIFFUSION = 0.18
VERTICAL = 0.1
CENTRE = 1.0 - 4.0 * DIFFUSION - 2.0 * VERTICAL

LEV, CX, CY = 8, 64, 128
HALO = 8
EXT = CX + 2 * HALO
TOP = 8
BUF = EXT + 2 * TOP
VMEM_LIMIT = 24 * 1024 * 1024
PACK_LIMIT = 60 * 1024 * 1024
NBLOCKS = 10 * LEV + 6
F32 = jnp.float32

VM = pl.BlockSpec(memory_space=pltpu.VMEM)
SM = pl.BlockSpec(memory_space=pltpu.SMEM)
FAR = pl.BlockSpec(memory_space=pltpu.HBM)


def call(body, outs, ins, scratch=(), micros=1.0, fetched=(), limit=VMEM_LIMIT):
    shapes = [jax.ShapeDtypeStruct(s, F32) for s in outs]
    nbytes = 4 * sum(int(a.size) for a in ins) + 4 * sum(
        functools.reduce(lambda a, b: a * b, s, 1) for s in outs
    )
    in_specs = [SM if (a.dtype == jnp.int32 and a.size < 64) else VM for a in ins]
    for i in fetched:
        in_specs[i] = FAR
    return pl.pallas_call(
        body,
        out_shape=shapes,
        in_specs=in_specs,
        out_specs=[VM] * len(shapes),
        scratch_shapes=list(scratch),
        compiler_params=pltpu.CompilerParams(vmem_limit_bytes=limit),
        cost_estimate=pl.CostEstimate(
            flops=int(1.1e9 * micros), bytes_accessed=nbytes, transcendentals=0
        ),
    )(*ins)


def iota(shape, dim):
    return lax.broadcasted_iota(jnp.int32, shape, dim)


def split(x):
    high = x.astype(jnp.bfloat16)
    low = (x - high.astype(F32)).astype(jnp.bfloat16)
    return high, low


def one_hots(cells):
    n = cells.shape[1]
    rows = (iota((LEV * CX, n), 0) == (cells >> 7)).astype(jnp.bfloat16)
    lanes = iota((CY, n), 0) == (cells & 127)
    return rows, lanes


def scatter(rows, lanes, values):
    high, low = split(values)
    zero = jnp.zeros((), jnp.bfloat16)
    parts = jnp.concatenate(
        [jnp.where(lanes, high.astype(F32), 0.0), jnp.where(lanes, low.astype(F32), 0.0)], 0
    ).astype(jnp.bfloat16)
    both = lax.dot_general(
        rows, parts, (((1,), (1,)), ((), ())), preferred_element_type=F32
    )
    return both[:, :CY] + both[:, CY:]


def gather(rows, lanes, field):
    high, low = split(field)
    both = lax.dot_general(
        jnp.concatenate([high, low], 1), rows, (((0,), (0,)), ((), ())),
        preferred_element_type=F32,
    )
    picked = both[:CY] + both[CY:]
    return jnp.sum(jnp.where(lanes, picked, 0.0), 0, keepdims=True)


def swap_halves(x):
    inner = (iota(x.shape, x.ndim - 1) & 15) < 8
    axis = x.ndim - 1
    return jnp.where(inner, pltpu.roll(x, CY - 8, axis), pltpu.roll(x, 8, axis))


def own_half(shape, gy):
    lane = iota(shape, len(shape) - 1) & 15
    return jnp.where(gy == 0, lane, lane ^ 8) < 8


def pack_kernel(
    cells_h, m_h, l_h, f_h, mv_h, v_h, we_h, wn_h,
    b_out, a_out, strip_out, z_out, lh_out, g1_out,
    g_s, cells, m, l, f, mv, v, we, wn, sems,
):
    far = (cells_h, m_h, l_h, f_h, mv_h, v_h, we_h, wn_h)
    near = (cells, m, l, f, mv, v, we, wn)
    copies = [pltpu.make_async_copy(a, b, sems.at[i]) for i, (a, b) in enumerate(zip(far, near))]
    for copy in copies:
        copy.start()
    copies[0].wait()
    copies[1].wait()
    core = lax.axis_index("gx") % 2
    gy = lax.axis_index("gy")
    lane = iota((CX, CY), 1)
    for s in range(2):
        rows, lanes = one_hots(cells[s, 0])
        h = scatter(rows, lanes, m[s, 0])
        if s == 0:
            for copy in copies[2:]:
                copy.wait()
        lh_out[s] = l[s] + h.reshape(LEV, CX, CY)
        g_s[s] = f[s] - mv[s] * l[s] - v[s]
    g1_out[...] = g_s[1]
    for z in range(LEV):
        for i in range(CX // 8):
            z_out[z * 8 + i] = l[0, z, 8 * i : 8 * i + 8]
            z_out[64 + z * 8 + i] = g_s[0, z, 8 * i : 8 * i + 8]

    def own(get):
        packed = jnp.zeros((CX, CY), F32)
        for z in range(LEV):
            rolled = pltpu.roll(get(z), (16 * z + 8) % CY, 1)
            packed = jnp.where((lane >> 4) == z, rolled, packed)
        return packed

    half = own_half((CX, CY), gy)
    pairs = (
        ((v, 0), (v, 1)), ((l, 0), (g_s, 0)), ((l, 1), (g_s, 1)),
        ((lh_out, 0), (lh_out, 1)), ((we, 0), (wn, 0)), ((we, 1), (wn, 1)),
    )
    for p, (one, two) in enumerate(pairs):
        first = own(lambda z, one=one: one[0][one[1], z])
        second = own(lambda z, two=two: two[0][two[1], z])
        strip_out[p] = jnp.where(half, first, swap_halves(second))
    for i in range(CX // 8):
        z_out[128 + i] = strip_out[1, 8 * i : 8 * i + 8]

    sub = iota((8, CY), 0)
    for out, top in ((b_out, core == 0), (a_out, core != 0)):
        row = jnp.where(top, 0, CX - 8)
        row = pl.multiple_of(row, 8)
        edge = pl.ds(row, 8)
        for k, field in enumerate((v, l, we, wn)):
            for s in range(2):
                out[pl.ds((2 * k + s) * LEV, LEV)] = field[s, :, edge, :]
        keep = jnp.where(top, sub, 7 - sub) < 4
        for s in range(2):
            for z in range(LEV):
                lh_edge = lh_out[s, z, edge, :]
                g_edge = pltpu.roll(g_s[s, z, edge, :], 4, 0)
                out[(8 + s) * LEV + z] = jnp.where(keep, lh_edge, g_edge)
        out[pl.ds(10 * LEV, 6)] = strip_out[:, edge, :]


def obs_kernel(cells, m, v, dep, ov, rm_out, h2_out):
    for s in range(2):
        rows, lanes = one_hots(cells[s, 0])
        seen = gather(rows, lanes, v[s].reshape(LEV * CX, CY))
        rm = dep[s, 0] - (ov[s, 0] * m[s, 0] + seen)
        rm_out[s, 0] = rm
        h2_out[s] = scatter(rows, lanes, rm).reshape(LEV, CX, CY)


class Place:
    def __init__(self):
        gx = lax.axis_index("gx")
        self.gy = lax.axis_index("gy")
        core = gx % 2
        self.b_row = pl.multiple_of(jnp.where(core == 0, TOP, TOP + HALO + CX), 8)
        self.a_row = pl.multiple_of(jnp.where(core == 0, TOP + HALO + CX, TOP), 8)
        self.low = jnp.where(gx == 0, 0.0, 1.0)
        self.high = jnp.where(gx == lax.axis_size("gx") - 1, 0.0, 1.0)


def clear(ref, guard_levels):
    lead = ref.shape[:-2]
    zero = jnp.zeros(lead + (TOP, CY), F32)
    ref[..., 0:TOP, :] = zero
    ref[..., BUF - TOP : BUF, :] = zero
    if guard_levels:
        full = jnp.zeros((BUF, CY), F32)
        for i in range(lead[0]):
            ref[i, 0] = full
            ref[i, LEV + 1] = full


def fill(dst, base, place, tile, b_block, a_block):
    for z in range(LEV):
        dst[base + z, TOP + HALO : TOP + HALO + CX] = tile(z)
        dst[base + z, pl.ds(place.b_row, 8)] = b_block(z)
        dst[base + z, pl.ds(place.a_row, 8)] = a_block(z)


def unpack(place, own, received):
    half = own_half(own.shape, place.gy)
    return jnp.where(half, own, received), swap_halves(jnp.where(half, received, own))


def fill_strips(first, second, place, own, got, own_b, got_b, own_a, got_a):
    mid = pl.ds(TOP + HALO, CX)
    for where, a, b in (
        (mid, own, got),
        (pl.ds(place.b_row, 8), own_b, got_b),
        (pl.ds(place.a_row, 8), own_a, got_a),
    ):
        one, two = unpack(place, a, b)
        first[where] = one
        second[where] = two


ROWS = slice(TOP, TOP + EXT)
UP = slice(TOP + 1, TOP + EXT + 1)
DOWN = slice(TOP - 1, TOP + EXT - 1)


def injected(strip, gy):
    lane = iota((EXT, CY), 1) & 15
    moved = jnp.where(gy == 0, pltpu.roll(strip, 119, 1), pltpu.roll(strip, 121, 1))
    return jnp.where(lane == jnp.where(gy == 0, 15, 0), moved, 0.0)


def coefficients(place, wind, strip, coef, scoef, adjoint):
    lane = iota((EXT, CY), 1)
    if not adjoint:
        for z in range(LEV):
            east, north = 0.5 * wind[0, z, ROWS], 0.5 * wind[1, z, ROWS]
            coef[0, z] = DIFFUSION - east
            coef[1, z] = DIFFUSION + east
            coef[2, z] = DIFFUSION - north
            coef[3, z] = DIFFUSION + north
        east, north = 0.5 * strip[0, ROWS], 0.5 * strip[1, ROWS]
        scoef[0] = DIFFUSION - east
        scoef[1] = DIFFUSION + east
        scoef[2] = DIFFUSION - north
        scoef[3] = DIFFUSION + north
        return
    inj = injected(strip[1, ROWS], place.gy)
    for z in range(LEV):
        north = wind[1, z, ROWS]
        edge = pltpu.roll(inj, (CY - 16 * z) % CY, 1)
        after = jnp.where(lane == CY - 1, edge, pltpu.roll(north, CY - 1, 1))
        before = jnp.where(lane == 0, edge, pltpu.roll(north, 1, 1))
        coef[0, z] = DIFFUSION + 0.5 * wind[0, z, UP]
        coef[1, z] = DIFFUSION - 0.5 * wind[0, z, DOWN]
        coef[2, z] = DIFFUSION + 0.5 * after
        coef[3, z] = DIFFUSION - 0.5 * before
    scoef[0] = DIFFUSION + 0.5 * strip[0, UP]
    scoef[1] = DIFFUSION - 0.5 * strip[0, DOWN]
    scoef[2] = DIFFUSION + 0.5 * pltpu.roll(strip[1, ROWS], CY - 1, 1)
    scoef[3] = DIFFUSION - 0.5 * pltpu.roll(strip[1, ROWS], 1, 1)


def store(dst, z, out, place):
    dst[z, TOP : TOP + HALO] = out[:HALO] * place.low
    dst[z, TOP + HALO : TOP + HALO + CX] = out[HALO : HALO + CX]
    dst[z, TOP + HALO + CX : TOP + EXT] = out[HALO + CX :] * place.high


def sweep(place, state, strip, coef, scoef, count):
    lane = iota((EXT, CY), 1)

    def one(step, _):
        now = step & 1
        src, dst = state.at[now], state.at[1 - now]
        ssrc, sdst = strip.at[now], strip.at[1 - now]
        own = ssrc[0, ROWS]
        inj = injected(own, place.gy)
        for z in range(LEV):
            mid = src[z + 1, ROWS]
            edge = pltpu.roll(inj, (CY - 16 * z) % CY, 1)
            after = jnp.where(lane == CY - 1, edge, pltpu.roll(mid, CY - 1, 1))
            before = jnp.where(lane == 0, edge, pltpu.roll(mid, 1, 1))
            out = (
                CENTRE * mid
                + coef[0, z] * src[z + 1, UP]
                + coef[1, z] * src[z + 1, DOWN]
                + coef[2, z] * after
                + coef[3, z] * before
                + VERTICAL * (src[z + 2, ROWS] + src[z, ROWS])
            )
            store(dst, z + 1, out, place)
        above = jnp.where(lane < CY - 16, pltpu.roll(own, CY - 16, 1), 0.0)
        below = jnp.where(lane >= 16, pltpu.roll(own, 16, 1), 0.0)
        out = (
            CENTRE * own
            + scoef[0] * ssrc[0, UP]
            + scoef[1] * ssrc[0, DOWN]
            + scoef[2] * pltpu.roll(own, CY - 1, 1)
            + scoef[3] * pltpu.roll(own, 1, 1)
            + VERTICAL * (above + below)
        )
        store(sdst, 0, out, place)
        return 0

    lax.fori_loop(0, count, one, 0)


STATE = pltpu.VMEM((2, LEV + 2, BUF, CY), F32)
STRIP = pltpu.VMEM((2, 1, BUF, CY), F32)
COEF = pltpu.VMEM((4, LEV, EXT, CY), F32)
SCOEF = pltpu.VMEM((4, EXT, CY), F32)
WIND = pltpu.VMEM((2, LEV, BUF, CY), F32)
WSTRIP = pltpu.VMEM((2, BUF, CY), F32)


def fill_winds(place, s, we, wn, bg, ag, own, got, by, wind, wstrip):
    for k, field in enumerate((we, wn)):
        fill(
            wind.at[k], 0, place, lambda z, field=field: field[s, z],
            lambda z, k=k: bg[(4 + 2 * k + s) * LEV + z],
            lambda z, k=k: ag[(4 + 2 * k + s) * LEV + z],
        )
    p = 4 + s
    fill_strips(
        wstrip.at[0], wstrip.at[1], place, own[p], got[p, :CX],
        bg[10 * LEV + p], by[p], ag[10 * LEV + p], got[p, CX:],
    )


def first_kernel(
    counts, v, l, we, wn, mv, lh, g1, own, got, bg, ag, by,
    ext_out, rv_out, f1_out,
    x_f, x_b, s_f, s_b, coef, scoef, wind, wstrip, extra, estrip,
):
    place = Place()
    clear(x_f, True)
    clear(x_b, True)
    for ref in (s_f, s_b, wind, wstrip, extra, estrip):
        clear(ref, False)

    def strips(p, first, second):
        fill_strips(
            first, second, place, own[p], got[p, :CX],
            bg[10 * LEV + p], by[p], ag[10 * LEV + p], got[p, CX:],
        )

    fill_winds(place, 0, we, wn, bg, ag, own, got, by, wind, wstrip)
    fill(
        x_b.at[0], 1, place, lambda z: l[1, z],
        lambda z: bg[3 * LEV + z], lambda z: ag[3 * LEV + z],
    )
    strips(2, s_b.at[0, 0], estrip.at[1])
    coefficients(place, wind, wstrip, coef, scoef, True)
    sweep(place, x_b, s_b, coef, scoef, counts[0])
    end = counts[0] & 1
    fill(
        extra.at[0], 0, place, lambda z: lh[0, z],
        lambda z: bg[8 * LEV + z], lambda z: ag[8 * LEV + z],
    )
    fill(
        extra.at[1], 0, place, lambda z: g1[z],
        lambda z: pltpu.roll(bg[9 * LEV + z], 4, 0),
        lambda z: pltpu.roll(ag[9 * LEV + z], 4, 0),
    )
    for z in range(LEV):
        rv = x_b[end, z + 1, ROWS] - extra[0, z, ROWS]
        ext_out[0, z] = rv
        rv_out[0, z] = rv[HALO : HALO + CX]
        rv_out[1, z] = mv[0, z]
    strips(3, estrip.at[0], s_f.at[0, 0])
    ext_out[0, LEV] = s_b[end, 0, ROWS] - estrip[0, ROWS]

    for s in range(2):
        if s == 1:
            fill_winds(place, 1, we, wn, bg, ag, own, got, by, wind, wstrip)
        coefficients(place, wind, wstrip, coef, scoef, False)
        fill(
            x_f.at[0], 1, place, lambda z, s=s: v[s, z],
            lambda z, s=s: bg[s * LEV + z], lambda z, s=s: ag[s * LEV + z],
        )
        if s == 0:
            strips(0, s_f.at[0, 0], estrip.at[0])
        else:
            strips(0, estrip.at[0], s_f.at[0, 0])
        sweep(place, x_f, s_f, coef, scoef, counts[s])
        end = counts[s] & 1
        for z in range(LEV):
            out = x_f[end, z + 1, ROWS]
            if s == 0:
                ext_out[1, z] = out + extra[1, z, ROWS]
            else:
                ext_out[2, z] = out
                f1_out[z] = out[HALO : HALO + CX]
        out = s_f[end, 0, ROWS]
        ext_out[1 + s, LEV] = out + estrip[1, ROWS] if s == 0 else out


def lane_sum(x):
    return functools.reduce(
        lambda a, b: a + b, [x[:, i : i + CY] for i in range(0, x.shape[1], CY)]
    )


def second_kernel(
    counts, cells, ext, we, wn, lh, own, got, bg, ag, by, zt, zh,
    mv, h2, rm, ov,
    rv1_out, rl1_out, rl2_out, f21_out, b20_out, ql1_out, qv1_out, qm_out, dots_out,
    x_f, x_b, s_f, s_b, coef, scoef, wind, wstrip, extra, estrip,
):
    place = Place()
    clear(x_f, True)
    clear(x_b, True)
    for ref in (s_f, s_b, wind, wstrip, extra, estrip):
        clear(ref, False)
    tile = slice(HALO, HALO + CX)
    follows = jnp.where(lax.axis_index("tm") == lax.axis_size("tm") - 1, 0.0, 1.0)

    fill_winds(place, 1, we, wn, bg, ag, own, got, by, wind, wstrip)
    coefficients(place, wind, wstrip, coef, scoef, True)

    def z_tile(base):
        return lambda z: zt[base + 8 * z : base + 8 * z + 8].reshape(CX, CY)

    fill(x_b.at[0], 1, place, z_tile(0), lambda z: zh[z], lambda z: zh[16 + z])
    fill(
        extra.at[1], 0, place, z_tile(64),
        lambda z: pltpu.roll(zh[8 + z], 4, 0), lambda z: pltpu.roll(zh[24 + z], 4, 0),
    )
    fill_strips(
        s_b.at[0, 0], estrip.at[1], place,
        zt[128:136].reshape(CX, CY), zh[36:44].reshape(CX, CY),
        zh[32], zh[33], zh[34], zh[35],
    )
    sweep(place, x_b, s_b, coef, scoef, counts[1])
    end = counts[1] & 1

    fill(
        extra.at[0], 0, place, lambda z: lh[1, z],
        lambda z: bg[9 * LEV + z], lambda z: ag[9 * LEV + z],
    )
    fill_strips(
        s_f.at[0, 0], estrip.at[0], place, own[3], got[3, :CX],
        bg[10 * LEV + 3], by[3], ag[10 * LEV + 3], got[3, CX:],
    )
    for z in range(LEV):
        rv = x_b[end, z + 1, ROWS] - extra[0, z, ROWS]
        x_f[0, z + 1, ROWS] = rv
        rv1_out[z] = rv[tile]
        rl = (extra[1, z, ROWS] + ext[2, z]) * follows
        x_b[0, z + 1, ROWS] = rl
        rl2_out[z] = rl[tile]
    s_f[0, 0, ROWS] = s_b[end, 0, ROWS] - estrip[0, ROWS]
    s_b[0, 0, ROWS] = (estrip[1, ROWS] + ext[2, LEV]) * follows

    sweep(place, x_b, s_b, coef, scoef, counts[1])
    cross = jnp.zeros((8, CY), F32)
    square = jnp.zeros((8, CY), F32)

    def dots(r, q):
        return jnp.sum((r * q).reshape(-1, 8, CY), 0), jnp.sum((q * q).reshape(-1, 8, CY), 0)

    for z in range(LEV):
        rl1 = ext[1, z, tile]
        rl1_out[z] = rl1
        qv = rl1 - x_b[end, z + 1, TOP + HALO : TOP + HALO + CX] + h2[1, z]
        qv1_out[z] = qv
        c, q = dots(rv1_out[z], qv)
        cross, square = cross + c, square + q
    coefficients(place, wind, wstrip, coef, scoef, False)
    sweep(place, x_f, s_f, coef, scoef, counts[1])
    for z in range(LEV):
        f21_out[z] = x_f[end, z + 1, TOP + HALO : TOP + HALO + CX]

    end = counts[0] & 1
    fill_winds(place, 0, we, wn, bg, ag, own, got, by, wind, wstrip)
    coefficients(place, wind, wstrip, coef, scoef, False)
    for z in range(LEV):
        x_f[0, z + 1, ROWS] = ext[0, z]
        x_b[0, z + 1, ROWS] = ext[1, z]
    s_f[0, 0, ROWS] = ext[0, LEV]
    s_b[0, 0, ROWS] = ext[1, LEV]
    sweep(place, x_f, s_f, coef, scoef, counts[0])
    for z in range(LEV):
        rl1 = ext[1, z, tile]
        ql = mv[1, z] * rl1 + rv1_out[z] - x_f[end, z + 1, TOP + HALO : TOP + HALO + CX]
        ql1_out[z] = ql
        c, q = dots(rl1, ql)
        cross, square = cross + c, square + q
    coefficients(place, wind, wstrip, coef, scoef, True)
    sweep(place, x_b, s_b, coef, scoef, counts[0])
    for z in range(LEV):
        b20_out[z] = x_b[end, z + 1, TOP + HALO : TOP + HALO + CX]

    for s in range(2):
        rows, lanes = one_hots(cells[s, 0])
        if s == 0:
            field = ext[0, 0:LEV, tile].reshape(LEV * CX, CY)
        else:
            field = rv1_out[...].reshape(LEV * CX, CY)
        seen = gather(rows, lanes, field)
        r = rm[s, 0]
        q = ov[s, 0] * r + seen
        qm_out[s, 0] = q
        c, q = lane_sum(r * q), lane_sum(q * q)
        first = iota((8, CY), 0) == 0
        cross = cross + jnp.where(first, c, 0.0)
        square = square + jnp.where(first, q, 0.0)
    dots_out[0] = cross
    dots_out[1] = square


def dots_kernel(
    z_f, z_rv, rl2, f21, b20, z_own, h2, rv0, dots_in, rl0_out, qv0_out, send_out
):
    follows = jnp.where(lax.axis_index("tm") == lax.axis_size("tm") - 1, 0.0, 1.0)
    starts = jnp.where(lax.axis_index("tm") == 0, 1.0, 0.0)
    cross, square = dots_in[0], dots_in[1]

    def total(x):
        return jnp.sum(x.reshape(-1, 8, CY), 0)

    for z in range(LEV):
        rl0 = z_own[64 + 8 * z : 72 + 8 * z].reshape(CX, CY) + z_f[z]
        rv = rv0[0, z]
        qv = rl0 - b20[z] + h2[0, z]
        rl0_out[z] = rl0
        qv0_out[z] = qv
        ql = (rv0[1, z] * rl0 + rv) * starts
        rl2z = rl2[z]
        q2 = (z_rv[1, z] * rl2z + z_rv[0, z] - f21[z]) * follows
        cross += total(rv * qv) + total(rl0 * ql) + total(rl2z * q2)
        square += total(qv * qv) + total(ql * ql) + total(q2 * q2)
    cross = jnp.sum(jnp.sum(cross, 0, keepdims=True), 1, keepdims=True)
    square = jnp.sum(jnp.sum(square, 0, keepdims=True), 1, keepdims=True)
    n = send_out.shape[0]
    lane = iota((n, CY), 1)
    send_out[...] = jnp.where(lane == 0, cross, jnp.where(lane == 1, square, 0.0))


def last_kernel(
    sums, l, m, v, rl0, rl1, rv0, rv1, rm, z_f2, ql1, qv0, qv1, qm,
    l_out, m_out, v_out, a_out, b_out, c_out,
):
    total = jnp.sum(sums[...], 0, keepdims=True)
    lane = iota((1, CY), 1)
    cross = jnp.sum(jnp.where(lane == 0, total, 0.0), 1, keepdims=True)
    square = jnp.sum(jnp.where(lane == 1, total, 0.0), 1, keepdims=True)
    alpha = cross / (square + 1e-06)
    m_out[...] = m[...] + alpha * rm[...]
    b_out[...] = rm[...] - alpha * qm[...]
    for z in range(LEV):
        ql0 = rv0[1, z] * rl0[z] + rv0[0, z] - z_f2[z]
        l_out[0, z] = l[0, z] + alpha * rl0[z]
        l_out[1, z] = l[1, z] + alpha * rl1[z]
        v_out[0, z] = v[0, z] + alpha * rv0[0, z]
        v_out[1, z] = v[1, z] + alpha * rv1[z]
        a_out[0, z] = rl0[z] - alpha * ql0
        a_out[1, z] = rl1[z] - alpha * ql1[z]
        c_out[0, z] = rv0[0, z] - alpha * qv0[z]
        c_out[1, z] = rv1[z] - alpha * qv1[z]


def shards(sizes, l4, m4, v4, f4, d4, mv4, ov4, we4, wn4, cells4, counts):
    ntm, ngx, ngy = sizes
    tile = (LEV, CX, CY)
    obs = m4.shape

    def pair_b(i):
        return i - 1 if i % 2 == 0 else i + 1

    def plane(move_x, move_y):
        pairs = []
        for x in range(ngx):
            for y in range(ngy):
                to = move_x(x)
                if 0 <= to < ngx:
                    pairs.append((x * ngy + y, to * ngy + (1 - y if move_y else y)))
        return pairs

    axes = ("gx", "gy")
    down = [(i + 1, i) for i in range(ntm - 1)]
    up = [(i, i + 1) for i in range(ntm - 1)]
    edge = 10 * LEV

    fields = pltpu.VMEM((2,) + tile, F32)
    b_send, a_send, own, z_send, lh, g1 = call(
        pack_kernel,
        [(NBLOCKS, 8, CY)] * 2 + [(6, CX, CY), (136, 8, CY), (2,) + tile, tile],
        [cells4, m4, l4, f4, mv4, v4, we4, wn4],
        [fields, pltpu.VMEM(obs, jnp.int32), pltpu.VMEM(obs, F32)]
        + [fields] * 6
        + [pltpu.SemaphoreType.DMA((8,))],
        micros=2.5,
        fetched=range(8),
        limit=PACK_LIMIT,
    )
    ag = lax.ppermute(a_send, axes, plane(lambda i: i ^ 1, False))
    bg = lax.ppermute(b_send, axes, plane(pair_b, False))
    by = lax.ppermute(b_send[edge:], axes, plane(pair_b, True))
    y_send = jnp.concatenate([own, ag[edge:]], 1)
    y_send, late_cells = lax.optimization_barrier((y_send, cells4))
    got = lax.ppermute(y_send, axes, plane(lambda i: i, True))
    zt = lax.ppermute(z_send, "tm", down)
    rm, h2 = call(obs_kernel, [obs, (2,) + tile], [late_cells, m4, v4, d4, ov4], micros=2.4)

    z_edges = jnp.concatenate(
        [
            bg[2 * LEV : 3 * LEV], bg[8 * LEV : 9 * LEV],
            ag[2 * LEV : 3 * LEV], ag[8 * LEV : 9 * LEV],
            bg[edge + 1 : edge + 2], by[1:2], ag[edge + 1 : edge + 2], got[1:2, CX:],
            got[1, :CX].reshape(8, 8, CY),
        ],
        0,
    )
    zh = lax.ppermute(z_edges, "tm", down)
    scratch = [
        STATE, STATE, STRIP, STRIP, COEF, SCOEF, WIND, WSTRIP,
        pltpu.VMEM((2, LEV, BUF, CY), F32), pltpu.VMEM((2, BUF, CY), F32),
    ]
    ext, rv0, f1 = call(
        first_kernel,
        [(3, LEV + 1, EXT, CY), (2,) + tile, tile],
        [counts, v4, l4, we4, wn4, mv4, lh, g1, own, got, bg, ag, by],
        scratch,
        micros=5.0,
    )
    z_rv = lax.ppermute(rv0, "tm", down)
    z_f = lax.ppermute(f1, "tm", up)
    rv1, rl1, rl2, f21, b20, ql1, qv1, qm, dots = call(
        second_kernel,
        [tile] * 7 + [obs, (2, 8, CY)],
        [counts, cells4, ext, we4, wn4, lh, own, got, bg, ag, by, zt, zh, mv4, h2, rm, ov4],
        scratch,
        micros=9.0,
    )
    z_f2 = lax.ppermute(f21, "tm", up)
    n = ntm * ngx * ngy
    rl0, qv0, send = call(
        dots_kernel,
        [tile, tile, (n, CY)],
        [z_f, z_rv, rl2, f21, b20, z_send, h2, rv0, dots],
        micros=0.4,
    )
    sums = lax.all_to_all(send, ("tm", "gx", "gy"), 0, 0, tiled=True)
    return call(
        last_kernel,
        [l4.shape, obs, l4.shape, l4.shape, obs, l4.shape],
        [sums, l4, m4, v4, rl0, rl1, rv0, rv1, rm, z_f2, ql1, qv0, qv1, qm],
        micros=1.5,
    )


def solution(mesh):
    field = P("tm", None, "gx", "gy")
    obs = P("tm", "gx", "gy", None)
    sizes = tuple(mesh.shape[a] for a in ("tm", "gx", "gy"))
    return jax.shard_map(
        functools.partial(shards, sizes),
        mesh=mesh,
        in_specs=(field, obs, field, field, obs, field, obs, field, field, obs, P("tm")),
        out_specs=(field, obs, field, field, obs, field),
        check_vma=False,
    )
```

```python
import functools

import jax
import jax.numpy as jnp
from jax import lax
from jax.experimental import pallas as pl
from jax.experimental.pallas import tpu as pltpu
from jax.sharding import PartitionSpec as P

DIFFUSION = 0.18
VERTICAL = 0.1
CENTRE = 1.0 - 4.0 * DIFFUSION - 2.0 * VERTICAL

LEV, CX, CY = 8, 64, 128
HALO = 8
EXT = CX + 2 * HALO
TOP = 8
BUF = EXT + 2 * TOP
VMEM_LIMIT = 16 * 1024 * 1024
PACK_LIMIT = 60 * 1024 * 1024
NBLOCKS = 10 * LEV + 6
F32 = jnp.float32

VM = pl.BlockSpec(memory_space=pltpu.VMEM)
SM = pl.BlockSpec(memory_space=pltpu.SMEM)
FAR = pl.BlockSpec(memory_space=pltpu.HBM)


def call(body, outs, ins, scratch=(), micros=1.0, fetched=(), limit=VMEM_LIMIT):
    shapes = [jax.ShapeDtypeStruct(s, F32) for s in outs]
    nbytes = 4 * sum(int(a.size) for a in ins) + 4 * sum(
        functools.reduce(lambda a, b: a * b, s, 1) for s in outs
    )
    in_specs = [SM if (a.dtype == jnp.int32 and a.size < 64) else VM for a in ins]
    for i in fetched:
        in_specs[i] = FAR
    return pl.pallas_call(
        body,
        out_shape=shapes,
        in_specs=in_specs,
        out_specs=[VM] * len(shapes),
        scratch_shapes=list(scratch),
        compiler_params=pltpu.CompilerParams(vmem_limit_bytes=limit),
        cost_estimate=pl.CostEstimate(
            flops=int(1.1e9 * micros), bytes_accessed=nbytes, transcendentals=0
        ),
    )(*ins)


def iota(shape, dim):
    return lax.broadcasted_iota(jnp.int32, shape, dim)


def split(x):
    high = x.astype(jnp.bfloat16)
    low = (x - high.astype(F32)).astype(jnp.bfloat16)
    return high, low


def one_hots(cells):
    n = cells.shape[1]
    rows = (iota((LEV * CX, n), 0) == (cells >> 7)).astype(jnp.bfloat16)
    lanes = iota((CY, n), 0) == (cells & 127)
    return rows, lanes


def scatter(rows, lanes, values):
    high, low = split(values)
    zero = jnp.zeros((), jnp.bfloat16)
    parts = jnp.concatenate(
        [jnp.where(lanes, high.astype(F32), 0.0), jnp.where(lanes, low.astype(F32), 0.0)], 0
    ).astype(jnp.bfloat16)
    both = lax.dot_general(
        rows, parts, (((1,), (1,)), ((), ())), preferred_element_type=F32
    )
    return both[:, :CY] + both[:, CY:]


def gather(rows, lanes, field):
    high, low = split(field)
    both = lax.dot_general(
        jnp.concatenate([high, low], 1), rows, (((0,), (0,)), ((), ())),
        preferred_element_type=F32,
    )
    picked = both[:CY] + both[CY:]
    return jnp.sum(jnp.where(lanes, picked, 0.0), 0, keepdims=True)


def swap_halves(x):
    inner = (iota(x.shape, x.ndim - 1) & 15) < 8
    axis = x.ndim - 1
    return jnp.where(inner, pltpu.roll(x, CY - 8, axis), pltpu.roll(x, 8, axis))


def own_half(shape, gy):
    lane = iota(shape, len(shape) - 1) & 15
    return jnp.where(gy == 0, lane, lane ^ 8) < 8


def pack_kernel(
    cells_h, m_h, l_h, f_h, mv_h, v_h, we_h, wn_h,
    b_out, a_out, by_out, strip_out, z_out, lh_out, g1_out,
    g_s, cells, m, l, f, mv, v, we, wn, sems,
):
    far = (cells_h, m_h, l_h, f_h, mv_h, v_h, we_h, wn_h)
    near = (cells, m, l, f, mv, v, we, wn)
    copies = [pltpu.make_async_copy(a, b, sems.at[i]) for i, (a, b) in enumerate(zip(far, near))]
    for copy in copies:
        copy.start()
    copies[0].wait()
    copies[1].wait()
    core = lax.axis_index("gx") % 2
    gy = lax.axis_index("gy")
    lane = iota((CX, CY), 1)
    for s in range(2):
        rows, lanes = one_hots(cells[s, 0])
        h = scatter(rows, lanes, m[s, 0])
        if s == 0:
            for copy in copies[2:]:
                copy.wait()
        lh_out[s] = l[s] + h.reshape(LEV, CX, CY)
        g_s[s] = f[s] - mv[s] * l[s] - v[s]
    g1_out[...] = g_s[1]
    for z in range(LEV):
        for i in range(CX // 8):
            z_out[z * 8 + i] = l[0, z, 8 * i : 8 * i + 8]
            z_out[64 + z * 8 + i] = g_s[0, z, 8 * i : 8 * i + 8]

    def own(get):
        packed = jnp.zeros((CX, CY), F32)
        for z in range(LEV):
            rolled = pltpu.roll(get(z), (16 * z + 8) % CY, 1)
            packed = jnp.where((lane >> 4) == z, rolled, packed)
        return packed

    half = own_half((CX, CY), gy)
    pairs = (
        ((v, 0), (v, 1)), ((l, 0), (g_s, 0)), ((l, 1), (g_s, 1)),
        ((lh_out, 0), (lh_out, 1)), ((we, 0), (wn, 0)), ((we, 1), (wn, 1)),
    )
    for p, (one, two) in enumerate(pairs):
        first = own(lambda z, one=one: one[0][one[1], z])
        second = own(lambda z, two=two: two[0][two[1], z])
        strip_out[p] = jnp.where(half, first, swap_halves(second))
    for i in range(CX // 8):
        z_out[128 + i] = strip_out[1, 8 * i : 8 * i + 8]

    sub = iota((8, CY), 0)
    for out, top in ((b_out, core == 0), (a_out, core != 0)):
        row = jnp.where(top, 0, CX - 8)
        row = pl.multiple_of(row, 8)
        edge = pl.ds(row, 8)
        for k, field in enumerate((v, l, we, wn)):
            for s in range(2):
                out[pl.ds((2 * k + s) * LEV, LEV)] = field[s, :, edge, :]
        keep = jnp.where(top, sub, 7 - sub) < 4
        for s in range(2):
            for z in range(LEV):
                lh_edge = lh_out[s, z, edge, :]
                g_edge = pltpu.roll(g_s[s, z, edge, :], 4, 0)
                out[(8 + s) * LEV + z] = jnp.where(keep, lh_edge, g_edge)
        out[pl.ds(10 * LEV, 6)] = strip_out[:, edge, :]
    by_out[...] = b_out[10 * LEV :]


def obs_kernel(cells, m, v, dep, ov, rm_out, h2_out):
    for s in range(2):
        rows, lanes = one_hots(cells[s, 0])
        seen = gather(rows, lanes, v[s].reshape(LEV * CX, CY))
        rm = dep[s, 0] - (ov[s, 0] * m[s, 0] + seen)
        rm_out[s, 0] = rm
        h2_out[s] = scatter(rows, lanes, rm).reshape(LEV, CX, CY)


class Place:
    def __init__(self):
        gx = lax.axis_index("gx")
        self.gy = lax.axis_index("gy")
        core = gx % 2
        self.b_row = pl.multiple_of(jnp.where(core == 0, TOP, TOP + HALO + CX), 8)
        self.a_row = pl.multiple_of(jnp.where(core == 0, TOP + HALO + CX, TOP), 8)
        self.core = core
        self.ay_rows = pl.ds(pl.multiple_of(core * 8, 8), 8)
        self.low = jnp.where(gx == 0, 0.0, 1.0)
        self.high = jnp.where(gx == lax.axis_size("gx") - 1, 0.0, 1.0)


def clear(ref, guard_levels):
    lead = ref.shape[:-2]
    zero = jnp.zeros(lead + (TOP, CY), F32)
    ref[..., 0:TOP, :] = zero
    ref[..., BUF - TOP : BUF, :] = zero
    if guard_levels:
        full = jnp.zeros((BUF, CY), F32)
        for i in range(lead[0]):
            ref[i, 0] = full
            ref[i, LEV + 1] = full


def fill(dst, base, place, tile, b_block, a_block):
    for z in range(LEV):
        dst[base + z, TOP + HALO : TOP + HALO + CX] = tile(z)
        dst[base + z, pl.ds(place.b_row, 8)] = b_block(z)
        dst[base + z, pl.ds(place.a_row, 8)] = a_block(z)


def unpack(place, own, received):
    half = own_half(own.shape, place.gy)
    return jnp.where(half, own, received), swap_halves(jnp.where(half, received, own))


def fill_strips(first, second, place, own, got, own_b, got_b, own_a, got_a):
    mid = pl.ds(TOP + HALO, CX)
    for where, a, b in (
        (mid, own, got),
        (pl.ds(place.b_row, 8), own_b, got_b),
        (pl.ds(place.a_row, 8), own_a, got_a),
    ):
        one, two = unpack(place, a, b)
        first[where] = one
        second[where] = two


ROWS = slice(TOP, TOP + EXT)
UP = slice(TOP + 1, TOP + EXT + 1)
DOWN = slice(TOP - 1, TOP + EXT - 1)


def injected(strip, gy):
    lane = iota((EXT, CY), 1) & 15
    moved = jnp.where(gy == 0, pltpu.roll(strip, 119, 1), pltpu.roll(strip, 121, 1))
    return jnp.where(lane == jnp.where(gy == 0, 15, 0), moved, 0.0)


def coefficients(place, wind, strip, coef, scoef, adjoint):
    lane = iota((EXT, CY), 1)
    if not adjoint:
        for z in range(LEV):
            east, north = 0.5 * wind[0, z, ROWS], 0.5 * wind[1, z, ROWS]
            coef[0, z] = DIFFUSION - east
            coef[1, z] = DIFFUSION + east
            coef[2, z] = DIFFUSION - north
            coef[3, z] = DIFFUSION + north
        east, north = 0.5 * strip[0, ROWS], 0.5 * strip[1, ROWS]
        scoef[0] = DIFFUSION - east
        scoef[1] = DIFFUSION + east
        scoef[2] = DIFFUSION - north
        scoef[3] = DIFFUSION + north
        return
    inj = injected(strip[1, ROWS], place.gy)
    for z in range(LEV):
        north = wind[1, z, ROWS]
        edge = pltpu.roll(inj, (CY - 16 * z) % CY, 1)
        after = jnp.where(lane == CY - 1, edge, pltpu.roll(north, CY - 1, 1))
        before = jnp.where(lane == 0, edge, pltpu.roll(north, 1, 1))
        coef[0, z] = DIFFUSION + 0.5 * wind[0, z, UP]
        coef[1, z] = DIFFUSION - 0.5 * wind[0, z, DOWN]
        coef[2, z] = DIFFUSION + 0.5 * after
        coef[3, z] = DIFFUSION - 0.5 * before
    scoef[0] = DIFFUSION + 0.5 * strip[0, UP]
    scoef[1] = DIFFUSION - 0.5 * strip[0, DOWN]
    scoef[2] = DIFFUSION + 0.5 * pltpu.roll(strip[1, ROWS], CY - 1, 1)
    scoef[3] = DIFFUSION - 0.5 * pltpu.roll(strip[1, ROWS], 1, 1)


def store(dst, z, out, place):
    dst[z, TOP : TOP + HALO] = out[:HALO] * place.low
    dst[z, TOP + HALO : TOP + HALO + CX] = out[HALO : HALO + CX]
    dst[z, TOP + HALO + CX : TOP + EXT] = out[HALO + CX :] * place.high


def first_slot(count):
    return count & 1


def one_step(place, src, dst, ssrc, sdst, coef, scoef):
    lane = iota((EXT, CY), 1)
    own = ssrc[ROWS]
    inj = injected(own, place.gy)
    for z in range(LEV):
        mid = src[z + 1, ROWS]
        edge = pltpu.roll(inj, (CY - 16 * z) % CY, 1)
        after = jnp.where(lane == CY - 1, edge, pltpu.roll(mid, CY - 1, 1))
        before = jnp.where(lane == 0, edge, pltpu.roll(mid, 1, 1))
        out = (
            CENTRE * mid
            + coef[0, z] * src[z + 1, UP]
            + coef[1, z] * src[z + 1, DOWN]
            + coef[2, z] * after
            + coef[3, z] * before
            + VERTICAL * (src[z + 2, ROWS] + src[z, ROWS])
        )
        store(dst, z + 1, out, place)
    above = jnp.where(lane < CY - 16, pltpu.roll(own, CY - 16, 1), 0.0)
    below = jnp.where(lane >= 16, pltpu.roll(own, 16, 1), 0.0)
    out = (
        CENTRE * own
        + scoef[0] * ssrc[UP]
        + scoef[1] * ssrc[DOWN]
        + scoef[2] * pltpu.roll(own, CY - 1, 1)
        + scoef[3] * pltpu.roll(own, 1, 1)
        + VERTICAL * (above + below)
    )
    sdst[TOP : TOP + HALO] = out[:HALO] * place.low
    sdst[TOP + HALO : TOP + HALO + CX] = out[HALO : HALO + CX]
    sdst[TOP + HALO + CX : TOP + EXT] = out[HALO + CX :] * place.high


def sweep(place, state, strip, coef, scoef, count):
    def two(i, _):
        for j in range(2):

            @pl.when(2 * i + j >= 4 - count)
            def _():
                one_step(
                    place, state.at[j], state.at[1 - j], strip.at[j, 0], strip.at[1 - j, 0],
                    coef, scoef,
                )

        return 0

    lax.fori_loop(0, 2, two, 0)


STATE = pltpu.VMEM((2, LEV + 2, BUF, CY), F32)
STRIP = pltpu.VMEM((2, 1, BUF, CY), F32)
COEF = pltpu.VMEM((4, LEV, EXT, CY), F32)
SCOEF = pltpu.VMEM((4, EXT, CY), F32)
WIND = pltpu.VMEM((2, LEV, BUF, CY), F32)
WSTRIP = pltpu.VMEM((2, BUF, CY), F32)


def fill_winds(place, s, we, wn, bg, ag, own, got, by, ay, wind, wstrip):
    for k, field in enumerate((we, wn)):
        fill(
            wind.at[k], 0, place, lambda z, field=field: field[s, z],
            lambda z, k=k: bg[(4 + 2 * k + s) * LEV + z],
            lambda z, k=k: ag[(4 + 2 * k + s) * LEV + z],
        )
    p = 4 + s
    fill_strips(
        wstrip.at[0], wstrip.at[1], place, own[p], got[p],
        bg[10 * LEV + p], by[p], ag[10 * LEV + p], ay[p, place.ay_rows],
    )


def first_kernel(
    counts, v, l, we, wn, mv, lh, g1, own, got, bg, ag, by, ay,
    ext_out, rv_out, even_out, odd_out,
    x_f, x_b, s_f, s_b, coef, scoef, wind, wstrip, extra, estrip,
):
    place = Place()
    clear(x_f, True)
    clear(x_b, True)
    for ref in (s_f, s_b, wind, wstrip, extra, estrip):
        clear(ref, False)

    def strips(p, first, second):
        fill_strips(
            first, second, place, own[p], got[p],
            bg[10 * LEV + p], by[p], ag[10 * LEV + p], ay[p, place.ay_rows],
        )

    fill_winds(place, 0, we, wn, bg, ag, own, got, by, ay, wind, wstrip)
    fill(
        x_b.at[first_slot(counts[0])], 1, place, lambda z: l[1, z],
        lambda z: bg[3 * LEV + z], lambda z: ag[3 * LEV + z],
    )
    strips(2, s_b.at[first_slot(counts[0]), 0], estrip.at[1])
    coefficients(place, wind, wstrip, coef, scoef, True)
    sweep(place, x_b, s_b, coef, scoef, counts[0])
    end = 0
    fill(
        extra.at[0], 0, place, lambda z: lh[0, z],
        lambda z: bg[8 * LEV + z], lambda z: ag[8 * LEV + z],
    )
    fill(
        extra.at[1], 0, place, lambda z: g1[z],
        lambda z: pltpu.roll(bg[9 * LEV + z], 4, 0),
        lambda z: pltpu.roll(ag[9 * LEV + z], 4, 0),
    )
    for z in range(LEV):
        rv = x_b[end, z + 1, ROWS] - extra[0, z, ROWS]
        ext_out[0, z] = rv
        rv_out[0, z] = rv[HALO : HALO + CX]
        rv_out[1, z] = mv[0, z]
    strips(3, estrip.at[0], s_f.at[0, 0])
    ext_out[0, LEV] = s_b[end, 0, ROWS] - estrip[0, ROWS]

    for s in range(2):
        if s == 1:
            fill_winds(place, 1, we, wn, bg, ag, own, got, by, ay, wind, wstrip)
        coefficients(place, wind, wstrip, coef, scoef, False)
        fill(
            x_f.at[first_slot(counts[s])], 1, place, lambda z, s=s: v[s, z],
            lambda z, s=s: bg[s * LEV + z], lambda z, s=s: ag[s * LEV + z],
        )
        if s == 0:
            strips(0, s_f.at[first_slot(counts[s]), 0], estrip.at[0])
        else:
            strips(0, estrip.at[0], s_f.at[first_slot(counts[s]), 0])
        sweep(place, x_f, s_f, coef, scoef, counts[s])
        for z in range(LEV):
            out = x_f[end, z + 1, ROWS]
            if s == 0:
                ext_out[1, z] = out + extra[1, z, ROWS]
            else:
                ext_out[2, z] = out
        out = s_f[end, 0, ROWS]
        ext_out[1 + s, LEV] = out + estrip[1, ROWS] if s == 0 else out

    tile = slice(HALO, HALO + CX)
    odd = lax.axis_index("tm") % 2

    @pl.when(odd == 0)
    def _():
        even_out[0] = ext_out[2, :LEV, tile]
        even_out[1] = rv_out[1]
        odd_out[...] = rv_out[...]

    @pl.when(odd == 1)
    def _():
        even_out[...] = rv_out[...]
        odd_out[0] = ext_out[2, :LEV, tile]
        odd_out[1] = rv_out[1]


def lane_sum(x):
    return functools.reduce(
        lambda a, b: a + b, [x[:, i : i + CY] for i in range(0, x.shape[1], CY)]
    )


def second_kernel(
    counts, cells, ext, we, wn, lh, own, got, bg, ag, by, ay, zt, zh,
    mv, h2, rm, ov,
    rv1_out, rl1_out, rl2_out, f21_out, b20_out, ql1_out, qv1_out, qm_out, dots_out,
    x_f, x_b, s_f, s_b, coef, scoef, wind, wstrip, extra, estrip,
):
    place = Place()
    clear(x_f, True)
    clear(x_b, True)
    for ref in (s_f, s_b, wind, wstrip, extra, estrip):
        clear(ref, False)
    tile = slice(HALO, HALO + CX)
    follows = jnp.where(lax.axis_index("tm") == lax.axis_size("tm") - 1, 0.0, 1.0)

    fill_winds(place, 1, we, wn, bg, ag, own, got, by, ay, wind, wstrip)
    coefficients(place, wind, wstrip, coef, scoef, True)

    def z_tile(base):
        return lambda z: zt[base + 8 * z : base + 8 * z + 8].reshape(CX, CY)

    fill(x_b.at[first_slot(counts[1])], 1, place, z_tile(0), lambda z: zh[z], lambda z: zh[16 + z])
    fill(
        extra.at[1], 0, place, z_tile(64),
        lambda z: pltpu.roll(zh[8 + z], 4, 0), lambda z: pltpu.roll(zh[24 + z], 4, 0),
    )
    fill_strips(
        s_b.at[first_slot(counts[1]), 0], estrip.at[1], place,
        zt[128:136].reshape(CX, CY), zh[37:45].reshape(CX, CY),
        zh[32], zh[33], zh[34], zh[35 + place.core],
    )
    sweep(place, x_b, s_b, coef, scoef, counts[1])
    end = 0
    slot = first_slot(counts[1])

    fill(
        extra.at[0], 0, place, lambda z: lh[1, z],
        lambda z: bg[9 * LEV + z], lambda z: ag[9 * LEV + z],
    )
    fill_strips(
        s_f.at[0, 0], estrip.at[0], place, own[3], got[3],
        bg[10 * LEV + 3], by[3], ag[10 * LEV + 3], ay[3, place.ay_rows],
    )
    for z in range(LEV):
        rv = x_b[end, z + 1, ROWS] - extra[0, z, ROWS]
        x_f[slot, z + 1, ROWS] = rv
        rv1_out[z] = rv[tile]
        rl = (extra[1, z, ROWS] + ext[2, z]) * follows
        x_b[slot, z + 1, ROWS] = rl
        rl2_out[z] = rl[tile]
    s_f[slot, 0, ROWS] = s_b[end, 0, ROWS] - estrip[0, ROWS]
    s_b[slot, 0, ROWS] = (estrip[1, ROWS] + ext[2, LEV]) * follows

    sweep(place, x_b, s_b, coef, scoef, counts[1])
    cross = jnp.zeros((8, CY), F32)
    square = jnp.zeros((8, CY), F32)

    def dots(r, q):
        return jnp.sum((r * q).reshape(-1, 8, CY), 0), jnp.sum((q * q).reshape(-1, 8, CY), 0)

    for z in range(LEV):
        rl1 = ext[1, z, tile]
        rl1_out[z] = rl1
        qv = rl1 - x_b[end, z + 1, TOP + HALO : TOP + HALO + CX] + h2[1, z]
        qv1_out[z] = qv
        c, q = dots(rv1_out[z], qv)
        cross, square = cross + c, square + q
    coefficients(place, wind, wstrip, coef, scoef, False)
    sweep(place, x_f, s_f, coef, scoef, counts[1])
    for z in range(LEV):
        f21_out[z] = x_f[end, z + 1, TOP + HALO : TOP + HALO + CX]

    slot = first_slot(counts[0])
    fill_winds(place, 0, we, wn, bg, ag, own, got, by, ay, wind, wstrip)
    coefficients(place, wind, wstrip, coef, scoef, False)
    for z in range(LEV):
        x_f[slot, z + 1, ROWS] = ext[0, z]
        x_b[slot, z + 1, ROWS] = ext[1, z]
    s_f[slot, 0, ROWS] = ext[0, LEV]
    s_b[slot, 0, ROWS] = ext[1, LEV]
    sweep(place, x_f, s_f, coef, scoef, counts[0])
    for z in range(LEV):
        rl1 = ext[1, z, tile]
        ql = mv[1, z] * rl1 + rv1_out[z] - x_f[end, z + 1, TOP + HALO : TOP + HALO + CX]
        ql1_out[z] = ql
        c, q = dots(rl1, ql)
        cross, square = cross + c, square + q
    coefficients(place, wind, wstrip, coef, scoef, True)
    sweep(place, x_b, s_b, coef, scoef, counts[0])
    for z in range(LEV):
        b20_out[z] = x_b[end, z + 1, TOP + HALO : TOP + HALO + CX]

    for s in range(2):
        rows, lanes = one_hots(cells[s, 0])
        if s == 0:
            field = ext[0, 0:LEV, tile].reshape(LEV * CX, CY)
        else:
            field = rv1_out[...].reshape(LEV * CX, CY)
        seen = gather(rows, lanes, field)
        r = rm[s, 0]
        q = ov[s, 0] * r + seen
        qm_out[s, 0] = q
        c, q = lane_sum(r * q), lane_sum(q * q)
        first = iota((8, CY), 0) == 0
        cross = cross + jnp.where(first, c, 0.0)
        square = square + jnp.where(first, q, 0.0)
    dots_out[0] = cross
    dots_out[1] = square


def dots_kernel(
    even, odd, rl2, f21, b20, z_own, h2, rv0, dots_in, rl0_out, qv0_out, send_out
):
    follows = jnp.where(lax.axis_index("tm") == lax.axis_size("tm") - 1, 0.0, 1.0)
    starts = jnp.where(lax.axis_index("tm") == 0, 1.0, 0.0)
    cross, square = dots_in[0], dots_in[1]
    is_odd = lax.axis_index("tm") % 2 == 1

    def total(x):
        return jnp.sum(x.reshape(-1, 8, CY), 0)

    for z in range(LEV):
        rl0 = z_own[64 + 8 * z : 72 + 8 * z].reshape(CX, CY) + jnp.where(is_odd, even[0, z], odd[0, z])
        rv = rv0[0, z]
        qv = rl0 - b20[z] + h2[0, z]
        rl0_out[z] = rl0
        qv0_out[z] = qv
        ql = (rv0[1, z] * rl0 + rv) * starts
        rl2z = rl2[z]
        next_mv = jnp.where(is_odd, odd[1, z], even[1, z])
        next_rv = jnp.where(is_odd, odd[0, z], even[0, z])
        q2 = (next_mv * rl2z + next_rv - f21[z]) * follows
        cross += total(rv * qv) + total(rl0 * ql) + total(rl2z * q2)
        square += total(qv * qv) + total(ql * ql) + total(q2 * q2)
    cross = jnp.sum(jnp.sum(cross, 0, keepdims=True), 1, keepdims=True)
    square = jnp.sum(jnp.sum(square, 0, keepdims=True), 1, keepdims=True)
    n = send_out.shape[0]
    lane = iota((n, CY), 1)
    send_out[...] = jnp.where(lane == 0, cross, jnp.where(lane == 1, square, 0.0))


def last_kernel(
    sums, l, m, v, rl0, rl1, rv0, rv1, rm, z_f2, ql1, qv0, qv1, qm,
    l_out, m_out, v_out, a_out, b_out, c_out,
):
    total = jnp.sum(sums[...], 0, keepdims=True)
    lane = iota((1, CY), 1)
    cross = jnp.sum(jnp.where(lane == 0, total, 0.0), 1, keepdims=True)
    square = jnp.sum(jnp.where(lane == 1, total, 0.0), 1, keepdims=True)
    alpha = cross / (square + 1e-06)
    m_out[...] = m[...] + alpha * rm[...]
    b_out[...] = rm[...] - alpha * qm[...]
    for z in range(LEV):
        ql0 = rv0[1, z] * rl0[z] + rv0[0, z] - z_f2[z]
        l_out[0, z] = l[0, z] + alpha * rl0[z]
        l_out[1, z] = l[1, z] + alpha * rl1[z]
        v_out[0, z] = v[0, z] + alpha * rv0[0, z]
        v_out[1, z] = v[1, z] + alpha * rv1[z]
        a_out[0, z] = rl0[z] - alpha * ql0
        a_out[1, z] = rl1[z] - alpha * ql1[z]
        c_out[0, z] = rv0[0, z] - alpha * qv0[z]
        c_out[1, z] = rv1[z] - alpha * qv1[z]


def shards(sizes, l4, m4, v4, f4, d4, mv4, ov4, we4, wn4, cells4, counts):
    ntm, ngx, ngy = sizes
    tile = (LEV, CX, CY)
    obs = m4.shape

    def pair_b(i):
        return i - 1 if i % 2 == 0 else i + 1

    def plane(move_x, move_y):
        pairs = []
        for x in range(ngx):
            for y in range(ngy):
                to = move_x(x)
                if 0 <= to < ngx:
                    pairs.append((x * ngy + y, to * ngy + (1 - y if move_y else y)))
        return pairs

    axes = ("gx", "gy")
    down = [(i + 1, i) for i in range(ntm - 1)]
    up = [(i, i + 1) for i in range(ntm - 1)]
    edge = 10 * LEV

    fields = pltpu.VMEM((2,) + tile, F32)
    b_send, a_send, by_send, own, z_send, lh, g1 = call(
        pack_kernel,
        [(NBLOCKS, 8, CY)] * 2 + [(6, 8, CY), (6, CX, CY), (136, 8, CY), (2,) + tile, tile],
        [cells4, m4, l4, f4, mv4, v4, we4, wn4],
        [fields, pltpu.VMEM(obs, jnp.int32), pltpu.VMEM(obs, F32)]
        + [fields] * 6
        + [pltpu.SemaphoreType.DMA((8,))],
        micros=2.5,
        fetched=range(8),
        limit=PACK_LIMIT,
    )
    got = lax.ppermute(own, axes, plane(lambda i: i, True))
    bg = lax.ppermute(b_send, axes, plane(pair_b, False))
    ag = lax.ppermute(a_send, axes, plane(lambda i: i ^ 1, False))
    by = lax.ppermute(by_send, axes, plane(pair_b, True))
    zt = lax.ppermute(z_send, "tm", down)
    ay_send = jnp.concatenate([got[:, :8], got[:, CX - 8 :]], 1)
    ay_send, late_cells = lax.optimization_barrier((ay_send, cells4))
    ay = lax.ppermute(ay_send, axes, plane(lambda i: i ^ 1, False))
    rm, h2 = call(obs_kernel, [obs, (2,) + tile], [late_cells, m4, v4, d4, ov4], micros=2.4)

    z_edges = jnp.concatenate(
        [
            bg[2 * LEV : 3 * LEV], bg[8 * LEV : 9 * LEV],
            ag[2 * LEV : 3 * LEV], ag[8 * LEV : 9 * LEV],
            bg[edge + 1 : edge + 2], by[1:2], ag[edge + 1 : edge + 2],
            ay[1].reshape(2, 8, CY), got[1].reshape(8, 8, CY),
        ],
        0,
    )
    zh = lax.ppermute(z_edges, "tm", down)
    scratch = [
        STATE, STATE, STRIP, STRIP, COEF, SCOEF, WIND, WSTRIP,
        pltpu.VMEM((2, LEV, BUF, CY), F32), pltpu.VMEM((2, BUF, CY), F32),
    ]
    ext, rv0, even_send, odd_send = call(
        first_kernel,
        [(3, LEV + 1, EXT, CY)] + [(2,) + tile] * 3,
        [counts, v4, l4, we4, wn4, mv4, lh, g1, own, got, bg, ag, by, ay],
        scratch,
        micros=5.0,
    )
    swap = lambda first: [(i, i + 1) for i in range(first, ntm - 1, 2)] + [
        (i + 1, i) for i in range(first, ntm - 1, 2)
    ]
    even = lax.ppermute(even_send, "tm", swap(0))
    odd = lax.ppermute(odd_send, "tm", swap(1))
    rv1, rl1, rl2, f21, b20, ql1, qv1, qm, dots = call(
        second_kernel,
        [tile] * 7 + [obs, (2, 8, CY)],
        [counts, cells4, ext, we4, wn4, lh, own, got, bg, ag, by, ay, zt, zh, mv4, h2, rm, ov4],
        scratch,
        micros=9.0,
    )
    z_f2 = lax.ppermute(f21, "tm", up)
    n = ntm * ngx * ngy
    rl0, qv0, send = call(
        dots_kernel,
        [tile, tile, (n, CY)],
        [even, odd, rl2, f21, b20, z_send, h2, rv0, dots],
        micros=0.4,
    )
    sums = lax.all_to_all(send, ("tm", "gx", "gy"), 0, 0, tiled=True)
    return call(
        last_kernel,
        [l4.shape, obs, l4.shape, l4.shape, obs, l4.shape],
        [sums, l4, m4, v4, rl0, rl1, rv0, rv1, rm, z_f2, ql1, qv0, qv1, qm],
        micros=1.5,
    )


def solution(mesh):
    field = P("tm", None, "gx", "gy")
    obs = P("tm", "gx", "gy", None)
    sizes = tuple(mesh.shape[a] for a in ("tm", "gx", "gy"))
    return jax.shard_map(
        functools.partial(shards, sizes),
        mesh=mesh,
        in_specs=(field, obs, field, field, obs, field, obs, field, field, obs, P("tm")),
        out_specs=(field, obs, field, field, obs, field),
        check_vma=False,
    )
```

```python
import functools

import jax
import jax.numpy as jnp
from jax import lax
from jax.experimental import pallas as pl
from jax.experimental.pallas import tpu as pltpu
from jax.sharding import PartitionSpec as P

DIFFUSION = 0.18
VERTICAL = 0.1
CENTRE = 1.0 - 4.0 * DIFFUSION - 2.0 * VERTICAL

LEV, CX, CY = 8, 64, 128
HALO = 8
EXT = CX + 2 * HALO
TOP = 8
BUF = EXT + 2 * TOP
VMEM_LIMIT = 16 * 1024 * 1024
PACK_LIMIT = 60 * 1024 * 1024
NBLOCKS = 10 * LEV + 6
F32 = jnp.float32

VM = pl.BlockSpec(memory_space=pltpu.VMEM)
SM = pl.BlockSpec(memory_space=pltpu.SMEM)
FAR = pl.BlockSpec(memory_space=pltpu.HBM)


def call(body, outs, ins, scratch=(), micros=1.0, fetched=(), written=(), limit=VMEM_LIMIT):
    shapes = [jax.ShapeDtypeStruct(s, F32) for s in outs]
    nbytes = 4 * sum(int(a.size) for a in ins) + 4 * sum(
        functools.reduce(lambda a, b: a * b, s, 1) for s in outs
    )
    in_specs = [SM if (a.dtype == jnp.int32 and a.size < 64) else VM for a in ins]
    for i in fetched:
        in_specs[i] = FAR
    return pl.pallas_call(
        body,
        out_shape=shapes,
        in_specs=in_specs,
        out_specs=[FAR if i in written else VM for i in range(len(shapes))],
        scratch_shapes=list(scratch),
        compiler_params=pltpu.CompilerParams(vmem_limit_bytes=limit),
        cost_estimate=pl.CostEstimate(
            flops=int(1.1e9 * micros), bytes_accessed=nbytes, transcendentals=0
        ),
    )(*ins)


def iota(shape, dim):
    return lax.broadcasted_iota(jnp.int32, shape, dim)


def split(x):
    high = x.astype(jnp.bfloat16)
    low = (x - high.astype(F32)).astype(jnp.bfloat16)
    return high, low


def one_hots(cells):
    n = cells.shape[1]
    rows = (iota((LEV * CX, n), 0) == (cells >> 7)).astype(jnp.bfloat16)
    lanes = iota((CY, n), 0) == (cells & 127)
    return rows, lanes


def scatter(rows, lanes, values):
    high, low = split(values)
    zero = jnp.zeros((), jnp.bfloat16)
    parts = jnp.concatenate(
        [jnp.where(lanes, high.astype(F32), 0.0), jnp.where(lanes, low.astype(F32), 0.0)], 0
    ).astype(jnp.bfloat16)
    both = lax.dot_general(
        rows, parts, (((1,), (1,)), ((), ())), preferred_element_type=F32
    )
    return both[:, :CY] + both[:, CY:]


def gather(rows, lanes, field):
    high, low = split(field)
    both = lax.dot_general(
        jnp.concatenate([high, low], 1), rows, (((0,), (0,)), ((), ())),
        preferred_element_type=F32,
    )
    picked = both[:CY] + both[CY:]
    return jnp.sum(jnp.where(lanes, picked, 0.0), 0, keepdims=True)


def swap_halves(x):
    inner = (iota(x.shape, x.ndim - 1) & 15) < 8
    axis = x.ndim - 1
    return jnp.where(inner, pltpu.roll(x, CY - 8, axis), pltpu.roll(x, 8, axis))


def own_half(shape, gy):
    lane = iota(shape, len(shape) - 1) & 15
    return jnp.where(gy == 0, lane, lane ^ 8) < 8


def pack_kernel(
    cells_h, m_h, l_h, f_h, mv_h, v_h, we_h, wn_h,
    b_out, a_out, strip_out, z_out, lh_out, g1_out,
    g_s, cells, m, l, f, mv, v, we, wn, sems,
):
    far = (cells_h, m_h, l_h, f_h, mv_h, v_h, we_h, wn_h)
    near = (cells, m, l, f, mv, v, we, wn)
    copies = [pltpu.make_async_copy(a, b, sems.at[i]) for i, (a, b) in enumerate(zip(far, near))]
    for copy in copies:
        copy.start()
    copies[0].wait()
    copies[1].wait()
    core = lax.axis_index("gx") % 2
    gy = lax.axis_index("gy")
    lane = iota((CX, CY), 1)
    for s in range(2):
        rows, lanes = one_hots(cells[s, 0])
        h = scatter(rows, lanes, m[s, 0])
        if s == 0:
            for copy in copies[2:]:
                copy.wait()
        lh_out[s] = l[s] + h.reshape(LEV, CX, CY)
        g_s[s] = f[s] - mv[s] * l[s] - v[s]
    g1_out[...] = g_s[1]
    for z in range(LEV):
        for i in range(CX // 8):
            z_out[z * 8 + i] = l[0, z, 8 * i : 8 * i + 8]
            z_out[64 + z * 8 + i] = g_s[0, z, 8 * i : 8 * i + 8]

    def own(get):
        packed = jnp.zeros((CX, CY), F32)
        for z in range(LEV):
            rolled = pltpu.roll(get(z), (16 * z + 8) % CY, 1)
            packed = jnp.where((lane >> 4) == z, rolled, packed)
        return packed

    half = own_half((CX, CY), gy)
    pairs = (
        ((v, 0), (v, 1)), ((l, 0), (g_s, 0)), ((l, 1), (g_s, 1)),
        ((lh_out, 0), (lh_out, 1)), ((we, 0), (wn, 0)), ((we, 1), (wn, 1)),
    )
    for p, (one, two) in enumerate(pairs):
        first = own(lambda z, one=one: one[0][one[1], z])
        second = own(lambda z, two=two: two[0][two[1], z])
        strip_out[p] = jnp.where(half, first, swap_halves(second))
    for i in range(CX // 8):
        z_out[128 + i] = strip_out[1, 8 * i : 8 * i + 8]

    sub = iota((8, CY), 0)
    for out, top in ((b_out, core == 0), (a_out, core != 0)):
        row = jnp.where(top, 0, CX - 8)
        row = pl.multiple_of(row, 8)
        edge = pl.ds(row, 8)
        for k, field in enumerate((v, l, we, wn)):
            for s in range(2):
                out[pl.ds((2 * k + s) * LEV, LEV)] = field[s, :, edge, :]
        keep = jnp.where(top, sub, 7 - sub) < 4
        for s in range(2):
            for z in range(LEV):
                lh_edge = lh_out[s, z, edge, :]
                g_edge = pltpu.roll(g_s[s, z, edge, :], 4, 0)
                out[(8 + s) * LEV + z] = jnp.where(keep, lh_edge, g_edge)
        out[pl.ds(10 * LEV, 6)] = strip_out[:, edge, :]


def obs_kernel(cells, m, v, dep, ov, rm_out, h2_out):
    for s in range(2):
        rows, lanes = one_hots(cells[s, 0])
        seen = gather(rows, lanes, v[s].reshape(LEV * CX, CY))
        rm = dep[s, 0] - (ov[s, 0] * m[s, 0] + seen)
        rm_out[s, 0] = rm
        h2_out[s] = scatter(rows, lanes, rm).reshape(LEV, CX, CY)


class Place:
    def __init__(self):
        gx = lax.axis_index("gx")
        self.gy = lax.axis_index("gy")
        core = gx % 2
        self.b_row = pl.multiple_of(jnp.where(core == 0, TOP, TOP + HALO + CX), 8)
        self.a_row = pl.multiple_of(jnp.where(core == 0, TOP + HALO + CX, TOP), 8)
        self.core = core
        self.ay_rows = pl.ds(pl.multiple_of(core * 8, 8), 8)
        self.low = jnp.where(gx == 0, 0.0, 1.0)
        self.high = jnp.where(gx == lax.axis_size("gx") - 1, 0.0, 1.0)


def clear(ref, guard_levels):
    lead = ref.shape[:-2]
    zero = jnp.zeros(lead + (TOP, CY), F32)
    ref[..., 0:TOP, :] = zero
    ref[..., BUF - TOP : BUF, :] = zero
    if guard_levels:
        full = jnp.zeros((BUF, CY), F32)
        for i in range(lead[0]):
            ref[i, 0] = full
            ref[i, LEV + 1] = full


def fill(dst, base, place, tile, b_block, a_block):
    for z in range(LEV):
        dst[base + z, TOP + HALO : TOP + HALO + CX] = tile(z)
        dst[base + z, pl.ds(place.b_row, 8)] = b_block(z)
        dst[base + z, pl.ds(place.a_row, 8)] = a_block(z)


def unpack(place, own, received):
    half = own_half(own.shape, place.gy)
    return jnp.where(half, own, received), swap_halves(jnp.where(half, received, own))


def fill_strips(first, second, place, own, got, own_b, got_b, own_a, got_a):
    mid = pl.ds(TOP + HALO, CX)
    for where, a, b in (
        (mid, own, got),
        (pl.ds(place.b_row, 8), own_b, got_b),
        (pl.ds(place.a_row, 8), own_a, got_a),
    ):
        one, two = unpack(place, a, b)
        first[where] = one
        second[where] = two


ROWS = slice(TOP, TOP + EXT)
UP = slice(TOP + 1, TOP + EXT + 1)
DOWN = slice(TOP - 1, TOP + EXT - 1)


def injected(strip, gy):
    lane = iota((EXT, CY), 1) & 15
    moved = jnp.where(gy == 0, pltpu.roll(strip, 119, 1), pltpu.roll(strip, 121, 1))
    return jnp.where(lane == jnp.where(gy == 0, 15, 0), moved, 0.0)


def coefficients(place, wind, strip, coef, scoef, adjoint):
    lane = iota((EXT, CY), 1)
    if not adjoint:
        for z in range(LEV):
            east, north = 0.5 * wind[0, z, ROWS], 0.5 * wind[1, z, ROWS]
            coef[0, z] = DIFFUSION - east
            coef[1, z] = DIFFUSION + east
            coef[2, z] = DIFFUSION - north
            coef[3, z] = DIFFUSION + north
        east, north = 0.5 * strip[0, ROWS], 0.5 * strip[1, ROWS]
        scoef[0] = DIFFUSION - east
        scoef[1] = DIFFUSION + east
        scoef[2] = DIFFUSION - north
        scoef[3] = DIFFUSION + north
        return
    inj = injected(strip[1, ROWS], place.gy)
    for z in range(LEV):
        north = wind[1, z, ROWS]
        edge = pltpu.roll(inj, (CY - 16 * z) % CY, 1)
        after = jnp.where(lane == CY - 1, edge, pltpu.roll(north, CY - 1, 1))
        before = jnp.where(lane == 0, edge, pltpu.roll(north, 1, 1))
        coef[0, z] = DIFFUSION + 0.5 * wind[0, z, UP]
        coef[1, z] = DIFFUSION - 0.5 * wind[0, z, DOWN]
        coef[2, z] = DIFFUSION + 0.5 * after
        coef[3, z] = DIFFUSION - 0.5 * before
    scoef[0] = DIFFUSION + 0.5 * strip[0, UP]
    scoef[1] = DIFFUSION - 0.5 * strip[0, DOWN]
    scoef[2] = DIFFUSION + 0.5 * pltpu.roll(strip[1, ROWS], CY - 1, 1)
    scoef[3] = DIFFUSION - 0.5 * pltpu.roll(strip[1, ROWS], 1, 1)


def store(dst, z, out, place):
    dst[z, TOP : TOP + HALO] = out[:HALO] * place.low
    dst[z, TOP + HALO : TOP + HALO + CX] = out[HALO : HALO + CX]
    dst[z, TOP + HALO + CX : TOP + EXT] = out[HALO + CX :] * place.high


def first_slot(count):
    return count & 1


def one_step(place, src, dst, ssrc, sdst, coef, scoef):
    lane = iota((EXT, CY), 1)
    own = ssrc[ROWS]
    inj = injected(own, place.gy)
    for z in range(LEV):
        mid = src[z + 1, ROWS]
        edge = pltpu.roll(inj, (CY - 16 * z) % CY, 1)
        after = jnp.where(lane == CY - 1, edge, pltpu.roll(mid, CY - 1, 1))
        before = jnp.where(lane == 0, edge, pltpu.roll(mid, 1, 1))
        out = (
            CENTRE * mid
            + coef[0, z] * src[z + 1, UP]
            + coef[1, z] * src[z + 1, DOWN]
            + coef[2, z] * after
            + coef[3, z] * before
            + VERTICAL * (src[z + 2, ROWS] + src[z, ROWS])
        )
        store(dst, z + 1, out, place)
    above = jnp.where(lane < CY - 16, pltpu.roll(own, CY - 16, 1), 0.0)
    below = jnp.where(lane >= 16, pltpu.roll(own, 16, 1), 0.0)
    out = (
        CENTRE * own
        + scoef[0] * ssrc[UP]
        + scoef[1] * ssrc[DOWN]
        + scoef[2] * pltpu.roll(own, CY - 1, 1)
        + scoef[3] * pltpu.roll(own, 1, 1)
        + VERTICAL * (above + below)
    )
    sdst[TOP : TOP + HALO] = out[:HALO] * place.low
    sdst[TOP + HALO : TOP + HALO + CX] = out[HALO : HALO + CX]
    sdst[TOP + HALO + CX : TOP + EXT] = out[HALO + CX :] * place.high


def sweep(place, state, strip, coef, scoef, count):
    def two(i, _):
        for j in range(2):

            @pl.when(2 * i + j >= 4 - count)
            def _():
                one_step(
                    place, state.at[j], state.at[1 - j], strip.at[j, 0], strip.at[1 - j, 0],
                    coef, scoef,
                )

        return 0

    lax.fori_loop(0, 2, two, 0)


STATE = pltpu.VMEM((2, LEV + 2, BUF, CY), F32)
STRIP = pltpu.VMEM((2, 1, BUF, CY), F32)
COEF = pltpu.VMEM((4, LEV, EXT, CY), F32)
SCOEF = pltpu.VMEM((4, EXT, CY), F32)
WIND = pltpu.VMEM((2, LEV, BUF, CY), F32)
WSTRIP = pltpu.VMEM((2, BUF, CY), F32)


def fill_winds(place, s, we, wn, bg, ag, own, got, by, ay, wind, wstrip):
    for k, field in enumerate((we, wn)):
        fill(
            wind.at[k], 0, place, lambda z, field=field: field[s, z],
            lambda z, k=k: bg[(4 + 2 * k + s) * LEV + z],
            lambda z, k=k: ag[(4 + 2 * k + s) * LEV + z],
        )
    p = 4 + s
    fill_strips(
        wstrip.at[0], wstrip.at[1], place, own[p], got[p],
        bg[10 * LEV + p], by[p], ag[10 * LEV + p], ay[p, place.ay_rows],
    )


def first_kernel(
    counts, v, l, we, wn, mv, lh, g1, own, got, bg, ag, by, ay,
    ext_out, rv_out, even_out, odd_out,
    x_f, x_b, s_f, s_b, coef, scoef, wind, wstrip, extra, estrip,
):
    place = Place()
    clear(x_f, True)
    clear(x_b, True)
    for ref in (s_f, s_b, wind, wstrip, extra, estrip):
        clear(ref, False)

    def strips(p, first, second):
        fill_strips(
            first, second, place, own[p], got[p],
            bg[10 * LEV + p], by[p], ag[10 * LEV + p], ay[p, place.ay_rows],
        )

    fill_winds(place, 0, we, wn, bg, ag, own, got, by, ay, wind, wstrip)
    fill(
        x_b.at[first_slot(counts[0])], 1, place, lambda z: l[1, z],
        lambda z: bg[3 * LEV + z], lambda z: ag[3 * LEV + z],
    )
    strips(2, s_b.at[first_slot(counts[0]), 0], estrip.at[1])
    coefficients(place, wind, wstrip, coef, scoef, True)
    sweep(place, x_b, s_b, coef, scoef, counts[0])
    end = 0
    fill(
        extra.at[0], 0, place, lambda z: lh[0, z],
        lambda z: bg[8 * LEV + z], lambda z: ag[8 * LEV + z],
    )
    fill(
        extra.at[1], 0, place, lambda z: g1[z],
        lambda z: pltpu.roll(bg[9 * LEV + z], 4, 0),
        lambda z: pltpu.roll(ag[9 * LEV + z], 4, 0),
    )
    for z in range(LEV):
        rv = x_b[end, z + 1, ROWS] - extra[0, z, ROWS]
        ext_out[0, z] = rv
        rv_out[0, z] = rv[HALO : HALO + CX]
        rv_out[1, z] = mv[0, z]
    strips(3, estrip.at[0], s_f.at[0, 0])
    ext_out[0, LEV] = s_b[end, 0, ROWS] - estrip[0, ROWS]

    for s in range(2):
        if s == 1:
            fill_winds(place, 1, we, wn, bg, ag, own, got, by, ay, wind, wstrip)
        coefficients(place, wind, wstrip, coef, scoef, False)
        fill(
            x_f.at[first_slot(counts[s])], 1, place, lambda z, s=s: v[s, z],
            lambda z, s=s: bg[s * LEV + z], lambda z, s=s: ag[s * LEV + z],
        )
        if s == 0:
            strips(0, s_f.at[first_slot(counts[s]), 0], estrip.at[0])
        else:
            strips(0, estrip.at[0], s_f.at[first_slot(counts[s]), 0])
        sweep(place, x_f, s_f, coef, scoef, counts[s])
        for z in range(LEV):
            out = x_f[end, z + 1, ROWS]
            if s == 0:
                ext_out[1, z] = out + extra[1, z, ROWS]
            else:
                ext_out[2, z] = out
        out = s_f[end, 0, ROWS]
        ext_out[1 + s, LEV] = out + estrip[1, ROWS] if s == 0 else out

    tile = slice(HALO, HALO + CX)
    odd = lax.axis_index("tm") % 2

    @pl.when(odd == 0)
    def _():
        even_out[0] = ext_out[2, :LEV, tile]
        even_out[1] = rv_out[1]
        odd_out[...] = rv_out[...]

    @pl.when(odd == 1)
    def _():
        even_out[...] = rv_out[...]
        odd_out[0] = ext_out[2, :LEV, tile]
        odd_out[1] = rv_out[1]


def lane_sum(x):
    return functools.reduce(
        lambda a, b: a + b, [x[:, i : i + CY] for i in range(0, x.shape[1], CY)]
    )


def second_kernel(
    counts, cells, ext, we, wn, lh, own, got, bg, ag, by, ay, zt, zh_even, zh_odd,
    mv, h2, rm, ov,
    rv1_out, rl1_out, rl2_out, f21_out, b20_out, ql1_out, qv1_out, qm_out, dots_out,
    x_f, x_b, s_f, s_b, coef, scoef, wind, wstrip, extra, estrip,
):
    place = Place()
    clear(x_f, True)
    clear(x_b, True)
    for ref in (s_f, s_b, wind, wstrip, extra, estrip):
        clear(ref, False)
    tile = slice(HALO, HALO + CX)
    follows = jnp.where(lax.axis_index("tm") == lax.axis_size("tm") - 1, 0.0, 1.0)

    def zh(i):
        return zh_even[i] + zh_odd[i]

    fill_winds(place, 1, we, wn, bg, ag, own, got, by, ay, wind, wstrip)
    coefficients(place, wind, wstrip, coef, scoef, True)

    def z_tile(base):
        return lambda z: zt[base + 8 * z : base + 8 * z + 8].reshape(CX, CY)

    fill(x_b.at[first_slot(counts[1])], 1, place, z_tile(0), lambda z: zh(z), lambda z: zh(16 + z))
    fill(
        extra.at[1], 0, place, z_tile(64),
        lambda z: pltpu.roll(zh(8 + z), 4, 0), lambda z: pltpu.roll(zh(24 + z), 4, 0),
    )
    fill_strips(
        s_b.at[first_slot(counts[1]), 0], estrip.at[1], place,
        zt[128:136].reshape(CX, CY), zh(slice(37, 45)).reshape(CX, CY),
        zh(32), zh(33), zh(34), zh(35 + place.core),
    )
    sweep(place, x_b, s_b, coef, scoef, counts[1])
    end = 0
    slot = first_slot(counts[1])

    fill(
        extra.at[0], 0, place, lambda z: lh[1, z],
        lambda z: bg[9 * LEV + z], lambda z: ag[9 * LEV + z],
    )
    fill_strips(
        s_f.at[0, 0], estrip.at[0], place, own[3], got[3],
        bg[10 * LEV + 3], by[3], ag[10 * LEV + 3], ay[3, place.ay_rows],
    )
    for z in range(LEV):
        rv = x_b[end, z + 1, ROWS] - extra[0, z, ROWS]
        x_f[slot, z + 1, ROWS] = rv
        rv1_out[z] = rv[tile]
        rl = (extra[1, z, ROWS] + ext[2, z]) * follows
        x_b[slot, z + 1, ROWS] = rl
        rl2_out[z] = rl[tile]
    s_f[slot, 0, ROWS] = s_b[end, 0, ROWS] - estrip[0, ROWS]
    s_b[slot, 0, ROWS] = (estrip[1, ROWS] + ext[2, LEV]) * follows

    sweep(place, x_b, s_b, coef, scoef, counts[1])
    cross = jnp.zeros((8, CY), F32)
    square = jnp.zeros((8, CY), F32)

    def dots(r, q):
        return jnp.sum((r * q).reshape(-1, 8, CY), 0), jnp.sum((q * q).reshape(-1, 8, CY), 0)

    for z in range(LEV):
        rl1 = ext[1, z, tile]
        rl1_out[z] = rl1
        qv = rl1 - x_b[end, z + 1, TOP + HALO : TOP + HALO + CX] + h2[1, z]
        qv1_out[z] = qv
        c, q = dots(rv1_out[z], qv)
        cross, square = cross + c, square + q
    coefficients(place, wind, wstrip, coef, scoef, False)
    sweep(place, x_f, s_f, coef, scoef, counts[1])
    for z in range(LEV):
        f21_out[z] = x_f[end, z + 1, TOP + HALO : TOP + HALO + CX]

    slot = first_slot(counts[0])
    fill_winds(place, 0, we, wn, bg, ag, own, got, by, ay, wind, wstrip)
    coefficients(place, wind, wstrip, coef, scoef, False)
    for z in range(LEV):
        x_f[slot, z + 1, ROWS] = ext[0, z]
        x_b[slot, z + 1, ROWS] = ext[1, z]
    s_f[slot, 0, ROWS] = ext[0, LEV]
    s_b[slot, 0, ROWS] = ext[1, LEV]
    sweep(place, x_f, s_f, coef, scoef, counts[0])
    for z in range(LEV):
        rl1 = ext[1, z, tile]
        ql = mv[1, z] * rl1 + rv1_out[z] - x_f[end, z + 1, TOP + HALO : TOP + HALO + CX]
        ql1_out[z] = ql
        c, q = dots(rl1, ql)
        cross, square = cross + c, square + q
    coefficients(place, wind, wstrip, coef, scoef, True)
    sweep(place, x_b, s_b, coef, scoef, counts[0])
    for z in range(LEV):
        b20_out[z] = x_b[end, z + 1, TOP + HALO : TOP + HALO + CX]

    for s in range(2):
        rows, lanes = one_hots(cells[s, 0])
        if s == 0:
            field = ext[0, 0:LEV, tile].reshape(LEV * CX, CY)
        else:
            field = rv1_out[...].reshape(LEV * CX, CY)
        seen = gather(rows, lanes, field)
        r = rm[s, 0]
        q = ov[s, 0] * r + seen
        qm_out[s, 0] = q
        c, q = lane_sum(r * q), lane_sum(q * q)
        first = iota((8, CY), 0) == 0
        cross = cross + jnp.where(first, c, 0.0)
        square = square + jnp.where(first, q, 0.0)
    dots_out[0] = cross
    dots_out[1] = square


def dots_kernel(
    even, odd, rl2, f21, b20, z_own, h2, rv0, dots_in, rl0_out, qv0_out, send_out
):
    follows = jnp.where(lax.axis_index("tm") == lax.axis_size("tm") - 1, 0.0, 1.0)
    starts = jnp.where(lax.axis_index("tm") == 0, 1.0, 0.0)
    cross, square = dots_in[0], dots_in[1]
    is_odd = lax.axis_index("tm") % 2 == 1

    def total(x):
        return jnp.sum(x.reshape(-1, 8, CY), 0)

    for z in range(LEV):
        rl0 = z_own[64 + 8 * z : 72 + 8 * z].reshape(CX, CY) + jnp.where(is_odd, even[0, z], odd[0, z])
        rv = rv0[0, z]
        qv = rl0 - b20[z] + h2[0, z]
        rl0_out[z] = rl0
        qv0_out[z] = qv
        ql = (rv0[1, z] * rl0 + rv) * starts
        rl2z = rl2[z]
        next_mv = jnp.where(is_odd, odd[1, z], even[1, z])
        next_rv = jnp.where(is_odd, odd[0, z], even[0, z])
        q2 = (next_mv * rl2z + next_rv - f21[z]) * follows
        cross += total(rv * qv) + total(rl0 * ql) + total(rl2z * q2)
        square += total(qv * qv) + total(ql * ql) + total(q2 * q2)
    cross = jnp.sum(jnp.sum(cross, 0, keepdims=True), 1, keepdims=True)
    square = jnp.sum(jnp.sum(square, 0, keepdims=True), 1, keepdims=True)
    n = send_out.shape[0]
    lane = iota((n, CY), 1)
    send_out[...] = jnp.where(lane == 0, cross, jnp.where(lane == 1, square, 0.0))


def last_kernel(
    sums, l, m, v, rl0, rl1, rv0, rv1, rm, f2_even, f2_odd, ql1, qv0, qv1_far, qm_far,
    l_far, m_out, v_far, a_far, b_out, c_far,
    qv1, qm, l_out, v_out, a_out, c_out, sems,
):
    fetches = [
        pltpu.make_async_copy(qv1_far, qv1, sems.at[0]),
        pltpu.make_async_copy(qm_far, qm, sems.at[1]),
    ]
    for copy in fetches:
        copy.start()
    writes = [
        pltpu.make_async_copy(near, far, sems.at[2 + i])
        for i, (near, far) in enumerate(
            ((l_out, l_far), (v_out, v_far), (a_out, a_far), (c_out, c_far))
        )
    ]
    total = jnp.sum(sums[...], 0, keepdims=True)
    lane = iota((1, CY), 1)
    cross = jnp.sum(jnp.where(lane == 0, total, 0.0), 1, keepdims=True)
    square = jnp.sum(jnp.where(lane == 1, total, 0.0), 1, keepdims=True)
    alpha = cross / (square + 1e-06)
    for z in range(LEV):
        l_out[0, z] = l[0, z] + alpha * rl0[z]
        l_out[1, z] = l[1, z] + alpha * rl1[z]
    writes[0].start()
    for z in range(LEV):
        v_out[0, z] = v[0, z] + alpha * rv0[0, z]
        v_out[1, z] = v[1, z] + alpha * rv1[z]
    writes[1].start()
    for z in range(LEV):
        ql0 = rv0[1, z] * rl0[z] + rv0[0, z] - (f2_even[z] + f2_odd[z])
        a_out[0, z] = rl0[z] - alpha * ql0
        a_out[1, z] = rl1[z] - alpha * ql1[z]
    writes[2].start()
    for copy in fetches:
        copy.wait()
    for z in range(LEV):
        c_out[0, z] = rv0[0, z] - alpha * qv0[z]
        c_out[1, z] = rv1[z] - alpha * qv1[z]
    writes[3].start()
    m_out[...] = m[...] + alpha * rm[...]
    b_out[...] = rm[...] - alpha * qm[...]
    for copy in writes:
        copy.wait()


def shards(sizes, l4, m4, v4, f4, d4, mv4, ov4, we4, wn4, cells4, counts):
    ntm, ngx, ngy = sizes
    tile = (LEV, CX, CY)
    obs = m4.shape

    def pair_b(i):
        return i - 1 if i % 2 == 0 else i + 1

    def plane(move_x, move_y):
        pairs = []
        for x in range(ngx):
            for y in range(ngy):
                to = move_x(x)
                if 0 <= to < ngx:
                    pairs.append((x * ngy + y, to * ngy + (1 - y if move_y else y)))
        return pairs

    axes = ("gx", "gy")
    down = [(i + 1, i) for i in range(ntm - 1)]
    up = [(i, i + 1) for i in range(ntm - 1)]
    edge = 10 * LEV

    fields = pltpu.VMEM((2,) + tile, F32)
    b_send, a_send, own, z_send, lh, g1 = call(
        pack_kernel,
        [(NBLOCKS, 8, CY)] * 2 + [(6, CX, CY), (136, 8, CY), (2,) + tile, tile],
        [cells4, m4, l4, f4, mv4, v4, we4, wn4],
        [fields, pltpu.VMEM(obs, jnp.int32), pltpu.VMEM(obs, F32)]
        + [fields] * 6
        + [pltpu.SemaphoreType.DMA((8,))],
        micros=2.5,
        fetched=range(8),
        limit=PACK_LIMIT,
    )
    got = lax.ppermute(own, axes, plane(lambda i: i, True))
    bg = lax.ppermute(b_send, axes, plane(pair_b, False))
    ag = lax.ppermute(a_send, axes, plane(lambda i: i ^ 1, False))
    by = lax.ppermute(b_send[edge:], axes, plane(pair_b, True))
    zt = lax.ppermute(z_send, "tm", down)
    ay_send = jnp.concatenate([got[:, :8], got[:, CX - 8 :]], 1)
    ay_send, late_cells = lax.optimization_barrier((ay_send, cells4))
    ay = lax.ppermute(ay_send, axes, plane(lambda i: i ^ 1, False))
    rm, h2 = call(obs_kernel, [obs, (2,) + tile], [late_cells, m4, v4, d4, ov4], micros=2.4)

    z_edges = jnp.concatenate(
        [
            bg[2 * LEV : 3 * LEV], bg[8 * LEV : 9 * LEV],
            ag[2 * LEV : 3 * LEV], ag[8 * LEV : 9 * LEV],
            bg[edge + 1 : edge + 2], by[1:2], ag[edge + 1 : edge + 2],
            ay[1].reshape(2, 8, CY), got[1].reshape(8, 8, CY),
        ],
        0,
    )
    zh_even = lax.ppermute(z_edges, "tm", down[0::2])
    zh_odd = lax.ppermute(z_edges, "tm", down[1::2])
    scratch = [
        STATE, STATE, STRIP, STRIP, COEF, SCOEF, WIND, WSTRIP,
        pltpu.VMEM((2, LEV, BUF, CY), F32), pltpu.VMEM((2, BUF, CY), F32),
    ]
    ext, rv0, even_send, odd_send = call(
        first_kernel,
        [(3, LEV + 1, EXT, CY)] + [(2,) + tile] * 3,
        [counts, v4, l4, we4, wn4, mv4, lh, g1, own, got, bg, ag, by, ay],
        scratch,
        micros=5.0,
    )
    swap = lambda first: [(i, i + 1) for i in range(first, ntm - 1, 2)] + [
        (i + 1, i) for i in range(first, ntm - 1, 2)
    ]
    even = lax.ppermute(even_send, "tm", swap(0))
    odd = lax.ppermute(odd_send, "tm", swap(1))
    rv1, rl1, rl2, f21, b20, ql1, qv1, qm, dots = call(
        second_kernel,
        [tile] * 7 + [obs, (2, 8, CY)],
        [counts, cells4, ext, we4, wn4, lh, own, got, bg, ag, by, ay, zt, zh_even, zh_odd, mv4, h2, rm, ov4],
        scratch,
        micros=9.0,
    )
    f2_even = lax.ppermute(f21, "tm", up[0::2])
    f2_odd = lax.ppermute(f21, "tm", up[1::2])
    n = ntm * ngx * ngy
    rl0, qv0, send = call(
        dots_kernel,
        [tile, tile, (n, CY)],
        [even, odd, rl2, f21, b20, z_send, h2, rv0, dots],
        micros=0.4,
    )
    sums = lax.all_to_all(send, ("tm", "gx", "gy"), 0, 0, tiled=True)
    return call(
        last_kernel,
        [l4.shape, obs, l4.shape, l4.shape, obs, l4.shape],
        [sums, l4, m4, v4, rl0, rl1, rv0, rv1, rm, f2_even, f2_odd, ql1, qv0, qv1, qm],
        [pltpu.VMEM(tile, F32), pltpu.VMEM(obs, F32)]
        + [fields] * 4
        + [pltpu.SemaphoreType.DMA((6,))],
        micros=1.5,
        fetched=(13, 14),
        written=(0, 2, 3, 5),
    )


def solution(mesh):
    field = P("tm", None, "gx", "gy")
    obs = P("tm", "gx", "gy", None)
    sizes = tuple(mesh.shape[a] for a in ("tm", "gx", "gy"))
    return jax.shard_map(
        functools.partial(shards, sizes),
        mesh=mesh,
        in_specs=(field, obs, field, field, obs, field, obs, field, field, obs, P("tm")),
        out_specs=(field, obs, field, field, obs, field),
        check_vma=False,
    )
```

```python
import functools

import jax
import jax.numpy as jnp
from jax import lax
from jax.experimental import pallas as pl
from jax.experimental.pallas import tpu as pltpu
from jax.sharding import PartitionSpec as P

DIFFUSION = 0.18
VERTICAL = 0.1
CENTRE = 1.0 - 4.0 * DIFFUSION - 2.0 * VERTICAL

LEV, CX, CY = 8, 64, 128
HALO = 8
EXT = CX + 2 * HALO
TOP = 8
BUF = EXT + 2 * TOP
VMEM_LIMIT = 16 * 1024 * 1024
PACK_LIMIT = 60 * 1024 * 1024
NBLOCKS = 10 * LEV + 6
F32 = jnp.float32

VM = pl.BlockSpec(memory_space=pltpu.VMEM)
SM = pl.BlockSpec(memory_space=pltpu.SMEM)
FAR = pl.BlockSpec(memory_space=pltpu.HBM)


def call(body, outs, ins, scratch=(), micros=1.0, fetched=(), written=(), limit=VMEM_LIMIT):
    shapes = [jax.ShapeDtypeStruct(s, F32) for s in outs]
    nbytes = 4 * sum(int(a.size) for a in ins) + 4 * sum(
        functools.reduce(lambda a, b: a * b, s, 1) for s in outs
    )
    in_specs = [SM if (a.dtype == jnp.int32 and a.size < 64) else VM for a in ins]
    for i in fetched:
        in_specs[i] = FAR
    return pl.pallas_call(
        body,
        out_shape=shapes,
        in_specs=in_specs,
        out_specs=[FAR if i in written else VM for i in range(len(shapes))],
        scratch_shapes=list(scratch),
        compiler_params=pltpu.CompilerParams(vmem_limit_bytes=limit),
        cost_estimate=pl.CostEstimate(
            flops=int(1.1e9 * micros), bytes_accessed=nbytes, transcendentals=0
        ),
    )(*ins)


def iota(shape, dim):
    return lax.broadcasted_iota(jnp.int32, shape, dim)


def split(x):
    high = x.astype(jnp.bfloat16)
    low = (x - high.astype(F32)).astype(jnp.bfloat16)
    return high, low


def one_hots(cells):
    n = cells.shape[1]
    rows = (iota((LEV * CX, n), 0) == (cells >> 7)).astype(jnp.bfloat16)
    lanes = iota((CY, n), 0) == (cells & 127)
    return rows, lanes


def scatter(rows, lanes, values):
    high, low = split(values)
    zero = jnp.zeros((), jnp.bfloat16)
    parts = jnp.concatenate(
        [jnp.where(lanes, high.astype(F32), 0.0), jnp.where(lanes, low.astype(F32), 0.0)], 0
    ).astype(jnp.bfloat16)
    both = lax.dot_general(
        rows, parts, (((1,), (1,)), ((), ())), preferred_element_type=F32
    )
    return both[:, :CY] + both[:, CY:]


def gather(rows, lanes, field):
    high, low = split(field)
    both = lax.dot_general(
        jnp.concatenate([high, low], 1), rows, (((0,), (0,)), ((), ())),
        preferred_element_type=F32,
    )
    picked = both[:CY] + both[CY:]
    return jnp.sum(jnp.where(lanes, picked, 0.0), 0, keepdims=True)


def swap_halves(x):
    inner = (iota(x.shape, x.ndim - 1) & 15) < 8
    axis = x.ndim - 1
    return jnp.where(inner, pltpu.roll(x, CY - 8, axis), pltpu.roll(x, 8, axis))


def own_half(shape, gy):
    lane = iota(shape, len(shape) - 1) & 15
    return jnp.where(gy == 0, lane, lane ^ 8) < 8


def pack_kernel(
    cells_h, m_h, l_h, f_h, mv_h, v_h, we_h, wn_h,
    b_out, a_out, strip_out, z_out, lh_out, g1_out,
    g_s, cells, m, l, f, mv, v, we, wn, sems,
):
    far = (cells_h, m_h, l_h, f_h, mv_h, v_h, we_h, wn_h)
    near = (cells, m, l, f, mv, v, we, wn)
    copies = [pltpu.make_async_copy(a, b, sems.at[i]) for i, (a, b) in enumerate(zip(far, near))]
    for copy in copies:
        copy.start()
    copies[0].wait()
    copies[1].wait()
    core = lax.axis_index("gx") % 2
    gy = lax.axis_index("gy")
    lane = iota((CX, CY), 1)
    for s in range(2):
        rows, lanes = one_hots(cells[s, 0])
        h = scatter(rows, lanes, m[s, 0])
        if s == 0:
            for copy in copies[2:]:
                copy.wait()
        lh_out[s] = l[s] + h.reshape(LEV, CX, CY)
        g_s[s] = f[s] - mv[s] * l[s] - v[s]
    g1_out[...] = g_s[1]
    for z in range(LEV):
        for i in range(CX // 8):
            z_out[z * 8 + i] = l[0, z, 8 * i : 8 * i + 8]
            z_out[64 + z * 8 + i] = g_s[0, z, 8 * i : 8 * i + 8]

    def own(get):
        packed = jnp.zeros((CX, CY), F32)
        for z in range(LEV):
            rolled = pltpu.roll(get(z), (16 * z + 8) % CY, 1)
            packed = jnp.where((lane >> 4) == z, rolled, packed)
        return packed

    half = own_half((CX, CY), gy)
    pairs = (
        ((v, 0), (v, 1)), ((l, 0), (g_s, 0)), ((l, 1), (g_s, 1)),
        ((lh_out, 0), (lh_out, 1)), ((we, 0), (wn, 0)), ((we, 1), (wn, 1)),
    )
    for p, (one, two) in enumerate(pairs):
        first = own(lambda z, one=one: one[0][one[1], z])
        second = own(lambda z, two=two: two[0][two[1], z])
        strip_out[p] = jnp.where(half, first, swap_halves(second))
    for i in range(CX // 8):
        z_out[128 + i] = strip_out[1, 8 * i : 8 * i + 8]

    sub = iota((8, CY), 0)
    for out, top in ((b_out, core == 0), (a_out, core != 0)):
        row = jnp.where(top, 0, CX - 8)
        row = pl.multiple_of(row, 8)
        edge = pl.ds(row, 8)
        for k, field in enumerate((v, l, we, wn)):
            for s in range(2):
                out[pl.ds((2 * k + s) * LEV, LEV)] = field[s, :, edge, :]
        keep = jnp.where(top, sub, 7 - sub) < 4
        for s in range(2):
            for z in range(LEV):
                lh_edge = lh_out[s, z, edge, :]
                g_edge = pltpu.roll(g_s[s, z, edge, :], 4, 0)
                out[(8 + s) * LEV + z] = jnp.where(keep, lh_edge, g_edge)
        out[pl.ds(10 * LEV, 6)] = strip_out[:, edge, :]


def obs_kernel(cells, m, v, dep, ov, rm_out, h2_out):
    for s in range(2):
        rows, lanes = one_hots(cells[s, 0])
        seen = gather(rows, lanes, v[s].reshape(LEV * CX, CY))
        rm = dep[s, 0] - (ov[s, 0] * m[s, 0] + seen)
        rm_out[s, 0] = rm
        h2_out[s] = scatter(rows, lanes, rm).reshape(LEV, CX, CY)


class Place:
    def __init__(self):
        gx = lax.axis_index("gx")
        self.gy = lax.axis_index("gy")
        core = gx % 2
        self.b_row = pl.multiple_of(jnp.where(core == 0, TOP, TOP + HALO + CX), 8)
        self.a_row = pl.multiple_of(jnp.where(core == 0, TOP + HALO + CX, TOP), 8)
        self.core = core
        self.ay_rows = pl.ds(pl.multiple_of(core * 8, 8), 8)
        self.low = jnp.where(gx == 0, 0.0, 1.0)
        self.high = jnp.where(gx == lax.axis_size("gx") - 1, 0.0, 1.0)


def clear(ref, guard_levels):
    lead = ref.shape[:-2]
    zero = jnp.zeros(lead + (TOP, CY), F32)
    ref[..., 0:TOP, :] = zero
    ref[..., BUF - TOP : BUF, :] = zero
    if guard_levels:
        full = jnp.zeros((BUF, CY), F32)
        for i in range(lead[0]):
            ref[i, 0] = full
            ref[i, LEV + 1] = full


def fill(dst, base, place, tile, b_block, a_block):
    for z in range(LEV):
        dst[base + z, TOP + HALO : TOP + HALO + CX] = tile(z)
        dst[base + z, pl.ds(place.b_row, 8)] = b_block(z)
        dst[base + z, pl.ds(place.a_row, 8)] = a_block(z)


def unpack(place, own, received):
    half = own_half(own.shape, place.gy)
    return jnp.where(half, own, received), swap_halves(jnp.where(half, received, own))


def fill_strips(first, second, place, own, got, own_b, got_b, own_a, got_a):
    mid = pl.ds(TOP + HALO, CX)
    for where, a, b in (
        (mid, own, got),
        (pl.ds(place.b_row, 8), own_b, got_b),
        (pl.ds(place.a_row, 8), own_a, got_a),
    ):
        one, two = unpack(place, a, b)
        first[where] = one
        second[where] = two


ROWS = slice(TOP, TOP + EXT)
UP = slice(TOP + 1, TOP + EXT + 1)
DOWN = slice(TOP - 1, TOP + EXT - 1)


def injected(strip, gy):
    lane = iota((EXT, CY), 1) & 15
    moved = jnp.where(gy == 0, pltpu.roll(strip, 119, 1), pltpu.roll(strip, 121, 1))
    return jnp.where(lane == jnp.where(gy == 0, 15, 0), moved, 0.0)


def coefficients(place, wind, strip, coef, scoef, adjoint):
    lane = iota((EXT, CY), 1)
    if not adjoint:
        for z in range(LEV):
            east, north = 0.5 * wind[0, z, ROWS], 0.5 * wind[1, z, ROWS]
            coef[0, z] = DIFFUSION - east
            coef[1, z] = DIFFUSION + east
            coef[2, z] = DIFFUSION - north
            coef[3, z] = DIFFUSION + north
        east, north = 0.5 * strip[0, ROWS], 0.5 * strip[1, ROWS]
        scoef[0] = DIFFUSION - east
        scoef[1] = DIFFUSION + east
        scoef[2] = DIFFUSION - north
        scoef[3] = DIFFUSION + north
        return
    inj = injected(strip[1, ROWS], place.gy)
    for z in range(LEV):
        north = wind[1, z, ROWS]
        edge = pltpu.roll(inj, (CY - 16 * z) % CY, 1)
        after = jnp.where(lane == CY - 1, edge, pltpu.roll(north, CY - 1, 1))
        before = jnp.where(lane == 0, edge, pltpu.roll(north, 1, 1))
        coef[0, z] = DIFFUSION + 0.5 * wind[0, z, UP]
        coef[1, z] = DIFFUSION - 0.5 * wind[0, z, DOWN]
        coef[2, z] = DIFFUSION + 0.5 * after
        coef[3, z] = DIFFUSION - 0.5 * before
    scoef[0] = DIFFUSION + 0.5 * strip[0, UP]
    scoef[1] = DIFFUSION - 0.5 * strip[0, DOWN]
    scoef[2] = DIFFUSION + 0.5 * pltpu.roll(strip[1, ROWS], CY - 1, 1)
    scoef[3] = DIFFUSION - 0.5 * pltpu.roll(strip[1, ROWS], 1, 1)


def store(dst, z, out, place):
    dst[z, TOP : TOP + HALO] = out[:HALO] * place.low
    dst[z, TOP + HALO : TOP + HALO + CX] = out[HALO : HALO + CX]
    dst[z, TOP + HALO + CX : TOP + EXT] = out[HALO + CX :] * place.high


def first_slot(count):
    return count & 1


def one_step(place, src, dst, ssrc, sdst, coef, scoef):
    lane = iota((EXT, CY), 1)
    own = ssrc[ROWS]
    inj = injected(own, place.gy)
    for z in range(LEV):
        mid = src[z + 1, ROWS]
        edge = pltpu.roll(inj, (CY - 16 * z) % CY, 1)
        after = jnp.where(lane == CY - 1, edge, pltpu.roll(mid, CY - 1, 1))
        before = jnp.where(lane == 0, edge, pltpu.roll(mid, 1, 1))
        out = (
            CENTRE * mid
            + coef[0, z] * src[z + 1, UP]
            + coef[1, z] * src[z + 1, DOWN]
            + coef[2, z] * after
            + coef[3, z] * before
            + VERTICAL * (src[z + 2, ROWS] + src[z, ROWS])
        )
        store(dst, z + 1, out, place)
    above = jnp.where(lane < CY - 16, pltpu.roll(own, CY - 16, 1), 0.0)
    below = jnp.where(lane >= 16, pltpu.roll(own, 16, 1), 0.0)
    out = (
        CENTRE * own
        + scoef[0] * ssrc[UP]
        + scoef[1] * ssrc[DOWN]
        + scoef[2] * pltpu.roll(own, CY - 1, 1)
        + scoef[3] * pltpu.roll(own, 1, 1)
        + VERTICAL * (above + below)
    )
    sdst[TOP : TOP + HALO] = out[:HALO] * place.low
    sdst[TOP + HALO : TOP + HALO + CX] = out[HALO : HALO + CX]
    sdst[TOP + HALO + CX : TOP + EXT] = out[HALO + CX :] * place.high


def sweep(place, state, strip, coef, scoef, count):
    def two(i, _):
        for j in range(2):

            @pl.when(2 * i + j >= 4 - count)
            def _():
                one_step(
                    place, state.at[j], state.at[1 - j], strip.at[j, 0], strip.at[1 - j, 0],
                    coef, scoef,
                )

        return 0

    lax.fori_loop(0, 2, two, 0)


STATE = pltpu.VMEM((2, LEV + 2, BUF, CY), F32)
STRIP = pltpu.VMEM((2, 1, BUF, CY), F32)
COEF = pltpu.VMEM((4, LEV, EXT, CY), F32)
SCOEF = pltpu.VMEM((4, EXT, CY), F32)
WIND = pltpu.VMEM((2, LEV, BUF, CY), F32)
WSTRIP = pltpu.VMEM((2, BUF, CY), F32)


def fill_winds(place, s, we, wn, bg, ag, own, got, by, ay, wind, wstrip):
    for k, field in enumerate((we, wn)):
        fill(
            wind.at[k], 0, place, lambda z, field=field: field[s, z],
            lambda z, k=k: bg[(4 + 2 * k + s) * LEV + z],
            lambda z, k=k: ag[(4 + 2 * k + s) * LEV + z],
        )
    p = 4 + s
    fill_strips(
        wstrip.at[0], wstrip.at[1], place, own[p], got[p],
        bg[10 * LEV + p], by[p], ag[10 * LEV + p], ay[p, place.ay_rows],
    )


def first_kernel(
    counts, v, l, we, wn, mv, lh, g1, own, got, bg, ag, by, ay,
    ext_out, rv_out, even_out, odd_out,
    x_f, x_b, s_f, s_b, coef, scoef, wind, wstrip, extra, estrip,
):
    place = Place()
    clear(x_f, True)
    clear(x_b, True)
    for ref in (s_f, s_b, wind, wstrip, extra, estrip):
        clear(ref, False)

    def strips(p, first, second):
        fill_strips(
            first, second, place, own[p], got[p],
            bg[10 * LEV + p], by[p], ag[10 * LEV + p], ay[p, place.ay_rows],
        )

    fill_winds(place, 0, we, wn, bg, ag, own, got, by, ay, wind, wstrip)
    fill(
        x_b.at[first_slot(counts[0])], 1, place, lambda z: l[1, z],
        lambda z: bg[3 * LEV + z], lambda z: ag[3 * LEV + z],
    )
    strips(2, s_b.at[first_slot(counts[0]), 0], estrip.at[1])
    coefficients(place, wind, wstrip, coef, scoef, True)
    sweep(place, x_b, s_b, coef, scoef, counts[0])
    end = 0
    fill(
        extra.at[0], 0, place, lambda z: lh[0, z],
        lambda z: bg[8 * LEV + z], lambda z: ag[8 * LEV + z],
    )
    fill(
        extra.at[1], 0, place, lambda z: g1[z],
        lambda z: pltpu.roll(bg[9 * LEV + z], 4, 0),
        lambda z: pltpu.roll(ag[9 * LEV + z], 4, 0),
    )
    for z in range(LEV):
        rv = x_b[end, z + 1, ROWS] - extra[0, z, ROWS]
        ext_out[0, z] = rv
        rv_out[0, z] = rv[HALO : HALO + CX]
        rv_out[1, z] = mv[0, z]
    strips(3, estrip.at[0], s_f.at[0, 0])
    ext_out[0, LEV] = s_b[end, 0, ROWS] - estrip[0, ROWS]

    for s in range(2):
        if s == 1:
            fill_winds(place, 1, we, wn, bg, ag, own, got, by, ay, wind, wstrip)
        coefficients(place, wind, wstrip, coef, scoef, False)
        fill(
            x_f.at[first_slot(counts[s])], 1, place, lambda z, s=s: v[s, z],
            lambda z, s=s: bg[s * LEV + z], lambda z, s=s: ag[s * LEV + z],
        )
        if s == 0:
            strips(0, s_f.at[first_slot(counts[s]), 0], estrip.at[0])
        else:
            strips(0, estrip.at[0], s_f.at[first_slot(counts[s]), 0])
        sweep(place, x_f, s_f, coef, scoef, counts[s])
        for z in range(LEV):
            out = x_f[end, z + 1, ROWS]
            if s == 0:
                ext_out[1, z] = out + extra[1, z, ROWS]
            else:
                ext_out[2, z] = out
        out = s_f[end, 0, ROWS]
        ext_out[1 + s, LEV] = out + estrip[1, ROWS] if s == 0 else out

    tile = slice(HALO, HALO + CX)
    odd = lax.axis_index("tm") % 2

    @pl.when(odd == 0)
    def _():
        even_out[0] = ext_out[2, :LEV, tile]
        even_out[1] = rv_out[1]
        odd_out[...] = rv_out[...]

    @pl.when(odd == 1)
    def _():
        even_out[...] = rv_out[...]
        odd_out[0] = ext_out[2, :LEV, tile]
        odd_out[1] = rv_out[1]


def lane_sum(x):
    return functools.reduce(
        lambda a, b: a + b, [x[:, i : i + CY] for i in range(0, x.shape[1], CY)]
    )


def second_kernel(
    counts, cells, ext, we, wn, lh, own, got, bg, ag, by, ay, zt, zh,
    mv, h2, rm, ov,
    rv1_out, rl1_out, rl2_out, f21_out, b20_out, ql1_out, qv1_out, qm_out, dots_out,
    x_f, x_b, s_f, s_b, coef, scoef, wind, wstrip, extra, estrip,
):
    place = Place()
    clear(x_f, True)
    clear(x_b, True)
    for ref in (s_f, s_b, wind, wstrip, extra, estrip):
        clear(ref, False)
    tile = slice(HALO, HALO + CX)
    follows = jnp.where(lax.axis_index("tm") == lax.axis_size("tm") - 1, 0.0, 1.0)

    fill_winds(place, 1, we, wn, bg, ag, own, got, by, ay, wind, wstrip)
    coefficients(place, wind, wstrip, coef, scoef, True)

    def z_tile(base):
        return lambda z: zt[base + 8 * z : base + 8 * z + 8].reshape(CX, CY)

    fill(x_b.at[first_slot(counts[1])], 1, place, z_tile(0), lambda z: zh[z], lambda z: zh[16 + z])
    fill(
        extra.at[1], 0, place, z_tile(64),
        lambda z: pltpu.roll(zh[8 + z], 4, 0), lambda z: pltpu.roll(zh[24 + z], 4, 0),
    )
    fill_strips(
        s_b.at[first_slot(counts[1]), 0], estrip.at[1], place,
        zt[128:136].reshape(CX, CY), zh[37:45].reshape(CX, CY),
        zh[32], zh[33], zh[34], zh[35 + place.core],
    )
    sweep(place, x_b, s_b, coef, scoef, counts[1])
    end = 0
    slot = first_slot(counts[1])

    fill(
        extra.at[0], 0, place, lambda z: lh[1, z],
        lambda z: bg[9 * LEV + z], lambda z: ag[9 * LEV + z],
    )
    fill_strips(
        s_f.at[0, 0], estrip.at[0], place, own[3], got[3],
        bg[10 * LEV + 3], by[3], ag[10 * LEV + 3], ay[3, place.ay_rows],
    )
    for z in range(LEV):
        rv = x_b[end, z + 1, ROWS] - extra[0, z, ROWS]
        x_f[slot, z + 1, ROWS] = rv
        rv1_out[z] = rv[tile]
        rl = (extra[1, z, ROWS] + ext[2, z]) * follows
        x_b[slot, z + 1, ROWS] = rl
        rl2_out[z] = rl[tile]
    s_f[slot, 0, ROWS] = s_b[end, 0, ROWS] - estrip[0, ROWS]
    s_b[slot, 0, ROWS] = (estrip[1, ROWS] + ext[2, LEV]) * follows

    sweep(place, x_b, s_b, coef, scoef, counts[1])
    cross = jnp.zeros((8, CY), F32)
    square = jnp.zeros((8, CY), F32)

    def dots(r, q):
        return jnp.sum((r * q).reshape(-1, 8, CY), 0), jnp.sum((q * q).reshape(-1, 8, CY), 0)

    for z in range(LEV):
        rl1 = ext[1, z, tile]
        rl1_out[z] = rl1
        qv = rl1 - x_b[end, z + 1, TOP + HALO : TOP + HALO + CX] + h2[1, z]
        qv1_out[z] = qv
        c, q = dots(rv1_out[z], qv)
        cross, square = cross + c, square + q
    coefficients(place, wind, wstrip, coef, scoef, False)
    sweep(place, x_f, s_f, coef, scoef, counts[1])
    for z in range(LEV):
        f21_out[z] = x_f[end, z + 1, TOP + HALO : TOP + HALO + CX]

    slot = first_slot(counts[0])
    fill_winds(place, 0, we, wn, bg, ag, own, got, by, ay, wind, wstrip)
    coefficients(place, wind, wstrip, coef, scoef, False)
    for z in range(LEV):
        x_f[slot, z + 1, ROWS] = ext[0, z]
        x_b[slot, z + 1, ROWS] = ext[1, z]
    s_f[slot, 0, ROWS] = ext[0, LEV]
    s_b[slot, 0, ROWS] = ext[1, LEV]
    sweep(place, x_f, s_f, coef, scoef, counts[0])
    for z in range(LEV):
        rl1 = ext[1, z, tile]
        ql = mv[1, z] * rl1 + rv1_out[z] - x_f[end, z + 1, TOP + HALO : TOP + HALO + CX]
        ql1_out[z] = ql
        c, q = dots(rl1, ql)
        cross, square = cross + c, square + q
    coefficients(place, wind, wstrip, coef, scoef, True)
    sweep(place, x_b, s_b, coef, scoef, counts[0])
    for z in range(LEV):
        b20_out[z] = x_b[end, z + 1, TOP + HALO : TOP + HALO + CX]

    for s in range(2):
        rows, lanes = one_hots(cells[s, 0])
        if s == 0:
            field = ext[0, 0:LEV, tile].reshape(LEV * CX, CY)
        else:
            field = rv1_out[...].reshape(LEV * CX, CY)
        seen = gather(rows, lanes, field)
        r = rm[s, 0]
        q = ov[s, 0] * r + seen
        qm_out[s, 0] = q
        c, q = lane_sum(r * q), lane_sum(q * q)
        first = iota((8, CY), 0) == 0
        cross = cross + jnp.where(first, c, 0.0)
        square = square + jnp.where(first, q, 0.0)
    dots_out[0] = cross
    dots_out[1] = square


def dots_kernel(
    even, odd, rl2, f21, b20, z_own, h2, rv0, dots_in, rl1, rv1, qv1, ql1, qm, rm, m,
    keep_out, obs_out, send_out,
):
    follows = jnp.where(lax.axis_index("tm") == lax.axis_size("tm") - 1, 0.0, 1.0)
    starts = jnp.where(lax.axis_index("tm") == 0, 1.0, 0.0)
    obs_out[0:2] = rm[...]
    obs_out[2:4] = qm[...]
    obs_out[4:6] = m[...]
    cross, square = dots_in[0], dots_in[1]
    is_odd = lax.axis_index("tm") % 2 == 1

    def total(x):
        return jnp.sum(x.reshape(-1, 8, CY), 0)

    for z in range(LEV):
        rl0 = z_own[64 + 8 * z : 72 + 8 * z].reshape(CX, CY) + jnp.where(is_odd, even[0, z], odd[0, z])
        rv = rv0[0, z]
        qv = rl0 - b20[z] + h2[0, z]
        for i, kept in enumerate((rl0, rl1[z], rv1[z], qv, qv1[z], ql1[z])):
            keep_out[i, z] = kept
        ql = (rv0[1, z] * rl0 + rv) * starts
        rl2z = rl2[z]
        next_mv = jnp.where(is_odd, odd[1, z], even[1, z])
        next_rv = jnp.where(is_odd, odd[0, z], even[0, z])
        q2 = (next_mv * rl2z + next_rv - f21[z]) * follows
        cross += total(rv * qv) + total(rl0 * ql) + total(rl2z * q2)
        square += total(qv * qv) + total(ql * ql) + total(q2 * q2)
    cross = jnp.sum(jnp.sum(cross, 0, keepdims=True), 1, keepdims=True)
    square = jnp.sum(jnp.sum(square, 0, keepdims=True), 1, keepdims=True)
    n = send_out.shape[0]
    lane = iota((n, CY), 1)
    send_out[...] = jnp.where(lane == 0, cross, jnp.where(lane == 1, square, 0.0))


def last_kernel(
    sums, l, v, rv0, z_f2, keep, obs_pair,
    l_out, m_out, v_out, a_out, b_out, c_out,
):
    total = jnp.sum(sums[...], 0, keepdims=True)
    lane = iota((1, CY), 1)
    cross = jnp.sum(jnp.where(lane == 0, total, 0.0), 1, keepdims=True)
    square = jnp.sum(jnp.where(lane == 1, total, 0.0), 1, keepdims=True)
    alpha = cross / (square + 1e-06)
    rm, qm = obs_pair[0:2], obs_pair[2:4]
    m_out[...] = obs_pair[4:6] + alpha * rm
    b_out[...] = rm - alpha * qm
    for z in range(LEV):
        rl0, rl1, rv1, qv0, qv1, ql1 = (keep[i, z] for i in range(6))
        ql0 = rv0[1, z] * rl0 + rv0[0, z] - z_f2[z]
        l_out[0, z] = l[0, z] + alpha * rl0
        l_out[1, z] = l[1, z] + alpha * rl1
        v_out[0, z] = v[0, z] + alpha * rv0[0, z]
        v_out[1, z] = v[1, z] + alpha * rv1
        a_out[0, z] = rl0 - alpha * ql0
        a_out[1, z] = rl1 - alpha * ql1
        c_out[0, z] = rv0[0, z] - alpha * qv0
        c_out[1, z] = rv1 - alpha * qv1


def shards(sizes, l4, m4, v4, f4, d4, mv4, ov4, we4, wn4, cells4, counts):
    ntm, ngx, ngy = sizes
    tile = (LEV, CX, CY)
    obs = m4.shape

    def pair_b(i):
        return i - 1 if i % 2 == 0 else i + 1

    def plane(move_x, move_y):
        pairs = []
        for x in range(ngx):
            for y in range(ngy):
                to = move_x(x)
                if 0 <= to < ngx:
                    pairs.append((x * ngy + y, to * ngy + (1 - y if move_y else y)))
        return pairs

    axes = ("gx", "gy")
    down = [(i + 1, i) for i in range(ntm - 1)]
    up = [(i, i + 1) for i in range(ntm - 1)]
    edge = 10 * LEV

    fields = pltpu.VMEM((2,) + tile, F32)
    b_send, a_send, own, z_send, lh, g1 = call(
        pack_kernel,
        [(NBLOCKS, 8, CY)] * 2 + [(6, CX, CY), (136, 8, CY), (2,) + tile, tile],
        [cells4, m4, l4, f4, mv4, v4, we4, wn4],
        [fields, pltpu.VMEM(obs, jnp.int32), pltpu.VMEM(obs, F32)]
        + [fields] * 6
        + [pltpu.SemaphoreType.DMA((8,))],
        micros=2.5,
        fetched=range(8),
        limit=PACK_LIMIT,
    )
    got = lax.ppermute(own, axes, plane(lambda i: i, True))
    bg = lax.ppermute(b_send, axes, plane(pair_b, False))
    ag = lax.ppermute(a_send, axes, plane(lambda i: i ^ 1, False))
    by = lax.ppermute(b_send[edge:], axes, plane(pair_b, True))
    zt = lax.ppermute(z_send, "tm", down)
    ay_send = jnp.concatenate([got[:, :8], got[:, CX - 8 :]], 1)
    ay_send, late_cells = lax.optimization_barrier((ay_send, cells4))
    ay = lax.ppermute(ay_send, axes, plane(lambda i: i ^ 1, False))
    rm, h2 = call(obs_kernel, [obs, (2,) + tile], [late_cells, m4, v4, d4, ov4], micros=2.4)

    z_edges = jnp.concatenate(
        [
            bg[2 * LEV : 3 * LEV], bg[8 * LEV : 9 * LEV],
            ag[2 * LEV : 3 * LEV], ag[8 * LEV : 9 * LEV],
            bg[edge + 1 : edge + 2], by[1:2], ag[edge + 1 : edge + 2],
            ay[1].reshape(2, 8, CY), got[1].reshape(8, 8, CY),
        ],
        0,
    )
    zh = lax.ppermute(z_edges, "tm", down)
    scratch = [
        STATE, STATE, STRIP, STRIP, COEF, SCOEF, WIND, WSTRIP,
        pltpu.VMEM((2, LEV, BUF, CY), F32), pltpu.VMEM((2, BUF, CY), F32),
    ]
    ext, rv0, even_send, odd_send = call(
        first_kernel,
        [(3, LEV + 1, EXT, CY)] + [(2,) + tile] * 3,
        [counts, v4, l4, we4, wn4, mv4, lh, g1, own, got, bg, ag, by, ay],
        scratch,
        micros=5.0,
    )
    swap = lambda first: [(i, i + 1) for i in range(first, ntm - 1, 2)] + [
        (i + 1, i) for i in range(first, ntm - 1, 2)
    ]
    even = lax.ppermute(even_send, "tm", swap(0))
    odd = lax.ppermute(odd_send, "tm", swap(1))
    rv1, rl1, rl2, f21, b20, ql1, qv1, qm, dots = call(
        second_kernel,
        [tile] * 7 + [obs, (2, 8, CY)],
        [counts, cells4, ext, we4, wn4, lh, own, got, bg, ag, by, ay, zt, zh, mv4, h2, rm, ov4],
        scratch,
        micros=9.0,
    )
    z_f2 = lax.ppermute(f21, "tm", up)
    n = ntm * ngx * ngy
    keep, obs_pair, send = call(
        dots_kernel,
        [(6,) + tile, (6,) + obs[1:], (n, CY)],
        [even, odd, rl2, f21, b20, z_send, h2, rv0, dots, rl1, rv1, qv1, ql1, qm, rm, m4],
        micros=0.4,
    )
    sums = lax.all_to_all(send, ("tm", "gx", "gy"), 0, 0, tiled=True)
    return call(
        last_kernel,
        [l4.shape, obs, l4.shape, l4.shape, obs, l4.shape],
        [sums, l4, v4, rv0, z_f2, keep, obs_pair],
        micros=1.5,
    )


def solution(mesh):
    field = P("tm", None, "gx", "gy")
    obs = P("tm", "gx", "gy", None)
    sizes = tuple(mesh.shape[a] for a in ("tm", "gx", "gy"))
    return jax.shard_map(
        functools.partial(shards, sizes),
        mesh=mesh,
        in_specs=(field, obs, field, field, obs, field, obs, field, field, obs, P("tm")),
        out_specs=(field, obs, field, field, obs, field),
        check_vma=False,
    )
```

```python
import functools

import jax
import jax.numpy as jnp
from jax import lax
from jax.experimental import pallas as pl
from jax.experimental.pallas import tpu as pltpu
from jax.sharding import PartitionSpec as P

DIFFUSION = 0.18
VERTICAL = 0.1
CENTRE = 1.0 - 4.0 * DIFFUSION - 2.0 * VERTICAL

LEV, CX, CY = 8, 64, 128
HALO = 8
EXT = CX + 2 * HALO
TOP = 8
BUF = EXT + 2 * TOP
VMEM_LIMIT = 16 * 1024 * 1024
PACK_LIMIT = 60 * 1024 * 1024
NBLOCKS = 10 * LEV + 6
F32 = jnp.float32

VM = pl.BlockSpec(memory_space=pltpu.VMEM)
SM = pl.BlockSpec(memory_space=pltpu.SMEM)
FAR = pl.BlockSpec(memory_space=pltpu.HBM)


def call(body, outs, ins, scratch=(), micros=1.0, fetched=(), written=(), limit=VMEM_LIMIT):
    shapes = [jax.ShapeDtypeStruct(s, F32) for s in outs]
    nbytes = 4 * sum(int(a.size) for a in ins) + 4 * sum(
        functools.reduce(lambda a, b: a * b, s, 1) for s in outs
    )
    in_specs = [SM if (a.dtype == jnp.int32 and a.size < 64) else VM for a in ins]
    for i in fetched:
        in_specs[i] = FAR
    return pl.pallas_call(
        body,
        out_shape=shapes,
        in_specs=in_specs,
        out_specs=[FAR if i in written else VM for i in range(len(shapes))],
        scratch_shapes=list(scratch),
        compiler_params=pltpu.CompilerParams(vmem_limit_bytes=limit),
        cost_estimate=pl.CostEstimate(
            flops=int(1.1e9 * micros), bytes_accessed=nbytes, transcendentals=0
        ),
    )(*ins)


def iota(shape, dim):
    return lax.broadcasted_iota(jnp.int32, shape, dim)


def split(x):
    high = x.astype(jnp.bfloat16)
    low = (x - high.astype(F32)).astype(jnp.bfloat16)
    return high, low


def one_hots(cells):
    n = cells.shape[1]
    rows = (iota((LEV * CX, n), 0) == (cells >> 7)).astype(jnp.bfloat16)
    lanes = iota((CY, n), 0) == (cells & 127)
    return rows, lanes


def scatter(rows, lanes, values):
    high, low = split(values)
    zero = jnp.zeros((), jnp.bfloat16)
    parts = jnp.concatenate(
        [jnp.where(lanes, high.astype(F32), 0.0), jnp.where(lanes, low.astype(F32), 0.0)], 0
    ).astype(jnp.bfloat16)
    both = lax.dot_general(
        rows, parts, (((1,), (1,)), ((), ())), preferred_element_type=F32
    )
    return both[:, :CY] + both[:, CY:]


def gather(rows, lanes, field):
    high, low = split(field)
    both = lax.dot_general(
        jnp.concatenate([high, low], 1), rows, (((0,), (0,)), ((), ())),
        preferred_element_type=F32,
    )
    picked = both[:CY] + both[CY:]
    return jnp.sum(jnp.where(lanes, picked, 0.0), 0, keepdims=True)


def swap_halves(x):
    inner = (iota(x.shape, x.ndim - 1) & 15) < 8
    axis = x.ndim - 1
    return jnp.where(inner, pltpu.roll(x, CY - 8, axis), pltpu.roll(x, 8, axis))


def own_half(shape, gy):
    lane = iota(shape, len(shape) - 1) & 15
    return jnp.where(gy == 0, lane, lane ^ 8) < 8


def pack_kernel(
    cells_h, m_h, l_h, f_h, mv_h, v_h, we_h, wn_h,
    b_out, a_out, strip_out, z_out, lh_out, g1_out,
    g_s, cells, m, l, f, mv, v, we, wn, sems,
):
    far = (cells_h, m_h, l_h, f_h, mv_h, v_h, we_h, wn_h)
    near = (cells, m, l, f, mv, v, we, wn)
    copies = [pltpu.make_async_copy(a, b, sems.at[i]) for i, (a, b) in enumerate(zip(far, near))]
    for copy in copies:
        copy.start()
    copies[0].wait()
    copies[1].wait()
    core = lax.axis_index("gx") % 2
    gy = lax.axis_index("gy")
    lane = iota((CX, CY), 1)
    for s in range(2):
        rows, lanes = one_hots(cells[s, 0])
        h = scatter(rows, lanes, m[s, 0])
        if s == 0:
            for copy in copies[2:]:
                copy.wait()
        lh_out[s] = l[s] + h.reshape(LEV, CX, CY)
        g_s[s] = f[s] - mv[s] * l[s] - v[s]
    g1_out[...] = g_s[1]
    for z in range(LEV):
        for i in range(CX // 8):
            z_out[z * 8 + i] = l[0, z, 8 * i : 8 * i + 8]
            z_out[64 + z * 8 + i] = g_s[0, z, 8 * i : 8 * i + 8]

    def own(get):
        packed = jnp.zeros((CX, CY), F32)
        for z in range(LEV):
            rolled = pltpu.roll(get(z), (16 * z + 8) % CY, 1)
            packed = jnp.where((lane >> 4) == z, rolled, packed)
        return packed

    half = own_half((CX, CY), gy)
    pairs = (
        ((v, 0), (v, 1)), ((l, 0), (g_s, 0)), ((l, 1), (g_s, 1)),
        ((lh_out, 0), (lh_out, 1)), ((we, 0), (wn, 0)), ((we, 1), (wn, 1)),
    )
    for p, (one, two) in enumerate(pairs):
        first = own(lambda z, one=one: one[0][one[1], z])
        second = own(lambda z, two=two: two[0][two[1], z])
        strip_out[p] = jnp.where(half, first, swap_halves(second))
    for i in range(CX // 8):
        z_out[128 + i] = strip_out[1, 8 * i : 8 * i + 8]

    sub = iota((8, CY), 0)
    for out, top in ((b_out, core == 0), (a_out, core != 0)):
        row = jnp.where(top, 0, CX - 8)
        row = pl.multiple_of(row, 8)
        edge = pl.ds(row, 8)
        for k, field in enumerate((v, l, we, wn)):
            for s in range(2):
                out[pl.ds((2 * k + s) * LEV, LEV)] = field[s, :, edge, :]
        keep = jnp.where(top, sub, 7 - sub) < 4
        for s in range(2):
            for z in range(LEV):
                lh_edge = lh_out[s, z, edge, :]
                g_edge = pltpu.roll(g_s[s, z, edge, :], 4, 0)
                out[(8 + s) * LEV + z] = jnp.where(keep, lh_edge, g_edge)
        out[pl.ds(10 * LEV, 6)] = strip_out[:, edge, :]


def obs_kernel(cells, m, v, dep, ov, rm_out, h2_out):
    for s in range(2):
        rows, lanes = one_hots(cells[s, 0])
        seen = gather(rows, lanes, v[s].reshape(LEV * CX, CY))
        rm = dep[s, 0] - (ov[s, 0] * m[s, 0] + seen)
        rm_out[s, 0] = rm
        h2_out[s] = scatter(rows, lanes, rm).reshape(LEV, CX, CY)


class Place:
    def __init__(self):
        gx = lax.axis_index("gx")
        self.gy = lax.axis_index("gy")
        core = gx % 2
        self.b_row = pl.multiple_of(jnp.where(core == 0, TOP, TOP + HALO + CX), 8)
        self.a_row = pl.multiple_of(jnp.where(core == 0, TOP + HALO + CX, TOP), 8)
        self.core = core
        self.ay_rows = pl.ds(pl.multiple_of(core * 8, 8), 8)
        self.low = jnp.where(gx == 0, 0.0, 1.0)
        self.high = jnp.where(gx == lax.axis_size("gx") - 1, 0.0, 1.0)


def clear(ref, guard_levels):
    lead = ref.shape[:-2]
    zero = jnp.zeros(lead + (TOP, CY), F32)
    ref[..., 0:TOP, :] = zero
    ref[..., BUF - TOP : BUF, :] = zero
    if guard_levels:
        full = jnp.zeros((BUF, CY), F32)
        for i in range(lead[0]):
            ref[i, 0] = full
            ref[i, LEV + 1] = full


def fill(dst, base, place, tile, b_block, a_block):
    for z in range(LEV):
        dst[base + z, TOP + HALO : TOP + HALO + CX] = tile(z)
        dst[base + z, pl.ds(place.b_row, 8)] = b_block(z)
        dst[base + z, pl.ds(place.a_row, 8)] = a_block(z)


def unpack(place, own, received):
    half = own_half(own.shape, place.gy)
    return jnp.where(half, own, received), swap_halves(jnp.where(half, received, own))


def fill_strips(first, second, place, own, got, own_b, got_b, own_a, got_a):
    mid = pl.ds(TOP + HALO, CX)
    for where, a, b in (
        (mid, own, got),
        (pl.ds(place.b_row, 8), own_b, got_b),
        (pl.ds(place.a_row, 8), own_a, got_a),
    ):
        one, two = unpack(place, a, b)
        first[where] = one
        second[where] = two


ROWS = slice(TOP, TOP + EXT)
UP = slice(TOP + 1, TOP + EXT + 1)
DOWN = slice(TOP - 1, TOP + EXT - 1)


def inject(place, state, strip):
    lane = iota((EXT, CY), 1)
    edge = jnp.where(place.gy == 0, lane, CY - 1 - lane) >= CY - 4
    for z in range(LEV):
        moved = pltpu.roll(strip[ROWS], (120 - 16 * z) % CY, 1)
        state[z + 1, ROWS] = jnp.where(edge, moved, state[z + 1, ROWS])


def extract(place, state, strip):
    lane = iota((EXT, CY), 1)
    half = own_half((EXT, CY), place.gy)
    group = jnp.where(half, lane >> 4, LEV)
    packed = strip[ROWS]
    for z in range(LEV):
        packed = jnp.where(
            group == z, pltpu.roll(state[z + 1, ROWS], (16 * z + 8) % CY, 1), packed
        )
    strip[ROWS] = packed


def coefficients(place, wind, strip, coef, scoef, adjoint):
    lane = iota((EXT, CY), 1)
    if not adjoint:
        for z in range(LEV):
            east, north = 0.5 * wind[0, z, ROWS], 0.5 * wind[1, z, ROWS]
            coef[0, z] = DIFFUSION - east
            coef[1, z] = DIFFUSION + east
            coef[2, z] = jnp.where(lane == CY - 1, 0.0, DIFFUSION - north)
            coef[3, z] = jnp.where(lane == 0, 0.0, DIFFUSION + north)
        east, north = 0.5 * strip[0, ROWS], 0.5 * strip[1, ROWS]
        scoef[0] = DIFFUSION - east
        scoef[1] = DIFFUSION + east
        scoef[2] = DIFFUSION - north
        scoef[3] = DIFFUSION + north
        return
    for z in range(LEV):
        north = wind[1, z, ROWS]
        after = pltpu.roll(north, CY - 1, 1)
        before = pltpu.roll(north, 1, 1)
        coef[0, z] = DIFFUSION + 0.5 * wind[0, z, UP]
        coef[1, z] = DIFFUSION - 0.5 * wind[0, z, DOWN]
        coef[2, z] = jnp.where(lane == CY - 1, 0.0, DIFFUSION + 0.5 * after)
        coef[3, z] = jnp.where(lane == 0, 0.0, DIFFUSION - 0.5 * before)
    scoef[0] = DIFFUSION + 0.5 * strip[0, UP]
    scoef[1] = DIFFUSION - 0.5 * strip[0, DOWN]
    scoef[2] = DIFFUSION + 0.5 * pltpu.roll(strip[1, ROWS], CY - 1, 1)
    scoef[3] = DIFFUSION - 0.5 * pltpu.roll(strip[1, ROWS], 1, 1)


def store(dst, z, out, place):
    dst[z, TOP : TOP + HALO] = out[:HALO] * place.low
    dst[z, TOP + HALO : TOP + HALO + CX] = out[HALO : HALO + CX]
    dst[z, TOP + HALO + CX : TOP + EXT] = out[HALO + CX :] * place.high


def first_slot(count):
    return count & 1


def one_step(place, src, dst, ssrc, sdst, coef, scoef):
    lane = iota((EXT, CY), 1)
    own = ssrc[ROWS]
    for z in range(LEV):
        mid = src[z + 1, ROWS]
        after = pltpu.roll(mid, CY - 1, 1)
        before = pltpu.roll(mid, 1, 1)
        out = (
            CENTRE * mid
            + coef[0, z] * src[z + 1, UP]
            + coef[1, z] * src[z + 1, DOWN]
            + coef[2, z] * after
            + coef[3, z] * before
            + VERTICAL * (src[z + 2, ROWS] + src[z, ROWS])
        )
        store(dst, z + 1, out, place)
    above = jnp.where(lane < CY - 16, pltpu.roll(own, CY - 16, 1), 0.0)
    below = jnp.where(lane >= 16, pltpu.roll(own, 16, 1), 0.0)
    out = (
        CENTRE * own
        + scoef[0] * ssrc[UP]
        + scoef[1] * ssrc[DOWN]
        + scoef[2] * pltpu.roll(own, CY - 1, 1)
        + scoef[3] * pltpu.roll(own, 1, 1)
        + VERTICAL * (above + below)
    )
    sdst[TOP : TOP + HALO] = out[:HALO] * place.low
    sdst[TOP + HALO : TOP + HALO + CX] = out[HALO : HALO + CX]
    sdst[TOP + HALO + CX : TOP + EXT] = out[HALO + CX :] * place.high


def sweep(place, state, strip, coef, scoef, count):
    def two(i, _):
        for j in range(2):

            @pl.when(2 * i + j >= 4 - count)
            def _():
                one_step(
                    place, state.at[j], state.at[1 - j], strip.at[j, 0], strip.at[1 - j, 0],
                    coef, scoef,
                )

        return 0

    lax.fori_loop(0, 2, two, 0)
    inject(place, state.at[0], strip.at[0, 0])


STATE = pltpu.VMEM((2, LEV + 2, BUF, CY), F32)
STRIP = pltpu.VMEM((2, 1, BUF, CY), F32)
COEF = pltpu.VMEM((4, LEV, EXT, CY), F32)
SCOEF = pltpu.VMEM((4, EXT, CY), F32)
WIND = pltpu.VMEM((2, LEV, BUF, CY), F32)
WSTRIP = pltpu.VMEM((2, BUF, CY), F32)


def fill_winds(place, s, we, wn, bg, ag, own, got, by, ay, wind, wstrip):
    for k, field in enumerate((we, wn)):
        fill(
            wind.at[k], 0, place, lambda z, field=field: field[s, z],
            lambda z, k=k: bg[(4 + 2 * k + s) * LEV + z],
            lambda z, k=k: ag[(4 + 2 * k + s) * LEV + z],
        )
    p = 4 + s
    fill_strips(
        wstrip.at[0], wstrip.at[1], place, own[p], got[p],
        bg[10 * LEV + p], by[p], ag[10 * LEV + p], ay[p, place.ay_rows],
    )


def first_kernel(
    counts, v, l, we, wn, mv, lh, g1, own, got, bg, ag, by, ay,
    ext_out, rv_out, even_out, odd_out,
    x_f, x_b, s_f, s_b, coef, scoef, wind, wstrip, extra, estrip,
):
    place = Place()
    clear(x_f, True)
    clear(x_b, True)
    for ref in (s_f, s_b, wind, wstrip, extra, estrip):
        clear(ref, False)

    def strips(p, first, second):
        fill_strips(
            first, second, place, own[p], got[p],
            bg[10 * LEV + p], by[p], ag[10 * LEV + p], ay[p, place.ay_rows],
        )

    fill_winds(place, 0, we, wn, bg, ag, own, got, by, ay, wind, wstrip)
    fill(
        x_b.at[first_slot(counts[0])], 1, place, lambda z: l[1, z],
        lambda z: bg[3 * LEV + z], lambda z: ag[3 * LEV + z],
    )
    strips(2, s_b.at[first_slot(counts[0]), 0], estrip.at[1])
    coefficients(place, wind, wstrip, coef, scoef, True)
    sweep(place, x_b, s_b, coef, scoef, counts[0])
    end = 0
    fill(
        extra.at[0], 0, place, lambda z: lh[0, z],
        lambda z: bg[8 * LEV + z], lambda z: ag[8 * LEV + z],
    )
    fill(
        extra.at[1], 0, place, lambda z: g1[z],
        lambda z: pltpu.roll(bg[9 * LEV + z], 4, 0),
        lambda z: pltpu.roll(ag[9 * LEV + z], 4, 0),
    )
    for z in range(LEV):
        rv = x_b[end, z + 1, ROWS] - extra[0, z, ROWS]
        ext_out[0, z] = rv
        rv_out[0, z] = rv[HALO : HALO + CX]
        rv_out[1, z] = mv[0, z]
    strips(3, estrip.at[0], s_f.at[0, 0])
    ext_out[0, LEV] = s_b[end, 0, ROWS] - estrip[0, ROWS]

    for s in range(2):
        if s == 1:
            fill_winds(place, 1, we, wn, bg, ag, own, got, by, ay, wind, wstrip)
        coefficients(place, wind, wstrip, coef, scoef, False)
        fill(
            x_f.at[first_slot(counts[s])], 1, place, lambda z, s=s: v[s, z],
            lambda z, s=s: bg[s * LEV + z], lambda z, s=s: ag[s * LEV + z],
        )
        if s == 0:
            strips(0, s_f.at[first_slot(counts[s]), 0], estrip.at[0])
        else:
            strips(0, estrip.at[0], s_f.at[first_slot(counts[s]), 0])
        sweep(place, x_f, s_f, coef, scoef, counts[s])
        for z in range(LEV):
            out = x_f[end, z + 1, ROWS]
            if s == 0:
                ext_out[1, z] = out + extra[1, z, ROWS]
            else:
                ext_out[2, z] = out
        out = s_f[end, 0, ROWS]
        ext_out[1 + s, LEV] = out + estrip[1, ROWS] if s == 0 else out

    tile = slice(HALO, HALO + CX)
    odd = lax.axis_index("tm") % 2

    @pl.when(odd == 0)
    def _():
        even_out[0] = ext_out[2, :LEV, tile]
        even_out[1] = rv_out[1]
        odd_out[...] = rv_out[...]

    @pl.when(odd == 1)
    def _():
        even_out[...] = rv_out[...]
        odd_out[0] = ext_out[2, :LEV, tile]
        odd_out[1] = rv_out[1]


def lane_sum(x):
    return functools.reduce(
        lambda a, b: a + b, [x[:, i : i + CY] for i in range(0, x.shape[1], CY)]
    )


def second_kernel(
    counts, cells, ext, we, wn, lh, own, got, bg, ag, by, ay, zt, zh,
    mv, h2, rm, ov,
    rv1_out, rl1_out, rl2_out, f21_out, b20_out, ql1_out, qv1_out, qm_out, dots_out,
    x_f, x_b, s_f, s_b, coef, scoef, wind, wstrip, extra, estrip,
):
    place = Place()
    clear(x_f, True)
    clear(x_b, True)
    for ref in (s_f, s_b, wind, wstrip, extra, estrip):
        clear(ref, False)
    tile = slice(HALO, HALO + CX)
    follows = jnp.where(lax.axis_index("tm") == lax.axis_size("tm") - 1, 0.0, 1.0)

    fill_winds(place, 1, we, wn, bg, ag, own, got, by, ay, wind, wstrip)
    coefficients(place, wind, wstrip, coef, scoef, True)

    def z_tile(base):
        return lambda z: zt[base + 8 * z : base + 8 * z + 8].reshape(CX, CY)

    fill(x_b.at[first_slot(counts[1])], 1, place, z_tile(0), lambda z: zh[z], lambda z: zh[16 + z])
    fill(
        extra.at[1], 0, place, z_tile(64),
        lambda z: pltpu.roll(zh[8 + z], 4, 0), lambda z: pltpu.roll(zh[24 + z], 4, 0),
    )
    fill_strips(
        s_b.at[first_slot(counts[1]), 0], estrip.at[1], place,
        zt[128:136].reshape(CX, CY), zh[37:45].reshape(CX, CY),
        zh[32], zh[33], zh[34], zh[35 + place.core],
    )
    sweep(place, x_b, s_b, coef, scoef, counts[1])
    end = 0
    slot = first_slot(counts[1])

    fill(
        extra.at[0], 0, place, lambda z: lh[1, z],
        lambda z: bg[9 * LEV + z], lambda z: ag[9 * LEV + z],
    )
    fill_strips(
        s_f.at[0, 0], estrip.at[0], place, own[3], got[3],
        bg[10 * LEV + 3], by[3], ag[10 * LEV + 3], ay[3, place.ay_rows],
    )
    for z in range(LEV):
        rv = x_b[end, z + 1, ROWS] - extra[0, z, ROWS]
        x_f[slot, z + 1, ROWS] = rv
        rv1_out[z] = rv[tile]
        rl = (extra[1, z, ROWS] + ext[2, z]) * follows
        x_b[slot, z + 1, ROWS] = rl
        rl2_out[z] = rl[tile]
    s_f[slot, 0, ROWS] = s_b[end, 0, ROWS] - estrip[0, ROWS]
    s_b[slot, 0, ROWS] = (estrip[1, ROWS] + ext[2, LEV]) * follows
    extract(place, x_f.at[slot], s_f.at[slot, 0])
    extract(place, x_b.at[slot], s_b.at[slot, 0])

    sweep(place, x_b, s_b, coef, scoef, counts[1])
    cross = jnp.zeros((8, CY), F32)
    square = jnp.zeros((8, CY), F32)

    def dots(r, q):
        return jnp.sum((r * q).reshape(-1, 8, CY), 0), jnp.sum((q * q).reshape(-1, 8, CY), 0)

    for z in range(LEV):
        rl1 = ext[1, z, tile]
        rl1_out[z] = rl1
        qv = rl1 - x_b[end, z + 1, TOP + HALO : TOP + HALO + CX] + h2[1, z]
        qv1_out[z] = qv
        c, q = dots(rv1_out[z], qv)
        cross, square = cross + c, square + q
    coefficients(place, wind, wstrip, coef, scoef, False)
    sweep(place, x_f, s_f, coef, scoef, counts[1])
    for z in range(LEV):
        f21_out[z] = x_f[end, z + 1, TOP + HALO : TOP + HALO + CX]

    slot = first_slot(counts[0])
    fill_winds(place, 0, we, wn, bg, ag, own, got, by, ay, wind, wstrip)
    coefficients(place, wind, wstrip, coef, scoef, False)
    for z in range(LEV):
        x_f[slot, z + 1, ROWS] = ext[0, z]
        x_b[slot, z + 1, ROWS] = ext[1, z]
    s_f[slot, 0, ROWS] = ext[0, LEV]
    s_b[slot, 0, ROWS] = ext[1, LEV]
    extract(place, x_f.at[slot], s_f.at[slot, 0])
    extract(place, x_b.at[slot], s_b.at[slot, 0])
    sweep(place, x_f, s_f, coef, scoef, counts[0])
    for z in range(LEV):
        rl1 = ext[1, z, tile]
        ql = mv[1, z] * rl1 + rv1_out[z] - x_f[end, z + 1, TOP + HALO : TOP + HALO + CX]
        ql1_out[z] = ql
        c, q = dots(rl1, ql)
        cross, square = cross + c, square + q
    coefficients(place, wind, wstrip, coef, scoef, True)
    sweep(place, x_b, s_b, coef, scoef, counts[0])
    for z in range(LEV):
        b20_out[z] = x_b[end, z + 1, TOP + HALO : TOP + HALO + CX]

    for s in range(2):
        rows, lanes = one_hots(cells[s, 0])
        if s == 0:
            field = ext[0, 0:LEV, tile].reshape(LEV * CX, CY)
        else:
            field = rv1_out[...].reshape(LEV * CX, CY)
        seen = gather(rows, lanes, field)
        r = rm[s, 0]
        q = ov[s, 0] * r + seen
        qm_out[s, 0] = q
        c, q = lane_sum(r * q), lane_sum(q * q)
        first = iota((8, CY), 0) == 0
        cross = cross + jnp.where(first, c, 0.0)
        square = square + jnp.where(first, q, 0.0)
    dots_out[0] = cross
    dots_out[1] = square


def dots_kernel(
    even, odd, rl2, f21, b20, z_own, h2, rv0, dots_in, rl1, rv1, qv1, ql1, qm, rm, m,
    keep_out, obs_out, send_out,
):
    follows = jnp.where(lax.axis_index("tm") == lax.axis_size("tm") - 1, 0.0, 1.0)
    starts = jnp.where(lax.axis_index("tm") == 0, 1.0, 0.0)
    obs_out[0:2] = rm[...]
    obs_out[2:4] = qm[...]
    obs_out[4:6] = m[...]
    cross, square = dots_in[0], dots_in[1]
    is_odd = lax.axis_index("tm") % 2 == 1

    def total(x):
        return jnp.sum(x.reshape(-1, 8, CY), 0)

    for z in range(LEV):
        rl0 = z_own[64 + 8 * z : 72 + 8 * z].reshape(CX, CY) + jnp.where(is_odd, even[0, z], odd[0, z])
        rv = rv0[0, z]
        qv = rl0 - b20[z] + h2[0, z]
        for i, kept in enumerate((rl0, rl1[z], rv1[z], qv, qv1[z], ql1[z])):
            keep_out[i, z] = kept
        ql = (rv0[1, z] * rl0 + rv) * starts
        rl2z = rl2[z]
        next_mv = jnp.where(is_odd, odd[1, z], even[1, z])
        next_rv = jnp.where(is_odd, odd[0, z], even[0, z])
        q2 = (next_mv * rl2z + next_rv - f21[z]) * follows
        cross += total(rv * qv) + total(rl0 * ql) + total(rl2z * q2)
        square += total(qv * qv) + total(ql * ql) + total(q2 * q2)
    cross = jnp.sum(jnp.sum(cross, 0, keepdims=True), 1, keepdims=True)
    square = jnp.sum(jnp.sum(square, 0, keepdims=True), 1, keepdims=True)
    n = send_out.shape[0]
    lane = iota((n, CY), 1)
    send_out[...] = jnp.where(lane == 0, cross, jnp.where(lane == 1, square, 0.0))


def last_kernel(
    sums, l, v, rv0, z_f2, keep, obs_pair,
    l_out, m_out, v_out, a_out, b_out, c_out,
):
    total = jnp.sum(sums[...], 0, keepdims=True)
    lane = iota((1, CY), 1)
    cross = jnp.sum(jnp.where(lane == 0, total, 0.0), 1, keepdims=True)
    square = jnp.sum(jnp.where(lane == 1, total, 0.0), 1, keepdims=True)
    alpha = cross / (square + 1e-06)
    rm, qm = obs_pair[0:2], obs_pair[2:4]
    m_out[...] = obs_pair[4:6] + alpha * rm
    b_out[...] = rm - alpha * qm
    for z in range(LEV):
        rl0, rl1, rv1, qv0, qv1, ql1 = (keep[i, z] for i in range(6))
        ql0 = rv0[1, z] * rl0 + rv0[0, z] - z_f2[z]
        l_out[0, z] = l[0, z] + alpha * rl0
        l_out[1, z] = l[1, z] + alpha * rl1
        v_out[0, z] = v[0, z] + alpha * rv0[0, z]
        v_out[1, z] = v[1, z] + alpha * rv1
        a_out[0, z] = rl0 - alpha * ql0
        a_out[1, z] = rl1 - alpha * ql1
        c_out[0, z] = rv0[0, z] - alpha * qv0
        c_out[1, z] = rv1 - alpha * qv1


def shards(sizes, l4, m4, v4, f4, d4, mv4, ov4, we4, wn4, cells4, counts):
    ntm, ngx, ngy = sizes
    tile = (LEV, CX, CY)
    obs = m4.shape

    def pair_b(i):
        return i - 1 if i % 2 == 0 else i + 1

    def plane(move_x, move_y):
        pairs = []
        for x in range(ngx):
            for y in range(ngy):
                to = move_x(x)
                if 0 <= to < ngx:
                    pairs.append((x * ngy + y, to * ngy + (1 - y if move_y else y)))
        return pairs

    axes = ("gx", "gy")
    down = [(i + 1, i) for i in range(ntm - 1)]
    up = [(i, i + 1) for i in range(ntm - 1)]
    edge = 10 * LEV

    fields = pltpu.VMEM((2,) + tile, F32)
    b_send, a_send, own, z_send, lh, g1 = call(
        pack_kernel,
        [(NBLOCKS, 8, CY)] * 2 + [(6, CX, CY), (136, 8, CY), (2,) + tile, tile],
        [cells4, m4, l4, f4, mv4, v4, we4, wn4],
        [fields, pltpu.VMEM(obs, jnp.int32), pltpu.VMEM(obs, F32)]
        + [fields] * 6
        + [pltpu.SemaphoreType.DMA((8,))],
        micros=2.5,
        fetched=range(8),
        limit=PACK_LIMIT,
    )
    got = lax.ppermute(own, axes, plane(lambda i: i, True))
    bg = lax.ppermute(b_send, axes, plane(pair_b, False))
    ag = lax.ppermute(a_send, axes, plane(lambda i: i ^ 1, False))
    by = lax.ppermute(b_send[edge:], axes, plane(pair_b, True))
    zt = lax.ppermute(z_send, "tm", down)
    ay_send = jnp.concatenate([got[:, :8], got[:, CX - 8 :]], 1)
    ay_send, late_cells = lax.optimization_barrier((ay_send, cells4))
    ay = lax.ppermute(ay_send, axes, plane(lambda i: i ^ 1, False))
    rm, h2 = call(obs_kernel, [obs, (2,) + tile], [late_cells, m4, v4, d4, ov4], micros=2.4)

    z_edges = jnp.concatenate(
        [
            bg[2 * LEV : 3 * LEV], bg[8 * LEV : 9 * LEV],
            ag[2 * LEV : 3 * LEV], ag[8 * LEV : 9 * LEV],
            bg[edge + 1 : edge + 2], by[1:2], ag[edge + 1 : edge + 2],
            ay[1].reshape(2, 8, CY), got[1].reshape(8, 8, CY),
        ],
        0,
    )
    zh = lax.ppermute(z_edges, "tm", down)
    scratch = [
        STATE, STATE, STRIP, STRIP, COEF, SCOEF, WIND, WSTRIP,
        pltpu.VMEM((2, LEV, BUF, CY), F32), pltpu.VMEM((2, BUF, CY), F32),
    ]
    ext, rv0, even_send, odd_send = call(
        first_kernel,
        [(3, LEV + 1, EXT, CY)] + [(2,) + tile] * 3,
        [counts, v4, l4, we4, wn4, mv4, lh, g1, own, got, bg, ag, by, ay],
        scratch,
        micros=5.0,
    )
    swap = lambda first: [(i, i + 1) for i in range(first, ntm - 1, 2)] + [
        (i + 1, i) for i in range(first, ntm - 1, 2)
    ]
    even = lax.ppermute(even_send, "tm", swap(0))
    odd = lax.ppermute(odd_send, "tm", swap(1))
    rv1, rl1, rl2, f21, b20, ql1, qv1, qm, dots = call(
        second_kernel,
        [tile] * 7 + [obs, (2, 8, CY)],
        [counts, cells4, ext, we4, wn4, lh, own, got, bg, ag, by, ay, zt, zh, mv4, h2, rm, ov4],
        scratch,
        micros=9.0,
    )
    z_f2 = lax.ppermute(f21, "tm", up)
    n = ntm * ngx * ngy
    keep, obs_pair, send = call(
        dots_kernel,
        [(6,) + tile, (6,) + obs[1:], (n, CY)],
        [even, odd, rl2, f21, b20, z_send, h2, rv0, dots, rl1, rv1, qv1, ql1, qm, rm, m4],
        micros=0.4,
    )
    sums = lax.all_to_all(send, ("tm", "gx", "gy"), 0, 0, tiled=True)
    return call(
        last_kernel,
        [l4.shape, obs, l4.shape, l4.shape, obs, l4.shape],
        [sums, l4, v4, rv0, z_f2, keep, obs_pair],
        micros=1.5,
    )


def solution(mesh):
    field = P("tm", None, "gx", "gy")
    obs = P("tm", "gx", "gy", None)
    sizes = tuple(mesh.shape[a] for a in ("tm", "gx", "gy"))
    return jax.shard_map(
        functools.partial(shards, sizes),
        mesh=mesh,
        in_specs=(field, obs, field, field, obs, field, obs, field, field, obs, P("tm")),
        out_specs=(field, obs, field, field, obs, field),
        check_vma=False,
    )
```

```python
import functools

import jax
import jax.numpy as jnp
from jax import lax
from jax.experimental import pallas as pl
from jax.experimental.pallas import tpu as pltpu
from jax.sharding import PartitionSpec as P

DIFFUSION = 0.18
VERTICAL = 0.1
CENTRE = 1.0 - 4.0 * DIFFUSION - 2.0 * VERTICAL

LEV, CX, CY = 8, 64, 128
HALO = 8
EXT = CX + 2 * HALO
TOP = 8
BUF = EXT + 2 * TOP
VMEM_LIMIT = 16 * 1024 * 1024
PACK_LIMIT = 60 * 1024 * 1024
NBLOCKS = 10 * LEV + 6
F32 = jnp.float32

VM = pl.BlockSpec(memory_space=pltpu.VMEM)
SM = pl.BlockSpec(memory_space=pltpu.SMEM)
FAR = pl.BlockSpec(memory_space=pltpu.HBM)


def call(body, outs, ins, scratch=(), micros=1.0, fetched=(), written=(), limit=VMEM_LIMIT):
    shapes = [jax.ShapeDtypeStruct(s, F32) for s in outs]
    nbytes = 4 * sum(int(a.size) for a in ins) + 4 * sum(
        functools.reduce(lambda a, b: a * b, s, 1) for s in outs
    )
    in_specs = [SM if (a.dtype == jnp.int32 and a.size < 64) else VM for a in ins]
    for i in fetched:
        in_specs[i] = FAR
    return pl.pallas_call(
        body,
        out_shape=shapes,
        in_specs=in_specs,
        out_specs=[FAR if i in written else VM for i in range(len(shapes))],
        scratch_shapes=list(scratch),
        compiler_params=pltpu.CompilerParams(vmem_limit_bytes=limit),
        cost_estimate=pl.CostEstimate(
            flops=int(1.1e9 * micros), bytes_accessed=nbytes, transcendentals=0
        ),
    )(*ins)


def iota(shape, dim):
    return lax.broadcasted_iota(jnp.int32, shape, dim)


def split(x):
    high = x.astype(jnp.bfloat16)
    low = (x - high.astype(F32)).astype(jnp.bfloat16)
    return high, low


def one_hots(cells):
    n = cells.shape[1]
    rows = (iota((LEV * CX, n), 0) == (cells >> 7)).astype(jnp.bfloat16)
    lanes = iota((CY, n), 0) == (cells & 127)
    return rows, lanes


def scatter(rows, lanes, values):
    high, low = split(values)
    zero = jnp.zeros((), jnp.bfloat16)
    parts = jnp.concatenate(
        [jnp.where(lanes, high.astype(F32), 0.0), jnp.where(lanes, low.astype(F32), 0.0)], 0
    ).astype(jnp.bfloat16)
    both = lax.dot_general(
        rows, parts, (((1,), (1,)), ((), ())), preferred_element_type=F32
    )
    return both[:, :CY] + both[:, CY:]


def gather(rows, lanes, field):
    high, low = split(field)
    both = lax.dot_general(
        jnp.concatenate([high, low], 1), rows, (((0,), (0,)), ((), ())),
        preferred_element_type=F32,
    )
    picked = both[:CY] + both[CY:]
    return jnp.sum(jnp.where(lanes, picked, 0.0), 0, keepdims=True)


def swap_halves(x):
    inner = (iota(x.shape, x.ndim - 1) & 15) < 8
    axis = x.ndim - 1
    return jnp.where(inner, pltpu.roll(x, CY - 8, axis), pltpu.roll(x, 8, axis))


def own_half(shape, gy):
    lane = iota(shape, len(shape) - 1) & 15
    return jnp.where(gy == 0, lane, lane ^ 8) < 8


def pack_kernel(
    cells_h, m_h, l_h, f_h, mv_h, v_h, we_h, wn_h,
    b_out, a_out, strip_out, z_out, lh_out, g1_out,
    g_s, cells, m, l, f, mv, v, we, wn, sems,
):
    far = (cells_h, m_h, l_h, f_h, mv_h, v_h, we_h, wn_h)
    near = (cells, m, l, f, mv, v, we, wn)
    copies = [pltpu.make_async_copy(a, b, sems.at[i]) for i, (a, b) in enumerate(zip(far, near))]
    for copy in copies:
        copy.start()
    copies[0].wait()
    copies[1].wait()
    core = lax.axis_index("gx") % 2
    gy = lax.axis_index("gy")
    lane = iota((CX, CY), 1)
    for s in range(2):
        rows, lanes = one_hots(cells[s, 0])
        h = scatter(rows, lanes, m[s, 0])
        if s == 0:
            for copy in copies[2:]:
                copy.wait()
        lh_out[s] = l[s] + h.reshape(LEV, CX, CY)
        g_s[s] = f[s] - mv[s] * l[s] - v[s]
    g1_out[...] = g_s[1]
    for z in range(LEV):
        for i in range(CX // 8):
            z_out[z * 8 + i] = l[0, z, 8 * i : 8 * i + 8]
            z_out[64 + z * 8 + i] = g_s[0, z, 8 * i : 8 * i + 8]

    def own(get):
        packed = jnp.zeros((CX, CY), F32)
        for z in range(LEV):
            rolled = pltpu.roll(get(z), (16 * z + 8) % CY, 1)
            packed = jnp.where((lane >> 4) == z, rolled, packed)
        return packed

    half = own_half((CX, CY), gy)
    pairs = (
        ((v, 0), (v, 1)), ((l, 0), (g_s, 0)), ((l, 1), (g_s, 1)),
        ((lh_out, 0), (lh_out, 1)), ((we, 0), (wn, 0)), ((we, 1), (wn, 1)),
    )
    for p, (one, two) in enumerate(pairs):
        first = own(lambda z, one=one: one[0][one[1], z])
        second = own(lambda z, two=two: two[0][two[1], z])
        strip_out[p] = jnp.where(half, first, swap_halves(second))
    for i in range(CX // 8):
        z_out[128 + i] = strip_out[1, 8 * i : 8 * i + 8]

    sub = iota((8, CY), 0)
    for out, top in ((b_out, core == 0), (a_out, core != 0)):
        row = jnp.where(top, 0, CX - 8)
        row = pl.multiple_of(row, 8)
        edge = pl.ds(row, 8)
        for k, field in enumerate((v, l, we, wn)):
            for s in range(2):
                out[pl.ds((2 * k + s) * LEV, LEV)] = field[s, :, edge, :]
        keep = jnp.where(top, sub, 7 - sub) < 4
        for s in range(2):
            for z in range(LEV):
                lh_edge = lh_out[s, z, edge, :]
                g_edge = pltpu.roll(g_s[s, z, edge, :], 4, 0)
                out[(8 + s) * LEV + z] = jnp.where(keep, lh_edge, g_edge)
        out[pl.ds(10 * LEV, 6)] = strip_out[:, edge, :]


def obs_kernel(cells, m, v, dep, ov, rm_out, h2_out):
    for s in range(2):
        rows, lanes = one_hots(cells[s, 0])
        seen = gather(rows, lanes, v[s].reshape(LEV * CX, CY))
        rm = dep[s, 0] - (ov[s, 0] * m[s, 0] + seen)
        rm_out[s, 0] = rm
        h2_out[s] = scatter(rows, lanes, rm).reshape(LEV, CX, CY)


class Place:
    def __init__(self):
        gx = lax.axis_index("gx")
        self.gy = lax.axis_index("gy")
        core = gx % 2
        self.b_row = pl.multiple_of(jnp.where(core == 0, TOP, TOP + HALO + CX), 8)
        self.a_row = pl.multiple_of(jnp.where(core == 0, TOP + HALO + CX, TOP), 8)
        self.core = core
        self.ay_rows = pl.ds(pl.multiple_of(core * 8, 8), 8)
        self.low = jnp.where(gx == 0, 0.0, 1.0)
        self.high = jnp.where(gx == lax.axis_size("gx") - 1, 0.0, 1.0)


def clear(ref, guard_levels):
    lead = ref.shape[:-2]
    zero = jnp.zeros(lead + (TOP, CY), F32)
    ref[..., 0:TOP, :] = zero
    ref[..., BUF - TOP : BUF, :] = zero
    if guard_levels:
        full = jnp.zeros((BUF, CY), F32)
        for i in range(lead[0]):
            ref[i, 0] = full
            ref[i, LEV + 1] = full


def fill(dst, base, place, tile, b_block, a_block):
    for z in range(LEV):
        dst[base + z, TOP + HALO : TOP + HALO + CX] = tile(z)
        dst[base + z, pl.ds(place.b_row, 8)] = b_block(z)
        dst[base + z, pl.ds(place.a_row, 8)] = a_block(z)


def unpack(place, own, received):
    half = own_half(own.shape, place.gy)
    return jnp.where(half, own, received), swap_halves(jnp.where(half, received, own))


def fill_strips(first, second, place, own, got, own_b, got_b, own_a, got_a):
    mid = pl.ds(TOP + HALO, CX)
    for where, a, b in (
        (mid, own, got),
        (pl.ds(place.b_row, 8), own_b, got_b),
        (pl.ds(place.a_row, 8), own_a, got_a),
    ):
        one, two = unpack(place, a, b)
        first[where] = one
        second[where] = two


ROWS = slice(TOP, TOP + EXT)
UP = slice(TOP + 1, TOP + EXT + 1)
DOWN = slice(TOP - 1, TOP + EXT - 1)


def inject(place, state, strip):
    lane = iota((EXT, CY), 1)
    edge = jnp.where(place.gy == 0, lane, CY - 1 - lane) >= CY - 4
    for z in range(LEV):
        moved = pltpu.roll(strip[ROWS], (120 - 16 * z) % CY, 1)
        state[z + 1, ROWS] = jnp.where(edge, moved, state[z + 1, ROWS])


def extract(place, state, strip):
    lane = iota((EXT, CY), 1)
    half = own_half((EXT, CY), place.gy)
    group = jnp.where(half, lane >> 4, LEV)
    packed = strip[ROWS]
    for z in range(LEV):
        packed = jnp.where(
            group == z, pltpu.roll(state[z + 1, ROWS], (16 * z + 8) % CY, 1), packed
        )
    strip[ROWS] = packed


def coefficients(place, wind, strip, coef, scoef, adjoint):
    lane = iota((EXT, CY), 1)
    if not adjoint:
        for z in range(LEV):
            east, north = 0.5 * wind[0, z, ROWS], 0.5 * wind[1, z, ROWS]
            coef[0, z] = DIFFUSION - east
            coef[1, z] = DIFFUSION + east
            coef[2, z] = jnp.where(lane == CY - 1, 0.0, DIFFUSION - north)
            coef[3, z] = jnp.where(lane == 0, 0.0, DIFFUSION + north)
        east, north = 0.5 * strip[0, ROWS], 0.5 * strip[1, ROWS]
        scoef[0] = DIFFUSION - east
        scoef[1] = DIFFUSION + east
        scoef[2] = DIFFUSION - north
        scoef[3] = DIFFUSION + north
        return
    for z in range(LEV):
        north = wind[1, z, ROWS]
        after = pltpu.roll(north, CY - 1, 1)
        before = pltpu.roll(north, 1, 1)
        coef[0, z] = DIFFUSION + 0.5 * wind[0, z, UP]
        coef[1, z] = DIFFUSION - 0.5 * wind[0, z, DOWN]
        coef[2, z] = jnp.where(lane == CY - 1, 0.0, DIFFUSION + 0.5 * after)
        coef[3, z] = jnp.where(lane == 0, 0.0, DIFFUSION - 0.5 * before)
    scoef[0] = DIFFUSION + 0.5 * strip[0, UP]
    scoef[1] = DIFFUSION - 0.5 * strip[0, DOWN]
    scoef[2] = DIFFUSION + 0.5 * pltpu.roll(strip[1, ROWS], CY - 1, 1)
    scoef[3] = DIFFUSION - 0.5 * pltpu.roll(strip[1, ROWS], 1, 1)


def store(dst, z, out, place):
    dst[z, TOP : TOP + HALO] = out[:HALO] * place.low
    dst[z, TOP + HALO : TOP + HALO + CX] = out[HALO : HALO + CX]
    dst[z, TOP + HALO + CX : TOP + EXT] = out[HALO + CX :] * place.high


def first_slot(count):
    return count & 1


def one_step(place, src, dst, ssrc, sdst, coef, scoef):
    lane = iota((EXT, CY), 1)
    own = ssrc[ROWS]
    for z in range(LEV):
        mid = src[z + 1, ROWS]
        after = pltpu.roll(mid, CY - 1, 1)
        before = pltpu.roll(mid, 1, 1)
        out = (
            CENTRE * mid
            + coef[0, z] * src[z + 1, UP]
            + coef[1, z] * src[z + 1, DOWN]
            + coef[2, z] * after
            + coef[3, z] * before
            + VERTICAL * (src[z + 2, ROWS] + src[z, ROWS])
        )
        store(dst, z + 1, out, place)
    above = jnp.where(lane < CY - 16, pltpu.roll(own, CY - 16, 1), 0.0)
    below = jnp.where(lane >= 16, pltpu.roll(own, 16, 1), 0.0)
    out = (
        CENTRE * own
        + scoef[0] * ssrc[UP]
        + scoef[1] * ssrc[DOWN]
        + scoef[2] * pltpu.roll(own, CY - 1, 1)
        + scoef[3] * pltpu.roll(own, 1, 1)
        + VERTICAL * (above + below)
    )
    sdst[TOP : TOP + HALO] = out[:HALO] * place.low
    sdst[TOP + HALO : TOP + HALO + CX] = out[HALO : HALO + CX]
    sdst[TOP + HALO + CX : TOP + EXT] = out[HALO + CX :] * place.high


def sweep(place, state, strip, coef, scoef, count):
    def two(i, _):
        for j in range(2):

            @pl.when(2 * i + j >= 4 - count)
            def _():
                one_step(
                    place, state.at[j], state.at[1 - j], strip.at[j, 0], strip.at[1 - j, 0],
                    coef, scoef,
                )

        return 0

    lax.fori_loop(0, 2, two, 0)
    inject(place, state.at[0], strip.at[0, 0])


STATE = pltpu.VMEM((2, LEV + 2, BUF, CY), F32)
STRIP = pltpu.VMEM((2, 1, BUF, CY), F32)
COEF = pltpu.VMEM((4, LEV, EXT, CY), F32)
SCOEF = pltpu.VMEM((4, EXT, CY), F32)
WIND = pltpu.VMEM((2, LEV, BUF, CY), F32)
WSTRIP = pltpu.VMEM((2, BUF, CY), F32)


def fill_winds(place, s, we, wn, bg, ag, own, got, by, ay, wind, wstrip):
    for k, field in enumerate((we, wn)):
        fill(
            wind.at[k], 0, place, lambda z, field=field: field[s, z],
            lambda z, k=k: bg[(4 + 2 * k + s) * LEV + z],
            lambda z, k=k: ag[(4 + 2 * k + s) * LEV + z],
        )
    p = 4 + s
    fill_strips(
        wstrip.at[0], wstrip.at[1], place, own[p], got[p],
        bg[10 * LEV + p], by[p], ag[10 * LEV + p], ay[p, place.ay_rows],
    )


def first_kernel(
    counts, v, l, we, wn, mv, lh, g1, own, got, bg, ag, by, ay,
    ext_out, rv_out, even_out, odd_out,
    x_f, x_b, s_f, s_b, coef, scoef, wind, wstrip, extra, estrip,
):
    place = Place()
    clear(x_f, True)
    clear(x_b, True)
    for ref in (s_f, s_b, wind, wstrip, extra, estrip):
        clear(ref, False)

    def strips(p, first, second):
        fill_strips(
            first, second, place, own[p], got[p],
            bg[10 * LEV + p], by[p], ag[10 * LEV + p], ay[p, place.ay_rows],
        )

    fill_winds(place, 0, we, wn, bg, ag, own, got, by, ay, wind, wstrip)
    fill(
        x_b.at[first_slot(counts[0])], 1, place, lambda z: l[1, z],
        lambda z: bg[3 * LEV + z], lambda z: ag[3 * LEV + z],
    )
    strips(2, s_b.at[first_slot(counts[0]), 0], estrip.at[1])
    coefficients(place, wind, wstrip, coef, scoef, True)
    sweep(place, x_b, s_b, coef, scoef, counts[0])
    end = 0
    fill(
        extra.at[0], 0, place, lambda z: lh[0, z],
        lambda z: bg[8 * LEV + z], lambda z: ag[8 * LEV + z],
    )
    fill(
        extra.at[1], 0, place, lambda z: g1[z],
        lambda z: pltpu.roll(bg[9 * LEV + z], 4, 0),
        lambda z: pltpu.roll(ag[9 * LEV + z], 4, 0),
    )
    for z in range(LEV):
        rv = x_b[end, z + 1, ROWS] - extra[0, z, ROWS]
        ext_out[0, z] = rv
        rv_out[0, z] = rv[HALO : HALO + CX]
        rv_out[1, z] = mv[0, z]
    strips(3, estrip.at[0], s_f.at[0, 0])
    ext_out[0, LEV] = s_b[end, 0, ROWS] - estrip[0, ROWS]

    for s in range(2):
        if s == 1:
            fill_winds(place, 1, we, wn, bg, ag, own, got, by, ay, wind, wstrip)
        coefficients(place, wind, wstrip, coef, scoef, False)
        fill(
            x_f.at[first_slot(counts[s])], 1, place, lambda z, s=s: v[s, z],
            lambda z, s=s: bg[s * LEV + z], lambda z, s=s: ag[s * LEV + z],
        )
        if s == 0:
            strips(0, s_f.at[first_slot(counts[s]), 0], estrip.at[0])
        else:
            strips(0, estrip.at[0], s_f.at[first_slot(counts[s]), 0])
        sweep(place, x_f, s_f, coef, scoef, counts[s])
        for z in range(LEV):
            out = x_f[end, z + 1, ROWS]
            if s == 0:
                ext_out[1, z] = out + extra[1, z, ROWS]
            else:
                ext_out[2, z] = out
        out = s_f[end, 0, ROWS]
        ext_out[1 + s, LEV] = out + estrip[1, ROWS] if s == 0 else out

    tile = slice(HALO, HALO + CX)
    odd = lax.axis_index("tm") % 2

    @pl.when(odd == 0)
    def _():
        even_out[0] = ext_out[2, :LEV, tile]
        even_out[1] = rv_out[1]
        odd_out[...] = rv_out[...]

    @pl.when(odd == 1)
    def _():
        even_out[...] = rv_out[...]
        odd_out[0] = ext_out[2, :LEV, tile]
        odd_out[1] = rv_out[1]


def lane_sum(x):
    return functools.reduce(
        lambda a, b: a + b, [x[:, i : i + CY] for i in range(0, x.shape[1], CY)]
    )


def second_kernel(
    counts, cells, ext, we, wn, lh, own, got, bg, ag, by, ay, zt, zh,
    mv, h2, rm, ov,
    rv1_out, rl1_out, rl2_out, f21_out, b20_out, ql1_out, qv1_out, qm_out, dots_out,
    x_f, x_b, s_f, s_b, coef, scoef, wind, wstrip, extra, estrip,
):
    place = Place()
    clear(x_f, True)
    clear(x_b, True)
    for ref in (s_f, s_b, wind, wstrip, extra, estrip):
        clear(ref, False)
    tile = slice(HALO, HALO + CX)
    follows = jnp.where(lax.axis_index("tm") == lax.axis_size("tm") - 1, 0.0, 1.0)

    fill_winds(place, 1, we, wn, bg, ag, own, got, by, ay, wind, wstrip)
    coefficients(place, wind, wstrip, coef, scoef, True)

    def z_tile(base):
        return lambda z: zt[base + 8 * z : base + 8 * z + 8].reshape(CX, CY)

    fill(x_b.at[first_slot(counts[1])], 1, place, z_tile(0), lambda z: zh[z], lambda z: zh[16 + z])
    fill(
        extra.at[1], 0, place, z_tile(64),
        lambda z: pltpu.roll(zh[8 + z], 4, 0), lambda z: pltpu.roll(zh[24 + z], 4, 0),
    )
    fill_strips(
        s_b.at[first_slot(counts[1]), 0], estrip.at[1], place,
        zt[128:136].reshape(CX, CY), zh[37:45].reshape(CX, CY),
        zh[32], zh[33], zh[34], zh[35 + place.core],
    )
    sweep(place, x_b, s_b, coef, scoef, counts[1])
    end = 0
    slot = first_slot(counts[1])

    fill(
        extra.at[0], 0, place, lambda z: lh[1, z],
        lambda z: bg[9 * LEV + z], lambda z: ag[9 * LEV + z],
    )
    fill_strips(
        s_f.at[0, 0], estrip.at[0], place, own[3], got[3],
        bg[10 * LEV + 3], by[3], ag[10 * LEV + 3], ay[3, place.ay_rows],
    )
    for z in range(LEV):
        rv = x_b[end, z + 1, ROWS] - extra[0, z, ROWS]
        x_f[slot, z + 1, ROWS] = rv
        rv1_out[z] = rv[tile]
        rl = (extra[1, z, ROWS] + ext[2, z]) * follows
        x_b[slot, z + 1, ROWS] = rl
        rl2_out[z] = rl[tile]
    s_f[slot, 0, ROWS] = s_b[end, 0, ROWS] - estrip[0, ROWS]
    s_b[slot, 0, ROWS] = (estrip[1, ROWS] + ext[2, LEV]) * follows
    extract(place, x_f.at[slot], s_f.at[slot, 0])
    extract(place, x_b.at[slot], s_b.at[slot, 0])

    sweep(place, x_b, s_b, coef, scoef, counts[1])
    cross = jnp.zeros((8, CY), F32)
    square = jnp.zeros((8, CY), F32)

    def dots(r, q):
        return jnp.sum((r * q).reshape(-1, 8, CY), 0), jnp.sum((q * q).reshape(-1, 8, CY), 0)

    for z in range(LEV):
        rl1 = ext[1, z, tile]
        rl1_out[z] = rl1
        qv = rl1 - x_b[end, z + 1, TOP + HALO : TOP + HALO + CX] + h2[1, z]
        qv1_out[z] = qv
        c, q = dots(rv1_out[z], qv)
        cross, square = cross + c, square + q
    coefficients(place, wind, wstrip, coef, scoef, False)
    sweep(place, x_f, s_f, coef, scoef, counts[1])
    for z in range(LEV):
        f21_out[z] = x_f[end, z + 1, TOP + HALO : TOP + HALO + CX]

    slot = first_slot(counts[0])
    fill_winds(place, 0, we, wn, bg, ag, own, got, by, ay, wind, wstrip)
    coefficients(place, wind, wstrip, coef, scoef, False)
    for z in range(LEV):
        x_f[slot, z + 1, ROWS] = ext[0, z]
        x_b[slot, z + 1, ROWS] = ext[1, z]
    s_f[slot, 0, ROWS] = ext[0, LEV]
    s_b[slot, 0, ROWS] = ext[1, LEV]
    extract(place, x_f.at[slot], s_f.at[slot, 0])
    extract(place, x_b.at[slot], s_b.at[slot, 0])
    sweep(place, x_f, s_f, coef, scoef, counts[0])
    for z in range(LEV):
        rl1 = ext[1, z, tile]
        ql = mv[1, z] * rl1 + rv1_out[z] - x_f[end, z + 1, TOP + HALO : TOP + HALO + CX]
        ql1_out[z] = ql
        c, q = dots(rl1, ql)
        cross, square = cross + c, square + q
    coefficients(place, wind, wstrip, coef, scoef, True)
    sweep(place, x_b, s_b, coef, scoef, counts[0])
    for z in range(LEV):
        b20_out[z] = x_b[end, z + 1, TOP + HALO : TOP + HALO + CX]

    for s in range(2):
        rows, lanes = one_hots(cells[s, 0])
        if s == 0:
            field = ext[0, 0:LEV, tile].reshape(LEV * CX, CY)
        else:
            field = rv1_out[...].reshape(LEV * CX, CY)
        seen = gather(rows, lanes, field)
        r = rm[s, 0]
        q = ov[s, 0] * r + seen
        qm_out[s, 0] = q
        c, q = lane_sum(r * q), lane_sum(q * q)
        first = iota((8, CY), 0) == 0
        cross = cross + jnp.where(first, c, 0.0)
        square = square + jnp.where(first, q, 0.0)
    dots_out[0] = cross
    dots_out[1] = square


def dots_kernel(
    even, odd, rl2, f21, b20, z_own, h2, rv0, dots_in, rl1, rv1, qv1, ql1, qm, rm, m,
    keep_out, send_out,
):
    follows = jnp.where(lax.axis_index("tm") == lax.axis_size("tm") - 1, 0.0, 1.0)
    starts = jnp.where(lax.axis_index("tm") == 0, 1.0, 0.0)
    for i, kept in enumerate((rm, qm, m)):
        for s in range(2):
            for k in range(m.shape[-1] // CY):
                keep_out[6, 2 * i + s, k : k + 1] = kept[s, 0, :, k * CY : (k + 1) * CY]
    cross, square = dots_in[0], dots_in[1]
    is_odd = lax.axis_index("tm") % 2 == 1

    def total(x):
        return jnp.sum(x.reshape(-1, 8, CY), 0)

    for z in range(LEV):
        rl0 = z_own[64 + 8 * z : 72 + 8 * z].reshape(CX, CY) + jnp.where(is_odd, even[0, z], odd[0, z])
        rv = rv0[0, z]
        qv = rl0 - b20[z] + h2[0, z]
        for i, kept in enumerate((rl0, rl1[z], rv1[z], qv, qv1[z], ql1[z])):
            keep_out[i, z] = kept
        ql = (rv0[1, z] * rl0 + rv) * starts
        rl2z = rl2[z]
        next_mv = jnp.where(is_odd, odd[1, z], even[1, z])
        next_rv = jnp.where(is_odd, odd[0, z], even[0, z])
        q2 = (next_mv * rl2z + next_rv - f21[z]) * follows
        cross += total(rv * qv) + total(rl0 * ql) + total(rl2z * q2)
        square += total(qv * qv) + total(ql * ql) + total(q2 * q2)
    cross = jnp.sum(jnp.sum(cross, 0, keepdims=True), 1, keepdims=True)
    square = jnp.sum(jnp.sum(square, 0, keepdims=True), 1, keepdims=True)
    n = send_out.shape[0]
    lane = iota((n, CY), 1)
    send_out[...] = jnp.where(lane == 0, cross, jnp.where(lane == 1, square, 0.0))


def last_kernel(
    sums, l, v, rv0, z_f2, keep,
    l_out, m_out, v_out, a_out, b_out, c_out,
):
    total = jnp.sum(sums[...], 0, keepdims=True)
    lane = iota((1, CY), 1)
    cross = jnp.sum(jnp.where(lane == 0, total, 0.0), 1, keepdims=True)
    square = jnp.sum(jnp.where(lane == 1, total, 0.0), 1, keepdims=True)
    alpha = cross / (square + 1e-06)
    for s in range(2):
        for k in range(m_out.shape[-1] // CY):
            rm, qm, m = (keep[6, 2 * i + s, k : k + 1] for i in range(3))
            m_out[s, 0, :, k * CY : (k + 1) * CY] = m + alpha * rm
            b_out[s, 0, :, k * CY : (k + 1) * CY] = rm - alpha * qm
    for z in range(LEV):
        rl0, rl1, rv1, qv0, qv1, ql1 = (keep[i, z] for i in range(6))
        ql0 = rv0[1, z] * rl0 + rv0[0, z] - z_f2[z]
        l_out[0, z] = l[0, z] + alpha * rl0
        l_out[1, z] = l[1, z] + alpha * rl1
        v_out[0, z] = v[0, z] + alpha * rv0[0, z]
        v_out[1, z] = v[1, z] + alpha * rv1
        a_out[0, z] = rl0 - alpha * ql0
        a_out[1, z] = rl1 - alpha * ql1
        c_out[0, z] = rv0[0, z] - alpha * qv0
        c_out[1, z] = rv1 - alpha * qv1


def shards(sizes, l4, m4, v4, f4, d4, mv4, ov4, we4, wn4, cells4, counts):
    ntm, ngx, ngy = sizes
    tile = (LEV, CX, CY)
    obs = m4.shape

    def pair_b(i):
        return i - 1 if i % 2 == 0 else i + 1

    def plane(move_x, move_y):
        pairs = []
        for x in range(ngx):
            for y in range(ngy):
                to = move_x(x)
                if 0 <= to < ngx:
                    pairs.append((x * ngy + y, to * ngy + (1 - y if move_y else y)))
        return pairs

    axes = ("gx", "gy")
    down = [(i + 1, i) for i in range(ntm - 1)]
    up = [(i, i + 1) for i in range(ntm - 1)]
    edge = 10 * LEV

    fields = pltpu.VMEM((2,) + tile, F32)
    b_send, a_send, own, z_send, lh, g1 = call(
        pack_kernel,
        [(NBLOCKS, 8, CY)] * 2 + [(6, CX, CY), (136, 8, CY), (2,) + tile, tile],
        [cells4, m4, l4, f4, mv4, v4, we4, wn4],
        [fields, pltpu.VMEM(obs, jnp.int32), pltpu.VMEM(obs, F32)]
        + [fields] * 6
        + [pltpu.SemaphoreType.DMA((8,))],
        micros=2.5,
        fetched=range(8),
        limit=PACK_LIMIT,
    )
    got = lax.ppermute(own, axes, plane(lambda i: i, True))
    bg = lax.ppermute(b_send, axes, plane(pair_b, False))
    ag = lax.ppermute(a_send, axes, plane(lambda i: i ^ 1, False))
    zt = lax.ppermute(z_send, "tm", down)
    ay_send = jnp.concatenate([got[:, :8], got[:, CX - 8 :]], 1)
    ay_send, late_cells, by_send = lax.optimization_barrier((ay_send, cells4, b_send[edge:]))
    by = lax.ppermute(by_send, axes, plane(pair_b, True))
    ay = lax.ppermute(ay_send, axes, plane(lambda i: i ^ 1, False))
    rm, h2 = call(obs_kernel, [obs, (2,) + tile], [late_cells, m4, v4, d4, ov4], micros=2.4)

    z_edges = jnp.concatenate(
        [
            bg[2 * LEV : 3 * LEV], bg[8 * LEV : 9 * LEV],
            ag[2 * LEV : 3 * LEV], ag[8 * LEV : 9 * LEV],
            bg[edge + 1 : edge + 2], by[1:2], ag[edge + 1 : edge + 2],
            ay[1].reshape(2, 8, CY), got[1].reshape(8, 8, CY),
        ],
        0,
    )
    zh = lax.ppermute(z_edges, "tm", down)
    scratch = [
        STATE, STATE, STRIP, STRIP, COEF, SCOEF, WIND, WSTRIP,
        pltpu.VMEM((2, LEV, BUF, CY), F32), pltpu.VMEM((2, BUF, CY), F32),
    ]
    ext, rv0, even_send, odd_send = call(
        first_kernel,
        [(3, LEV + 1, EXT, CY)] + [(2,) + tile] * 3,
        [counts, v4, l4, we4, wn4, mv4, lh, g1, own, got, bg, ag, by, ay],
        scratch,
        micros=5.0,
    )
    swap = lambda first: [(i, i + 1) for i in range(first, ntm - 1, 2)] + [
        (i + 1, i) for i in range(first, ntm - 1, 2)
    ]
    even = lax.ppermute(even_send, "tm", swap(0))
    odd = lax.ppermute(odd_send, "tm", swap(1))
    rv1, rl1, rl2, f21, b20, ql1, qv1, qm, dots = call(
        second_kernel,
        [tile] * 7 + [obs, (2, 8, CY)],
        [counts, cells4, ext, we4, wn4, lh, own, got, bg, ag, by, ay, zt, zh, mv4, h2, rm, ov4],
        scratch,
        micros=9.0,
    )
    n = ntm * ngx * ngy
    keep, send = call(
        dots_kernel,
        [(7,) + tile, (n, CY)],
        [even, odd, rl2, f21, b20, z_send, h2, rv0, dots, rl1, rv1, qv1, ql1, qm, rm, m4],
        micros=0.4,
    )
    send, late_f21 = lax.optimization_barrier((send, f21))
    sums = lax.all_to_all(send, ("tm", "gx", "gy"), 0, 0, tiled=True)
    z_f2 = lax.ppermute(late_f21, "tm", up)
    return call(
        last_kernel,
        [l4.shape, obs, l4.shape, l4.shape, obs, l4.shape],
        [sums, l4, v4, rv0, z_f2, keep],
        micros=1.5,
    )


def solution(mesh):
    field = P("tm", None, "gx", "gy")
    obs = P("tm", "gx", "gy", None)
    sizes = tuple(mesh.shape[a] for a in ("tm", "gx", "gy"))
    return jax.shard_map(
        functools.partial(shards, sizes),
        mesh=mesh,
        in_specs=(field, obs, field, field, obs, field, obs, field, field, obs, P("tm")),
        out_specs=(field, obs, field, field, obs, field),
        check_vma=False,
    )
```

```python
import functools

import jax
import jax.numpy as jnp
from jax import lax
from jax.experimental import pallas as pl
from jax.experimental.pallas import tpu as pltpu
from jax.sharding import PartitionSpec as P

DIFFUSION = 0.18
VERTICAL = 0.1
CENTRE = 1.0 - 4.0 * DIFFUSION - 2.0 * VERTICAL

LEV, CX, CY = 8, 64, 128
HALO = 8
EXT = CX + 2 * HALO
TOP = 8
BUF = EXT + 2 * TOP
VMEM_LIMIT = 16 * 1024 * 1024
PACK_LIMIT = 60 * 1024 * 1024
NBLOCKS = 10 * LEV + 6
F32 = jnp.float32

VM = pl.BlockSpec(memory_space=pltpu.VMEM)
SM = pl.BlockSpec(memory_space=pltpu.SMEM)
FAR = pl.BlockSpec(memory_space=pltpu.HBM)


def call(body, outs, ins, scratch=(), micros=1.0, fetched=(), written=(), limit=VMEM_LIMIT):
    shapes = [jax.ShapeDtypeStruct(s, F32) for s in outs]
    nbytes = 4 * sum(int(a.size) for a in ins) + 4 * sum(
        functools.reduce(lambda a, b: a * b, s, 1) for s in outs
    )
    in_specs = [SM if (a.dtype == jnp.int32 and a.size < 64) else VM for a in ins]
    for i in fetched:
        in_specs[i] = FAR
    return pl.pallas_call(
        body,
        out_shape=shapes,
        in_specs=in_specs,
        out_specs=[FAR if i in written else VM for i in range(len(shapes))],
        scratch_shapes=list(scratch),
        compiler_params=pltpu.CompilerParams(vmem_limit_bytes=limit),
        cost_estimate=pl.CostEstimate(
            flops=int(1.1e9 * micros), bytes_accessed=nbytes, transcendentals=0
        ),
    )(*ins)


def iota(shape, dim):
    return lax.broadcasted_iota(jnp.int32, shape, dim)


def split(x):
    high = x.astype(jnp.bfloat16)
    low = (x - high.astype(F32)).astype(jnp.bfloat16)
    return high, low


def one_hots(cells):
    n = cells.shape[1]
    rows = (iota((LEV * CX, n), 0) == (cells >> 7)).astype(jnp.bfloat16)
    lanes = iota((CY, n), 0) == (cells & 127)
    return rows, lanes


def scatter(rows, lanes, values):
    high, low = split(values)
    zero = jnp.zeros((), jnp.bfloat16)
    parts = jnp.concatenate(
        [jnp.where(lanes, high.astype(F32), 0.0), jnp.where(lanes, low.astype(F32), 0.0)], 0
    ).astype(jnp.bfloat16)
    both = lax.dot_general(
        rows, parts, (((1,), (1,)), ((), ())), preferred_element_type=F32
    )
    return both[:, :CY] + both[:, CY:]


def gather(rows, lanes, field):
    high, low = split(field)
    both = lax.dot_general(
        jnp.concatenate([high, low], 1), rows, (((0,), (0,)), ((), ())),
        preferred_element_type=F32,
    )
    picked = both[:CY] + both[CY:]
    return jnp.sum(jnp.where(lanes, picked, 0.0), 0, keepdims=True)


def swap_halves(x):
    inner = (iota(x.shape, x.ndim - 1) & 15) < 8
    axis = x.ndim - 1
    return jnp.where(inner, pltpu.roll(x, CY - 8, axis), pltpu.roll(x, 8, axis))


def own_half(shape, gy):
    lane = iota(shape, len(shape) - 1) & 15
    return jnp.where(gy == 0, lane, lane ^ 8) < 8


def pack_kernel(
    cells_h, m_h, l_h, f_h, mv_h, v_h, we_h, wn_h,
    b_out, a_out, by_out, strip_out, z_out, lh_out, g1_out,
    g_s, cells, m, l, f, mv, v, we, wn, sems,
):
    far = (cells_h, m_h, l_h, f_h, mv_h, v_h, we_h, wn_h)
    near = (cells, m, l, f, mv, v, we, wn)
    copies = [pltpu.make_async_copy(a, b, sems.at[i]) for i, (a, b) in enumerate(zip(far, near))]
    for copy in copies:
        copy.start()
    copies[0].wait()
    copies[1].wait()
    core = lax.axis_index("gx") % 2
    gy = lax.axis_index("gy")
    lane = iota((CX, CY), 1)
    for s in range(2):
        rows, lanes = one_hots(cells[s, 0])
        h = scatter(rows, lanes, m[s, 0])
        if s == 0:
            for copy in copies[2:]:
                copy.wait()
        lh_out[s] = l[s] + h.reshape(LEV, CX, CY)
        g_s[s] = f[s] - mv[s] * l[s] - v[s]
    g1_out[...] = g_s[1]
    for z in range(LEV):
        for i in range(CX // 8):
            z_out[z * 8 + i] = l[0, z, 8 * i : 8 * i + 8]
            z_out[64 + z * 8 + i] = g_s[0, z, 8 * i : 8 * i + 8]

    def own(get):
        packed = jnp.zeros((CX, CY), F32)
        for z in range(LEV):
            rolled = pltpu.roll(get(z), (16 * z + 8) % CY, 1)
            packed = jnp.where((lane >> 4) == z, rolled, packed)
        return packed

    half = own_half((CX, CY), gy)
    pairs = (
        ((v, 0), (v, 1)), ((l, 0), (g_s, 0)), ((l, 1), (g_s, 1)),
        ((lh_out, 0), (lh_out, 1)), ((we, 0), (wn, 0)), ((we, 1), (wn, 1)),
    )
    for p, (one, two) in enumerate(pairs):
        first = own(lambda z, one=one: one[0][one[1], z])
        second = own(lambda z, two=two: two[0][two[1], z])
        strip_out[p] = jnp.where(half, first, swap_halves(second))
    for i in range(CX // 8):
        z_out[128 + i] = strip_out[1, 8 * i : 8 * i + 8]

    sub = iota((8, CY), 0)
    for out, top in ((b_out, core == 0), (a_out, core != 0)):
        row = jnp.where(top, 0, CX - 8)
        row = pl.multiple_of(row, 8)
        edge = pl.ds(row, 8)
        for k, field in enumerate((v, l, we, wn)):
            for s in range(2):
                out[pl.ds((2 * k + s) * LEV, LEV)] = field[s, :, edge, :]
        keep = jnp.where(top, sub, 7 - sub) < 4
        for s in range(2):
            for z in range(LEV):
                lh_edge = lh_out[s, z, edge, :]
                g_edge = pltpu.roll(g_s[s, z, edge, :], 4, 0)
                out[(8 + s) * LEV + z] = jnp.where(keep, lh_edge, g_edge)
        out[pl.ds(10 * LEV, 6)] = strip_out[:, edge, :]
    by_out[...] = b_out[10 * LEV :]


def obs_kernel(cells, m, v, dep, ov, rv0, rv1, rm_out, qm_out, h2_out):
    for s in range(2):
        rows, lanes = one_hots(cells[s, 0])
        seen = gather(rows, lanes, v[s].reshape(LEV * CX, CY))
        rm = dep[s, 0] - (ov[s, 0] * m[s, 0] + seen)
        rm_out[s, 0] = rm
        h2_out[s] = scatter(rows, lanes, rm).reshape(LEV, CX, CY)
        rv = rv0[0] if s == 0 else rv1[...]
        qm_out[s, 0] = ov[s, 0] * rm + gather(rows, lanes, rv.reshape(LEV * CX, CY))


class Place:
    def __init__(self):
        gx = lax.axis_index("gx")
        self.gy = lax.axis_index("gy")
        core = gx % 2
        self.b_row = pl.multiple_of(jnp.where(core == 0, TOP, TOP + HALO + CX), 8)
        self.a_row = pl.multiple_of(jnp.where(core == 0, TOP + HALO + CX, TOP), 8)
        self.core = core
        self.ay_rows = pl.ds(pl.multiple_of(core * 8, 8), 8)
        self.low = jnp.where(gx == 0, 0.0, 1.0)
        self.high = jnp.where(gx == lax.axis_size("gx") - 1, 0.0, 1.0)


def clear(ref, guard_levels):
    lead = ref.shape[:-2]
    zero = jnp.zeros(lead + (TOP, CY), F32)
    ref[..., 0:TOP, :] = zero
    ref[..., BUF - TOP : BUF, :] = zero
    if guard_levels:
        full = jnp.zeros((BUF, CY), F32)
        for i in range(lead[0]):
            ref[i, 0] = full
            ref[i, LEV + 1] = full


def fill(dst, base, place, tile, b_block, a_block):
    for z in range(LEV):
        dst[base + z, TOP + HALO : TOP + HALO + CX] = tile(z)
        dst[base + z, pl.ds(place.b_row, 8)] = b_block(z)
        dst[base + z, pl.ds(place.a_row, 8)] = a_block(z)


def unpack(place, own, received):
    half = own_half(own.shape, place.gy)
    return jnp.where(half, own, received), swap_halves(jnp.where(half, received, own))


def fill_strips(first, second, place, own, got, own_b, got_b, own_a, got_a):
    mid = pl.ds(TOP + HALO, CX)
    for where, a, b in (
        (mid, own, got),
        (pl.ds(place.b_row, 8), own_b, got_b),
        (pl.ds(place.a_row, 8), own_a, got_a),
    ):
        one, two = unpack(place, a, b)
        first[where] = one
        second[where] = two


ROWS = slice(TOP, TOP + EXT)
UP = slice(TOP + 1, TOP + EXT + 1)
DOWN = slice(TOP - 1, TOP + EXT - 1)


def inject(place, state, strip):
    lane = iota((EXT, CY), 1)
    edge = jnp.where(place.gy == 0, lane, CY - 1 - lane) >= CY - 4
    for z in range(LEV):
        moved = pltpu.roll(strip[ROWS], (120 - 16 * z) % CY, 1)
        state[z + 1, ROWS] = jnp.where(edge, moved, state[z + 1, ROWS])


def extract(place, state, strip):
    lane = iota((EXT, CY), 1)
    half = own_half((EXT, CY), place.gy)
    group = jnp.where(half, lane >> 4, LEV)
    packed = strip[ROWS]
    for z in range(LEV):
        packed = jnp.where(
            group == z, pltpu.roll(state[z + 1, ROWS], (16 * z + 8) % CY, 1), packed
        )
    strip[ROWS] = packed


def coefficients(place, wind, strip, coef, scoef, adjoint):
    lane = iota((EXT, CY), 1)
    if not adjoint:
        for z in range(LEV):
            east, north = 0.5 * wind[0, z, ROWS], 0.5 * wind[1, z, ROWS]
            coef[0, z] = DIFFUSION - east
            coef[1, z] = DIFFUSION + east
            coef[2, z] = jnp.where(lane == CY - 1, 0.0, DIFFUSION - north)
            coef[3, z] = jnp.where(lane == 0, 0.0, DIFFUSION + north)
        east, north = 0.5 * strip[0, ROWS], 0.5 * strip[1, ROWS]
        scoef[0] = DIFFUSION - east
        scoef[1] = DIFFUSION + east
        scoef[2] = DIFFUSION - north
        scoef[3] = DIFFUSION + north
        return
    for z in range(LEV):
        north = wind[1, z, ROWS]
        after = pltpu.roll(north, CY - 1, 1)
        before = pltpu.roll(north, 1, 1)
        coef[0, z] = DIFFUSION + 0.5 * wind[0, z, UP]
        coef[1, z] = DIFFUSION - 0.5 * wind[0, z, DOWN]
        coef[2, z] = jnp.where(lane == CY - 1, 0.0, DIFFUSION + 0.5 * after)
        coef[3, z] = jnp.where(lane == 0, 0.0, DIFFUSION - 0.5 * before)
    scoef[0] = DIFFUSION + 0.5 * strip[0, UP]
    scoef[1] = DIFFUSION - 0.5 * strip[0, DOWN]
    scoef[2] = DIFFUSION + 0.5 * pltpu.roll(strip[1, ROWS], CY - 1, 1)
    scoef[3] = DIFFUSION - 0.5 * pltpu.roll(strip[1, ROWS], 1, 1)


def store(dst, z, out, place):
    dst[z, TOP : TOP + HALO] = out[:HALO] * place.low
    dst[z, TOP + HALO : TOP + HALO + CX] = out[HALO : HALO + CX]
    dst[z, TOP + HALO + CX : TOP + EXT] = out[HALO + CX :] * place.high


def first_slot(count):
    return count & 1


def one_step(place, src, dst, ssrc, sdst, coef, scoef):
    lane = iota((EXT, CY), 1)
    own = ssrc[ROWS]
    for z in range(LEV):
        mid = src[z + 1, ROWS]
        after = pltpu.roll(mid, CY - 1, 1)
        before = pltpu.roll(mid, 1, 1)
        out = (
            CENTRE * mid
            + coef[0, z] * src[z + 1, UP]
            + coef[1, z] * src[z + 1, DOWN]
            + coef[2, z] * after
            + coef[3, z] * before
            + VERTICAL * (src[z + 2, ROWS] + src[z, ROWS])
        )
        store(dst, z + 1, out, place)
    above = jnp.where(lane < CY - 16, pltpu.roll(own, CY - 16, 1), 0.0)
    below = jnp.where(lane >= 16, pltpu.roll(own, 16, 1), 0.0)
    out = (
        CENTRE * own
        + scoef[0] * ssrc[UP]
        + scoef[1] * ssrc[DOWN]
        + scoef[2] * pltpu.roll(own, CY - 1, 1)
        + scoef[3] * pltpu.roll(own, 1, 1)
        + VERTICAL * (above + below)
    )
    sdst[TOP : TOP + HALO] = out[:HALO] * place.low
    sdst[TOP + HALO : TOP + HALO + CX] = out[HALO : HALO + CX]
    sdst[TOP + HALO + CX : TOP + EXT] = out[HALO + CX :] * place.high


def sweep(place, state, strip, coef, scoef, count):
    def two(i, _):
        for j in range(2):

            @pl.when(2 * i + j >= 4 - count)
            def _():
                one_step(
                    place, state.at[j], state.at[1 - j], strip.at[j, 0], strip.at[1 - j, 0],
                    coef, scoef,
                )

        return 0

    lax.fori_loop(0, 2, two, 0)
    inject(place, state.at[0], strip.at[0, 0])


STATE = pltpu.VMEM((2, LEV + 2, BUF, CY), F32)
STRIP = pltpu.VMEM((2, 1, BUF, CY), F32)
COEF = pltpu.VMEM((4, LEV, EXT, CY), F32)
SCOEF = pltpu.VMEM((4, EXT, CY), F32)
WIND = pltpu.VMEM((2, LEV, BUF, CY), F32)
WSTRIP = pltpu.VMEM((2, BUF, CY), F32)


def fill_winds(place, s, we, wn, bg, ag, own, got, by, ay, wind, wstrip):
    for k, field in enumerate((we, wn)):
        fill(
            wind.at[k], 0, place, lambda z, field=field: field[s, z],
            lambda z, k=k: bg[(4 + 2 * k + s) * LEV + z],
            lambda z, k=k: ag[(4 + 2 * k + s) * LEV + z],
        )
    p = 4 + s
    fill_strips(
        wstrip.at[0], wstrip.at[1], place, own[p], got[p],
        bg[10 * LEV + p], by[p], ag[10 * LEV + p], ay[p, place.ay_rows],
    )


def first_kernel(
    counts, v, l, we, wn, mv, lh, g1, own, got, bg, ag, by, ay,
    ext_out, rv_out, even_out, odd_out,
    x_f, x_b, s_f, s_b, coef, scoef, wind, wstrip, extra, estrip,
):
    place = Place()
    clear(x_f, True)
    clear(x_b, True)
    for ref in (s_f, s_b, wind, wstrip, extra, estrip):
        clear(ref, False)

    def strips(p, first, second):
        fill_strips(
            first, second, place, own[p], got[p],
            bg[10 * LEV + p], by[p], ag[10 * LEV + p], ay[p, place.ay_rows],
        )

    fill_winds(place, 0, we, wn, bg, ag, own, got, by, ay, wind, wstrip)
    fill(
        x_b.at[first_slot(counts[0])], 1, place, lambda z: l[1, z],
        lambda z: bg[3 * LEV + z], lambda z: ag[3 * LEV + z],
    )
    strips(2, s_b.at[first_slot(counts[0]), 0], estrip.at[1])
    coefficients(place, wind, wstrip, coef, scoef, True)
    sweep(place, x_b, s_b, coef, scoef, counts[0])
    end = 0
    fill(
        extra.at[0], 0, place, lambda z: lh[0, z],
        lambda z: bg[8 * LEV + z], lambda z: ag[8 * LEV + z],
    )
    fill(
        extra.at[1], 0, place, lambda z: g1[z],
        lambda z: pltpu.roll(bg[9 * LEV + z], 4, 0),
        lambda z: pltpu.roll(ag[9 * LEV + z], 4, 0),
    )
    for z in range(LEV):
        rv = x_b[end, z + 1, ROWS] - extra[0, z, ROWS]
        ext_out[0, z] = rv
        rv_out[0, z] = rv[HALO : HALO + CX]
        rv_out[1, z] = mv[0, z]
    strips(3, estrip.at[0], s_f.at[0, 0])
    ext_out[0, LEV] = s_b[end, 0, ROWS] - estrip[0, ROWS]

    for s in range(2):
        if s == 1:
            fill_winds(place, 1, we, wn, bg, ag, own, got, by, ay, wind, wstrip)
        coefficients(place, wind, wstrip, coef, scoef, False)
        fill(
            x_f.at[first_slot(counts[s])], 1, place, lambda z, s=s: v[s, z],
            lambda z, s=s: bg[s * LEV + z], lambda z, s=s: ag[s * LEV + z],
        )
        if s == 0:
            strips(0, s_f.at[first_slot(counts[s]), 0], estrip.at[0])
        else:
            strips(0, estrip.at[0], s_f.at[first_slot(counts[s]), 0])
        sweep(place, x_f, s_f, coef, scoef, counts[s])
        for z in range(LEV):
            out = x_f[end, z + 1, ROWS]
            if s == 0:
                ext_out[1, z] = out + extra[1, z, ROWS]
            else:
                ext_out[2, z] = out
        out = s_f[end, 0, ROWS]
        ext_out[1 + s, LEV] = out + estrip[1, ROWS] if s == 0 else out

    tile = slice(HALO, HALO + CX)
    odd = lax.axis_index("tm") % 2

    @pl.when(odd == 0)
    def _():
        even_out[0] = ext_out[2, :LEV, tile]
        even_out[1] = rv_out[1]
        odd_out[...] = rv_out[...]

    @pl.when(odd == 1)
    def _():
        even_out[...] = rv_out[...]
        odd_out[0] = ext_out[2, :LEV, tile]
        odd_out[1] = rv_out[1]


def lane_sum(x):
    return functools.reduce(
        lambda a, b: a + b, [x[:, i : i + CY] for i in range(0, x.shape[1], CY)]
    )


def second_kernel(
    counts, ext, we, wn, lh, own, got, bg, ag, by, ay, zt, zh,
    mv,
    rv1_out, rl1_out, rl2_out, f21_out, b20_out, ql1_out, b21_out, dots_out,
    x_f, x_b, s_f, s_b, coef, scoef, wind, wstrip, extra, estrip,
):
    place = Place()
    clear(x_f, True)
    clear(x_b, True)
    for ref in (s_f, s_b, wind, wstrip, extra, estrip):
        clear(ref, False)
    tile = slice(HALO, HALO + CX)
    follows = jnp.where(lax.axis_index("tm") == lax.axis_size("tm") - 1, 0.0, 1.0)

    fill_winds(place, 1, we, wn, bg, ag, own, got, by, ay, wind, wstrip)
    coefficients(place, wind, wstrip, coef, scoef, True)

    def z_tile(base):
        return lambda z: zt[base + 8 * z : base + 8 * z + 8].reshape(CX, CY)

    fill(x_b.at[first_slot(counts[1])], 1, place, z_tile(0), lambda z: zh[z], lambda z: zh[16 + z])
    fill(
        extra.at[1], 0, place, z_tile(64),
        lambda z: pltpu.roll(zh[8 + z], 4, 0), lambda z: pltpu.roll(zh[24 + z], 4, 0),
    )
    fill_strips(
        s_b.at[first_slot(counts[1]), 0], estrip.at[1], place,
        zt[128:136].reshape(CX, CY), zh[37:45].reshape(CX, CY),
        zh[32], zh[33], zh[34], zh[35 + place.core],
    )
    sweep(place, x_b, s_b, coef, scoef, counts[1])
    end = 0
    slot = first_slot(counts[1])

    fill(
        extra.at[0], 0, place, lambda z: lh[1, z],
        lambda z: bg[9 * LEV + z], lambda z: ag[9 * LEV + z],
    )
    fill_strips(
        s_f.at[0, 0], estrip.at[0], place, own[3], got[3],
        bg[10 * LEV + 3], by[3], ag[10 * LEV + 3], ay[3, place.ay_rows],
    )
    for z in range(LEV):
        rv = x_b[end, z + 1, ROWS] - extra[0, z, ROWS]
        x_f[slot, z + 1, ROWS] = rv
        rv1_out[z] = rv[tile]
        rl = (extra[1, z, ROWS] + ext[2, z]) * follows
        x_b[slot, z + 1, ROWS] = rl
        rl2_out[z] = rl[tile]
    s_f[slot, 0, ROWS] = s_b[end, 0, ROWS] - estrip[0, ROWS]
    s_b[slot, 0, ROWS] = (estrip[1, ROWS] + ext[2, LEV]) * follows
    extract(place, x_f.at[slot], s_f.at[slot, 0])
    extract(place, x_b.at[slot], s_b.at[slot, 0])

    sweep(place, x_b, s_b, coef, scoef, counts[1])
    cross = jnp.zeros((8, CY), F32)
    square = jnp.zeros((8, CY), F32)

    def dots(r, q):
        return jnp.sum((r * q).reshape(-1, 8, CY), 0), jnp.sum((q * q).reshape(-1, 8, CY), 0)

    for z in range(LEV):
        rl1 = ext[1, z, tile]
        rl1_out[z] = rl1
        b21_out[z] = x_b[end, z + 1, TOP + HALO : TOP + HALO + CX]
    coefficients(place, wind, wstrip, coef, scoef, False)
    sweep(place, x_f, s_f, coef, scoef, counts[1])
    for z in range(LEV):
        f21_out[z] = x_f[end, z + 1, TOP + HALO : TOP + HALO + CX]

    slot = first_slot(counts[0])
    fill_winds(place, 0, we, wn, bg, ag, own, got, by, ay, wind, wstrip)
    coefficients(place, wind, wstrip, coef, scoef, False)
    for z in range(LEV):
        x_f[slot, z + 1, ROWS] = ext[0, z]
        x_b[slot, z + 1, ROWS] = ext[1, z]
    s_f[slot, 0, ROWS] = ext[0, LEV]
    s_b[slot, 0, ROWS] = ext[1, LEV]
    extract(place, x_f.at[slot], s_f.at[slot, 0])
    extract(place, x_b.at[slot], s_b.at[slot, 0])
    sweep(place, x_f, s_f, coef, scoef, counts[0])
    for z in range(LEV):
        rl1 = ext[1, z, tile]
        ql = mv[1, z] * rl1 + rv1_out[z] - x_f[end, z + 1, TOP + HALO : TOP + HALO + CX]
        ql1_out[z] = ql
        c, q = dots(rl1, ql)
        cross, square = cross + c, square + q
    coefficients(place, wind, wstrip, coef, scoef, True)
    sweep(place, x_b, s_b, coef, scoef, counts[0])
    for z in range(LEV):
        b20_out[z] = x_b[end, z + 1, TOP + HALO : TOP + HALO + CX]

    dots_out[0] = cross
    dots_out[1] = square


def dots_kernel(
    even, odd, rl2, f21, b20, z_own, h2, rv0, dots_in, rl1, rv1, b21, ql1, qm, rm, m,
    keep_out, send_out,
):
    follows = jnp.where(lax.axis_index("tm") == lax.axis_size("tm") - 1, 0.0, 1.0)
    starts = jnp.where(lax.axis_index("tm") == 0, 1.0, 0.0)
    for i, kept in enumerate((rm, qm, m)):
        for s in range(2):
            for k in range(m.shape[-1] // CY):
                keep_out[6, 2 * i + s, k : k + 1] = kept[s, 0, :, k * CY : (k + 1) * CY]
    rm_rows, qm_rows = keep_out[6, 0:2, 0:8], keep_out[6, 2:4, 0:8]
    cross = dots_in[0] + jnp.sum(rm_rows * qm_rows, 0)
    square = dots_in[1] + jnp.sum(qm_rows * qm_rows, 0)
    is_odd = lax.axis_index("tm") % 2 == 1

    def total(x):
        return jnp.sum(x.reshape(-1, 8, CY), 0)

    for z in range(LEV):
        rl0 = z_own[64 + 8 * z : 72 + 8 * z].reshape(CX, CY) + jnp.where(is_odd, even[0, z], odd[0, z])
        rv = rv0[0, z]
        qv = rl0 - b20[z] + h2[0, z]
        qv1 = rl1[z] - b21[z] + h2[1, z]
        for i, kept in enumerate((rl0, rl1[z], rv1[z], qv, qv1, ql1[z])):
            keep_out[i, z] = kept
        cross += total(rv1[z] * qv1)
        square += total(qv1 * qv1)
        ql = (rv0[1, z] * rl0 + rv) * starts
        rl2z = rl2[z]
        next_mv = jnp.where(is_odd, odd[1, z], even[1, z])
        next_rv = jnp.where(is_odd, odd[0, z], even[0, z])
        q2 = (next_mv * rl2z + next_rv - f21[z]) * follows
        cross += total(rv * qv) + total(rl0 * ql) + total(rl2z * q2)
        square += total(qv * qv) + total(ql * ql) + total(q2 * q2)
    cross = jnp.sum(jnp.sum(cross, 0, keepdims=True), 1, keepdims=True)
    square = jnp.sum(jnp.sum(square, 0, keepdims=True), 1, keepdims=True)
    n = send_out.shape[0]
    lane = iota((n, CY), 1)
    send_out[...] = jnp.where(lane == 0, cross, jnp.where(lane == 1, square, 0.0))


def last_kernel(
    sums, l, v, rv0, z_f2, keep,
    l_out, m_out, v_out, a_out, b_out, c_out,
):
    total = jnp.sum(sums[...], 0, keepdims=True)
    lane = iota((1, CY), 1)
    cross = jnp.sum(jnp.where(lane == 0, total, 0.0), 1, keepdims=True)
    square = jnp.sum(jnp.where(lane == 1, total, 0.0), 1, keepdims=True)
    alpha = cross / (square + 1e-06)
    for s in range(2):
        for k in range(m_out.shape[-1] // CY):
            rm, qm, m = (keep[6, 2 * i + s, k : k + 1] for i in range(3))
            m_out[s, 0, :, k * CY : (k + 1) * CY] = m + alpha * rm
            b_out[s, 0, :, k * CY : (k + 1) * CY] = rm - alpha * qm
    for z in range(LEV):
        rl0, rl1, rv1, qv0, qv1, ql1 = (keep[i, z] for i in range(6))
        ql0 = rv0[1, z] * rl0 + rv0[0, z] - z_f2[z]
        l_out[0, z] = l[0, z] + alpha * rl0
        l_out[1, z] = l[1, z] + alpha * rl1
        v_out[0, z] = v[0, z] + alpha * rv0[0, z]
        v_out[1, z] = v[1, z] + alpha * rv1
        a_out[0, z] = rl0 - alpha * ql0
        a_out[1, z] = rl1 - alpha * ql1
        c_out[0, z] = rv0[0, z] - alpha * qv0
        c_out[1, z] = rv1 - alpha * qv1


def shards(sizes, l4, m4, v4, f4, d4, mv4, ov4, we4, wn4, cells4, counts):
    ntm, ngx, ngy = sizes
    tile = (LEV, CX, CY)
    obs = m4.shape

    def pair_b(i):
        return i - 1 if i % 2 == 0 else i + 1

    def plane(move_x, move_y):
        pairs = []
        for x in range(ngx):
            for y in range(ngy):
                to = move_x(x)
                if 0 <= to < ngx:
                    pairs.append((x * ngy + y, to * ngy + (1 - y if move_y else y)))
        return pairs

    axes = ("gx", "gy")
    down = [(i + 1, i) for i in range(ntm - 1)]
    up = [(i, i + 1) for i in range(ntm - 1)]
    edge = 10 * LEV

    fields = pltpu.VMEM((2,) + tile, F32)
    b_send, a_send, by_send, own, z_send, lh, g1 = call(
        pack_kernel,
        [(NBLOCKS, 8, CY)] * 2 + [(6, 8, CY), (6, CX, CY), (136, 8, CY), (2,) + tile, tile],
        [cells4, m4, l4, f4, mv4, v4, we4, wn4],
        [fields, pltpu.VMEM(obs, jnp.int32), pltpu.VMEM(obs, F32)]
        + [fields] * 6
        + [pltpu.SemaphoreType.DMA((8,))],
        micros=2.5,
        fetched=range(8),
        limit=PACK_LIMIT,
    )
    got = lax.ppermute(own, axes, plane(lambda i: i, True))
    bg = lax.ppermute(b_send, axes, plane(pair_b, False))
    ag = lax.ppermute(a_send, axes, plane(lambda i: i ^ 1, False))
    zt = lax.ppermute(z_send, "tm", down)
    ay_send = jnp.concatenate([got[:, :8], got[:, CX - 8 :]], 1)
    ay_send, by_send = lax.optimization_barrier((ay_send, by_send))
    by = lax.ppermute(by_send, axes, plane(pair_b, True))
    ay = lax.ppermute(ay_send, axes, plane(lambda i: i ^ 1, False))

    z_edges = jnp.concatenate(
        [
            bg[2 * LEV : 3 * LEV], bg[8 * LEV : 9 * LEV],
            ag[2 * LEV : 3 * LEV], ag[8 * LEV : 9 * LEV],
            bg[edge + 1 : edge + 2], by[1:2], ag[edge + 1 : edge + 2],
            ay[1].reshape(2, 8, CY), got[1].reshape(8, 8, CY),
        ],
        0,
    )
    zh = lax.ppermute(z_edges, "tm", down)
    scratch = [
        STATE, STATE, STRIP, STRIP, COEF, SCOEF, WIND, WSTRIP,
        pltpu.VMEM((2, LEV, BUF, CY), F32), pltpu.VMEM((2, BUF, CY), F32),
    ]
    ext, rv0, even_send, odd_send = call(
        first_kernel,
        [(3, LEV + 1, EXT, CY)] + [(2,) + tile] * 3,
        [counts, v4, l4, we4, wn4, mv4, lh, g1, own, got, bg, ag, by, ay],
        scratch,
        micros=5.0,
    )
    swap = lambda first: [(i, i + 1) for i in range(first, ntm - 1, 2)] + [
        (i + 1, i) for i in range(first, ntm - 1, 2)
    ]
    even = lax.ppermute(even_send, "tm", swap(0))
    odd = lax.ppermute(odd_send, "tm", swap(1))
    rv1, rl1, rl2, f21, b20, ql1, b21, dots = call(
        second_kernel,
        [tile] * 7 + [(2, 8, CY)],
        [counts, ext, we4, wn4, lh, own, got, bg, ag, by, ay, zt, zh, mv4],
        scratch,
        micros=9.0,
    )
    z_f2 = lax.ppermute(f21, "tm", up)
    rm, qm, h2 = call(
        obs_kernel, [obs, obs, (2,) + tile], [cells4, m4, v4, d4, ov4, rv0, rv1], micros=3.4
    )
    n = ntm * ngx * ngy
    keep, send = call(
        dots_kernel,
        [(7,) + tile, (n, CY)],
        [even, odd, rl2, f21, b20, z_send, h2, rv0, dots, rl1, rv1, b21, ql1, qm, rm, m4],
        micros=0.4,
    )
    sums = lax.all_to_all(send, ("tm", "gx", "gy"), 0, 0, tiled=True)
    return call(
        last_kernel,
        [l4.shape, obs, l4.shape, l4.shape, obs, l4.shape],
        [sums, l4, v4, rv0, z_f2, keep],
        micros=1.5,
    )


def solution(mesh):
    field = P("tm", None, "gx", "gy")
    obs = P("tm", "gx", "gy", None)
    sizes = tuple(mesh.shape[a] for a in ("tm", "gx", "gy"))
    return jax.shard_map(
        functools.partial(shards, sizes),
        mesh=mesh,
        in_specs=(field, obs, field, field, obs, field, obs, field, field, obs, P("tm")),
        out_specs=(field, obs, field, field, obs, field),
        check_vma=False,
    )
```

```python
import functools

import jax
import jax.numpy as jnp
from jax import lax
from jax.experimental import pallas as pl
from jax.experimental.pallas import tpu as pltpu
from jax.sharding import PartitionSpec as P

DIFFUSION = 0.18
VERTICAL = 0.1
CENTRE = 1.0 - 4.0 * DIFFUSION - 2.0 * VERTICAL

LEV, CX, CY = 8, 64, 128
HALO = 8
EXT = CX + 2 * HALO
TOP = 8
BUF = EXT + 2 * TOP
VMEM_LIMIT = 16 * 1024 * 1024
PACK_LIMIT = 60 * 1024 * 1024
NBLOCKS = 10 * LEV + 6
F32 = jnp.float32

VM = pl.BlockSpec(memory_space=pltpu.VMEM)
SM = pl.BlockSpec(memory_space=pltpu.SMEM)
FAR = pl.BlockSpec(memory_space=pltpu.HBM)


def call(body, outs, ins, scratch=(), micros=1.0, fetched=(), written=(), limit=VMEM_LIMIT):
    shapes = [jax.ShapeDtypeStruct(s, F32) for s in outs]
    nbytes = 4 * sum(int(a.size) for a in ins) + 4 * sum(
        functools.reduce(lambda a, b: a * b, s, 1) for s in outs
    )
    in_specs = [SM if (a.dtype == jnp.int32 and a.size < 64) else VM for a in ins]
    for i in fetched:
        in_specs[i] = FAR
    return pl.pallas_call(
        body,
        out_shape=shapes,
        in_specs=in_specs,
        out_specs=[FAR if i in written else VM for i in range(len(shapes))],
        scratch_shapes=list(scratch),
        compiler_params=pltpu.CompilerParams(vmem_limit_bytes=limit),
        cost_estimate=pl.CostEstimate(
            flops=int(1.1e9 * micros), bytes_accessed=nbytes, transcendentals=0
        ),
    )(*ins)


def iota(shape, dim):
    return lax.broadcasted_iota(jnp.int32, shape, dim)


def split(x):
    high = x.astype(jnp.bfloat16)
    low = (x - high.astype(F32)).astype(jnp.bfloat16)
    return high, low


def one_hots(cells):
    n = cells.shape[1]
    rows = (iota((LEV * CX, n), 0) == (cells >> 7)).astype(jnp.bfloat16)
    lanes = iota((CY, n), 0) == (cells & 127)
    return rows, lanes


def scatter(rows, lanes, values):
    high, low = split(values)
    zero = jnp.zeros((), jnp.bfloat16)
    parts = jnp.concatenate(
        [jnp.where(lanes, high.astype(F32), 0.0), jnp.where(lanes, low.astype(F32), 0.0)], 0
    ).astype(jnp.bfloat16)
    both = lax.dot_general(
        rows, parts, (((1,), (1,)), ((), ())), preferred_element_type=F32
    )
    return both[:, :CY] + both[:, CY:]


def gather(rows, lanes, field):
    high, low = split(field)
    both = lax.dot_general(
        jnp.concatenate([high, low], 1), rows, (((0,), (0,)), ((), ())),
        preferred_element_type=F32,
    )
    picked = both[:CY] + both[CY:]
    return jnp.sum(jnp.where(lanes, picked, 0.0), 0, keepdims=True)


def swap_halves(x):
    inner = (iota(x.shape, x.ndim - 1) & 15) < 8
    axis = x.ndim - 1
    return jnp.where(inner, pltpu.roll(x, CY - 8, axis), pltpu.roll(x, 8, axis))


def own_half(shape, gy):
    lane = iota(shape, len(shape) - 1) & 15
    return jnp.where(gy == 0, lane, lane ^ 8) < 8


def pack_kernel(
    cells_h, m_h, l_h, f_h, mv_h, v_h, we_h, wn_h,
    b_out, a_out, by_out, strip_out, z_out,
    lh_out, g_s, cells, m, l, f, mv, v, we, wn, sems,
):
    far = (cells_h, m_h, l_h, f_h, mv_h, v_h, we_h, wn_h)
    near = (cells, m, l, f, mv, v, we, wn)
    copies = [pltpu.make_async_copy(a, b, sems.at[i]) for i, (a, b) in enumerate(zip(far, near))]
    for copy in copies:
        copy.start()
    copies[0].wait()
    copies[1].wait()
    core = lax.axis_index("gx") % 2
    gy = lax.axis_index("gy")
    lane = iota((CX, CY), 1)
    for s in range(2):
        rows, lanes = one_hots(cells[s, 0])
        h = scatter(rows, lanes, m[s, 0])
        if s == 0:
            for copy in copies[2:]:
                copy.wait()
        lh_out[s] = l[s] + h.reshape(LEV, CX, CY)
        g_s[s] = f[s] - mv[s] * l[s] - v[s]
    for z in range(LEV):
        for i in range(CX // 8):
            z_out[z * 8 + i] = l[0, z, 8 * i : 8 * i + 8]
            z_out[64 + z * 8 + i] = g_s[0, z, 8 * i : 8 * i + 8]

    def own(get):
        packed = jnp.zeros((CX, CY), F32)
        for z in range(LEV):
            rolled = pltpu.roll(get(z), (16 * z + 8) % CY, 1)
            packed = jnp.where((lane >> 4) == z, rolled, packed)
        return packed

    half = own_half((CX, CY), gy)
    pairs = (
        ((v, 0), (v, 1)), ((l, 0), (g_s, 0)), ((l, 1), (g_s, 1)),
        ((lh_out, 0), (lh_out, 1)), ((we, 0), (wn, 0)), ((we, 1), (wn, 1)),
    )
    for p, (one, two) in enumerate(pairs):
        first = own(lambda z, one=one: one[0][one[1], z])
        second = own(lambda z, two=two: two[0][two[1], z])
        strip_out[p] = jnp.where(half, first, swap_halves(second))
    for i in range(CX // 8):
        z_out[128 + i] = strip_out[1, 8 * i : 8 * i + 8]

    sub = iota((8, CY), 0)
    for out, top in ((b_out, core == 0), (a_out, core != 0)):
        row = jnp.where(top, 0, CX - 8)
        row = pl.multiple_of(row, 8)
        edge = pl.ds(row, 8)
        for k, field in enumerate((v, l, we, wn)):
            for s in range(2):
                out[pl.ds((2 * k + s) * LEV, LEV)] = field[s, :, edge, :]
        keep = jnp.where(top, sub, 7 - sub) < 4
        for s in range(2):
            for z in range(LEV):
                lh_edge = lh_out[s, z, edge, :]
                g_edge = pltpu.roll(g_s[s, z, edge, :], 4, 0)
                out[(8 + s) * LEV + z] = jnp.where(keep, lh_edge, g_edge)
        out[pl.ds(10 * LEV, 6)] = strip_out[:, edge, :]
    by_out[...] = b_out[10 * LEV :]


def local_kernel(cells, m, l, f, mv, v, strips, lh_out, g1_out, own_out):
    for s in range(2):
        rows, lanes = one_hots(cells[s, 0])
        lh_out[s] = l[s] + scatter(rows, lanes, m[s, 0]).reshape(LEV, CX, CY)
    g1_out[...] = f[1] - mv[1] * l[1] - v[1]
    own_out[...] = strips[...]


def obs_kernel(cells, m, v, dep, ov, rv0, rv1, rm_out, qm_out, h2_out):
    for s in range(2):
        rows, lanes = one_hots(cells[s, 0])
        seen = gather(rows, lanes, v[s].reshape(LEV * CX, CY))
        rm = dep[s, 0] - (ov[s, 0] * m[s, 0] + seen)
        rm_out[s, 0] = rm
        h2_out[s] = scatter(rows, lanes, rm).reshape(LEV, CX, CY)
        rv = rv0[0] if s == 0 else rv1[...]
        qm_out[s, 0] = ov[s, 0] * rm + gather(rows, lanes, rv.reshape(LEV * CX, CY))


class Place:
    def __init__(self):
        gx = lax.axis_index("gx")
        self.gy = lax.axis_index("gy")
        core = gx % 2
        self.b_row = pl.multiple_of(jnp.where(core == 0, TOP, TOP + HALO + CX), 8)
        self.a_row = pl.multiple_of(jnp.where(core == 0, TOP + HALO + CX, TOP), 8)
        self.core = core
        self.ay_rows = pl.ds(pl.multiple_of(core * 8, 8), 8)
        self.low = jnp.where(gx == 0, 0.0, 1.0)
        self.high = jnp.where(gx == lax.axis_size("gx") - 1, 0.0, 1.0)


def clear(ref, guard_levels):
    lead = ref.shape[:-2]
    zero = jnp.zeros(lead + (TOP, CY), F32)
    ref[..., 0:TOP, :] = zero
    ref[..., BUF - TOP : BUF, :] = zero
    if guard_levels:
        full = jnp.zeros((BUF, CY), F32)
        for i in range(lead[0]):
            ref[i, 0] = full
            ref[i, LEV + 1] = full


def fill(dst, base, place, tile, b_block, a_block):
    for z in range(LEV):
        dst[base + z, TOP + HALO : TOP + HALO + CX] = tile(z)
        dst[base + z, pl.ds(place.b_row, 8)] = b_block(z)
        dst[base + z, pl.ds(place.a_row, 8)] = a_block(z)


def unpack(place, own, received):
    half = own_half(own.shape, place.gy)
    return jnp.where(half, own, received), swap_halves(jnp.where(half, received, own))


def fill_strips(first, second, place, own, got, own_b, got_b, own_a, got_a):
    mid = pl.ds(TOP + HALO, CX)
    for where, a, b in (
        (mid, own, got),
        (pl.ds(place.b_row, 8), own_b, got_b),
        (pl.ds(place.a_row, 8), own_a, got_a),
    ):
        one, two = unpack(place, a, b)
        first[where] = one
        second[where] = two


ROWS = slice(TOP, TOP + EXT)
UP = slice(TOP + 1, TOP + EXT + 1)
DOWN = slice(TOP - 1, TOP + EXT - 1)


def inject(place, state, strip):
    lane = iota((EXT, CY), 1)
    edge = jnp.where(place.gy == 0, lane, CY - 1 - lane) >= CY - 4
    for z in range(LEV):
        moved = pltpu.roll(strip[ROWS], (120 - 16 * z) % CY, 1)
        state[z + 1, ROWS] = jnp.where(edge, moved, state[z + 1, ROWS])


def extract(place, state, strip):
    lane = iota((EXT, CY), 1)
    half = own_half((EXT, CY), place.gy)
    group = jnp.where(half, lane >> 4, LEV)
    packed = strip[ROWS]
    for z in range(LEV):
        packed = jnp.where(
            group == z, pltpu.roll(state[z + 1, ROWS], (16 * z + 8) % CY, 1), packed
        )
    strip[ROWS] = packed


def coefficients(place, wind, strip, coef, scoef, adjoint):
    lane = iota((EXT, CY), 1)
    if not adjoint:
        for z in range(LEV):
            east, north = 0.5 * wind[0, z, ROWS], 0.5 * wind[1, z, ROWS]
            coef[0, z] = DIFFUSION - east
            coef[1, z] = DIFFUSION + east
            coef[2, z] = jnp.where(lane == CY - 1, 0.0, DIFFUSION - north)
            coef[3, z] = jnp.where(lane == 0, 0.0, DIFFUSION + north)
        east, north = 0.5 * strip[0, ROWS], 0.5 * strip[1, ROWS]
        scoef[0] = DIFFUSION - east
        scoef[1] = DIFFUSION + east
        scoef[2] = DIFFUSION - north
        scoef[3] = DIFFUSION + north
        return
    for z in range(LEV):
        north = wind[1, z, ROWS]
        after = pltpu.roll(north, CY - 1, 1)
        before = pltpu.roll(north, 1, 1)
        coef[0, z] = DIFFUSION + 0.5 * wind[0, z, UP]
        coef[1, z] = DIFFUSION - 0.5 * wind[0, z, DOWN]
        coef[2, z] = jnp.where(lane == CY - 1, 0.0, DIFFUSION + 0.5 * after)
        coef[3, z] = jnp.where(lane == 0, 0.0, DIFFUSION - 0.5 * before)
    scoef[0] = DIFFUSION + 0.5 * strip[0, UP]
    scoef[1] = DIFFUSION - 0.5 * strip[0, DOWN]
    scoef[2] = DIFFUSION + 0.5 * pltpu.roll(strip[1, ROWS], CY - 1, 1)
    scoef[3] = DIFFUSION - 0.5 * pltpu.roll(strip[1, ROWS], 1, 1)


def store(dst, z, out, place):
    dst[z, TOP : TOP + HALO] = out[:HALO] * place.low
    dst[z, TOP + HALO : TOP + HALO + CX] = out[HALO : HALO + CX]
    dst[z, TOP + HALO + CX : TOP + EXT] = out[HALO + CX :] * place.high


def first_slot(count):
    return count & 1


def one_step(place, src, dst, ssrc, sdst, coef, scoef):
    lane = iota((EXT, CY), 1)
    own = ssrc[ROWS]
    for z in range(LEV):
        mid = src[z + 1, ROWS]
        after = pltpu.roll(mid, CY - 1, 1)
        before = pltpu.roll(mid, 1, 1)
        out = (
            CENTRE * mid
            + coef[0, z] * src[z + 1, UP]
            + coef[1, z] * src[z + 1, DOWN]
            + coef[2, z] * after
            + coef[3, z] * before
            + VERTICAL * (src[z + 2, ROWS] + src[z, ROWS])
        )
        store(dst, z + 1, out, place)
    above = jnp.where(lane < CY - 16, pltpu.roll(own, CY - 16, 1), 0.0)
    below = jnp.where(lane >= 16, pltpu.roll(own, 16, 1), 0.0)
    out = (
        CENTRE * own
        + scoef[0] * ssrc[UP]
        + scoef[1] * ssrc[DOWN]
        + scoef[2] * pltpu.roll(own, CY - 1, 1)
        + scoef[3] * pltpu.roll(own, 1, 1)
        + VERTICAL * (above + below)
    )
    sdst[TOP : TOP + HALO] = out[:HALO] * place.low
    sdst[TOP + HALO : TOP + HALO + CX] = out[HALO : HALO + CX]
    sdst[TOP + HALO + CX : TOP + EXT] = out[HALO + CX :] * place.high


def sweep(place, state, strip, coef, scoef, count):
    def two(i, _):
        for j in range(2):

            @pl.when(2 * i + j >= 4 - count)
            def _():
                one_step(
                    place, state.at[j], state.at[1 - j], strip.at[j, 0], strip.at[1 - j, 0],
                    coef, scoef,
                )

        return 0

    lax.fori_loop(0, 2, two, 0)
    inject(place, state.at[0], strip.at[0, 0])


STATE = pltpu.VMEM((2, LEV + 2, BUF, CY), F32)
STRIP = pltpu.VMEM((2, 1, BUF, CY), F32)
COEF = pltpu.VMEM((4, LEV, EXT, CY), F32)
SCOEF = pltpu.VMEM((4, EXT, CY), F32)
WIND = pltpu.VMEM((2, LEV, BUF, CY), F32)
WSTRIP = pltpu.VMEM((2, BUF, CY), F32)


def fill_winds(place, s, we, wn, bg, ag, own, got, by, ay, wind, wstrip):
    for k, field in enumerate((we, wn)):
        fill(
            wind.at[k], 0, place, lambda z, field=field: field[s, z],
            lambda z, k=k: bg[(4 + 2 * k + s) * LEV + z],
            lambda z, k=k: ag[(4 + 2 * k + s) * LEV + z],
        )
    p = 4 + s
    fill_strips(
        wstrip.at[0], wstrip.at[1], place, own[p], got[p],
        bg[10 * LEV + p], by[p], ag[10 * LEV + p], ay[p, place.ay_rows],
    )


def first_kernel(
    counts, v, l, we, wn, mv, lh, g1, own, got, bg, ag, by, ay,
    ext_out, rv_out, even_out, odd_out,
    x_f, x_b, s_f, s_b, coef, scoef, wind, wstrip, extra, estrip,
):
    place = Place()
    clear(x_f, True)
    clear(x_b, True)
    for ref in (s_f, s_b, wind, wstrip, extra, estrip):
        clear(ref, False)

    def strips(p, first, second):
        fill_strips(
            first, second, place, own[p], got[p],
            bg[10 * LEV + p], by[p], ag[10 * LEV + p], ay[p, place.ay_rows],
        )

    fill_winds(place, 0, we, wn, bg, ag, own, got, by, ay, wind, wstrip)
    fill(
        x_b.at[first_slot(counts[0])], 1, place, lambda z: l[1, z],
        lambda z: bg[3 * LEV + z], lambda z: ag[3 * LEV + z],
    )
    strips(2, s_b.at[first_slot(counts[0]), 0], estrip.at[1])
    coefficients(place, wind, wstrip, coef, scoef, True)
    sweep(place, x_b, s_b, coef, scoef, counts[0])
    end = 0
    fill(
        extra.at[0], 0, place, lambda z: lh[0, z],
        lambda z: bg[8 * LEV + z], lambda z: ag[8 * LEV + z],
    )
    fill(
        extra.at[1], 0, place, lambda z: g1[z],
        lambda z: pltpu.roll(bg[9 * LEV + z], 4, 0),
        lambda z: pltpu.roll(ag[9 * LEV + z], 4, 0),
    )
    for z in range(LEV):
        rv = x_b[end, z + 1, ROWS] - extra[0, z, ROWS]
        ext_out[0, z] = rv
        rv_out[0, z] = rv[HALO : HALO + CX]
        rv_out[1, z] = mv[0, z]
    strips(3, estrip.at[0], s_f.at[0, 0])
    ext_out[0, LEV] = s_b[end, 0, ROWS] - estrip[0, ROWS]

    for s in range(2):
        if s == 1:
            fill_winds(place, 1, we, wn, bg, ag, own, got, by, ay, wind, wstrip)
        coefficients(place, wind, wstrip, coef, scoef, False)
        fill(
            x_f.at[first_slot(counts[s])], 1, place, lambda z, s=s: v[s, z],
            lambda z, s=s: bg[s * LEV + z], lambda z, s=s: ag[s * LEV + z],
        )
        if s == 0:
            strips(0, s_f.at[first_slot(counts[s]), 0], estrip.at[0])
        else:
            strips(0, estrip.at[0], s_f.at[first_slot(counts[s]), 0])
        sweep(place, x_f, s_f, coef, scoef, counts[s])
        for z in range(LEV):
            out = x_f[end, z + 1, ROWS]
            if s == 0:
                ext_out[1, z] = out + extra[1, z, ROWS]
            else:
                ext_out[2, z] = out
        out = s_f[end, 0, ROWS]
        ext_out[1 + s, LEV] = out + estrip[1, ROWS] if s == 0 else out

    tile = slice(HALO, HALO + CX)
    odd = lax.axis_index("tm") % 2

    @pl.when(odd == 0)
    def _():
        even_out[0] = ext_out[2, :LEV, tile]
        even_out[1] = rv_out[1]
        odd_out[...] = rv_out[...]

    @pl.when(odd == 1)
    def _():
        even_out[...] = rv_out[...]
        odd_out[0] = ext_out[2, :LEV, tile]
        odd_out[1] = rv_out[1]


def lane_sum(x):
    return functools.reduce(
        lambda a, b: a + b, [x[:, i : i + CY] for i in range(0, x.shape[1], CY)]
    )


def second_kernel(
    counts, ext, we, wn, lh, own, got, bg, ag, by, ay, zt, zh,
    mv,
    rv1_out, rl1_out, rl2_out, f21_out, b20_out, ql1_out, b21_out, dots_out,
    x_f, x_b, s_f, s_b, coef, scoef, wind, wstrip, extra, estrip,
):
    place = Place()
    clear(x_f, True)
    clear(x_b, True)
    for ref in (s_f, s_b, wind, wstrip, extra, estrip):
        clear(ref, False)
    tile = slice(HALO, HALO + CX)
    follows = jnp.where(lax.axis_index("tm") == lax.axis_size("tm") - 1, 0.0, 1.0)

    fill_winds(place, 1, we, wn, bg, ag, own, got, by, ay, wind, wstrip)
    coefficients(place, wind, wstrip, coef, scoef, True)

    def z_tile(base):
        return lambda z: zt[base + 8 * z : base + 8 * z + 8].reshape(CX, CY)

    fill(x_b.at[first_slot(counts[1])], 1, place, z_tile(0), lambda z: zh[z], lambda z: zh[16 + z])
    fill(
        extra.at[1], 0, place, z_tile(64),
        lambda z: pltpu.roll(zh[8 + z], 4, 0), lambda z: pltpu.roll(zh[24 + z], 4, 0),
    )
    fill_strips(
        s_b.at[first_slot(counts[1]), 0], estrip.at[1], place,
        zt[128:136].reshape(CX, CY), zh[37:45].reshape(CX, CY),
        zh[32], zh[33], zh[34], zh[35 + place.core],
    )
    sweep(place, x_b, s_b, coef, scoef, counts[1])
    end = 0
    slot = first_slot(counts[1])

    fill(
        extra.at[0], 0, place, lambda z: lh[1, z],
        lambda z: bg[9 * LEV + z], lambda z: ag[9 * LEV + z],
    )
    fill_strips(
        s_f.at[0, 0], estrip.at[0], place, own[3], got[3],
        bg[10 * LEV + 3], by[3], ag[10 * LEV + 3], ay[3, place.ay_rows],
    )
    for z in range(LEV):
        rv = x_b[end, z + 1, ROWS] - extra[0, z, ROWS]
        x_f[slot, z + 1, ROWS] = rv
        rv1_out[z] = rv[tile]
        rl = (extra[1, z, ROWS] + ext[2, z]) * follows
        x_b[slot, z + 1, ROWS] = rl
        rl2_out[z] = rl[tile]
    s_f[slot, 0, ROWS] = s_b[end, 0, ROWS] - estrip[0, ROWS]
    s_b[slot, 0, ROWS] = (estrip[1, ROWS] + ext[2, LEV]) * follows
    extract(place, x_f.at[slot], s_f.at[slot, 0])
    extract(place, x_b.at[slot], s_b.at[slot, 0])

    sweep(place, x_b, s_b, coef, scoef, counts[1])
    cross = jnp.zeros((8, CY), F32)
    square = jnp.zeros((8, CY), F32)

    def dots(r, q):
        return jnp.sum((r * q).reshape(-1, 8, CY), 0), jnp.sum((q * q).reshape(-1, 8, CY), 0)

    for z in range(LEV):
        rl1 = ext[1, z, tile]
        rl1_out[z] = rl1
        b21_out[z] = x_b[end, z + 1, TOP + HALO : TOP + HALO + CX]
    coefficients(place, wind, wstrip, coef, scoef, False)
    sweep(place, x_f, s_f, coef, scoef, counts[1])
    for z in range(LEV):
        f21_out[z] = x_f[end, z + 1, TOP + HALO : TOP + HALO + CX]

    slot = first_slot(counts[0])
    fill_winds(place, 0, we, wn, bg, ag, own, got, by, ay, wind, wstrip)
    coefficients(place, wind, wstrip, coef, scoef, False)
    for z in range(LEV):
        x_f[slot, z + 1, ROWS] = ext[0, z]
        x_b[slot, z + 1, ROWS] = ext[1, z]
    s_f[slot, 0, ROWS] = ext[0, LEV]
    s_b[slot, 0, ROWS] = ext[1, LEV]
    extract(place, x_f.at[slot], s_f.at[slot, 0])
    extract(place, x_b.at[slot], s_b.at[slot, 0])
    sweep(place, x_f, s_f, coef, scoef, counts[0])
    for z in range(LEV):
        rl1 = ext[1, z, tile]
        ql = mv[1, z] * rl1 + rv1_out[z] - x_f[end, z + 1, TOP + HALO : TOP + HALO + CX]
        ql1_out[z] = ql
        c, q = dots(rl1, ql)
        cross, square = cross + c, square + q
    coefficients(place, wind, wstrip, coef, scoef, True)
    sweep(place, x_b, s_b, coef, scoef, counts[0])
    for z in range(LEV):
        b20_out[z] = x_b[end, z + 1, TOP + HALO : TOP + HALO + CX]

    dots_out[0] = cross
    dots_out[1] = square


def dots_kernel(
    even, odd, rl2, f21, b20, z_own, h2, rv0, dots_in, rl1, rv1, b21, ql1, qm, rm, m,
    keep_out, send_out,
):
    follows = jnp.where(lax.axis_index("tm") == lax.axis_size("tm") - 1, 0.0, 1.0)
    starts = jnp.where(lax.axis_index("tm") == 0, 1.0, 0.0)
    for i, kept in enumerate((rm, qm, m)):
        for s in range(2):
            for k in range(m.shape[-1] // CY):
                keep_out[6, 2 * i + s, k : k + 1] = kept[s, 0, :, k * CY : (k + 1) * CY]
    rm_rows, qm_rows = keep_out[6, 0:2, 0:8], keep_out[6, 2:4, 0:8]
    cross = dots_in[0] + jnp.sum(rm_rows * qm_rows, 0)
    square = dots_in[1] + jnp.sum(qm_rows * qm_rows, 0)
    is_odd = lax.axis_index("tm") % 2 == 1

    def total(x):
        return jnp.sum(x.reshape(-1, 8, CY), 0)

    for z in range(LEV):
        rl0 = z_own[64 + 8 * z : 72 + 8 * z].reshape(CX, CY) + jnp.where(is_odd, even[0, z], odd[0, z])
        rv = rv0[0, z]
        qv = rl0 - b20[z] + h2[0, z]
        qv1 = rl1[z] - b21[z] + h2[1, z]
        for i, kept in enumerate((rl0, rl1[z], rv1[z], qv, qv1, ql1[z])):
            keep_out[i, z] = kept
        cross += total(rv1[z] * qv1)
        square += total(qv1 * qv1)
        ql = (rv0[1, z] * rl0 + rv) * starts
        rl2z = rl2[z]
        next_mv = jnp.where(is_odd, odd[1, z], even[1, z])
        next_rv = jnp.where(is_odd, odd[0, z], even[0, z])
        q2 = (next_mv * rl2z + next_rv - f21[z]) * follows
        cross += total(rv * qv) + total(rl0 * ql) + total(rl2z * q2)
        square += total(qv * qv) + total(ql * ql) + total(q2 * q2)
    cross = jnp.sum(jnp.sum(cross, 0, keepdims=True), 1, keepdims=True)
    square = jnp.sum(jnp.sum(square, 0, keepdims=True), 1, keepdims=True)
    n = send_out.shape[0]
    lane = iota((n, CY), 1)
    send_out[...] = jnp.where(lane == 0, cross, jnp.where(lane == 1, square, 0.0))


def last_kernel(
    sums, l, v, rv0, z_f2, keep,
    l_out, m_out, v_out, a_out, b_out, c_out,
):
    total = jnp.sum(sums[...], 0, keepdims=True)
    lane = iota((1, CY), 1)
    cross = jnp.sum(jnp.where(lane == 0, total, 0.0), 1, keepdims=True)
    square = jnp.sum(jnp.where(lane == 1, total, 0.0), 1, keepdims=True)
    alpha = cross / (square + 1e-06)
    for s in range(2):
        for k in range(m_out.shape[-1] // CY):
            rm, qm, m = (keep[6, 2 * i + s, k : k + 1] for i in range(3))
            m_out[s, 0, :, k * CY : (k + 1) * CY] = m + alpha * rm
            b_out[s, 0, :, k * CY : (k + 1) * CY] = rm - alpha * qm
    for z in range(LEV):
        rl0, rl1, rv1, qv0, qv1, ql1 = (keep[i, z] for i in range(6))
        ql0 = rv0[1, z] * rl0 + rv0[0, z] - z_f2[z]
        l_out[0, z] = l[0, z] + alpha * rl0
        l_out[1, z] = l[1, z] + alpha * rl1
        v_out[0, z] = v[0, z] + alpha * rv0[0, z]
        v_out[1, z] = v[1, z] + alpha * rv1
        a_out[0, z] = rl0 - alpha * ql0
        a_out[1, z] = rl1 - alpha * ql1
        c_out[0, z] = rv0[0, z] - alpha * qv0
        c_out[1, z] = rv1 - alpha * qv1


def shards(sizes, l4, m4, v4, f4, d4, mv4, ov4, we4, wn4, cells4, counts):
    ntm, ngx, ngy = sizes
    tile = (LEV, CX, CY)
    obs = m4.shape

    def pair_b(i):
        return i - 1 if i % 2 == 0 else i + 1

    def plane(move_x, move_y):
        pairs = []
        for x in range(ngx):
            for y in range(ngy):
                to = move_x(x)
                if 0 <= to < ngx:
                    pairs.append((x * ngy + y, to * ngy + (1 - y if move_y else y)))
        return pairs

    axes = ("gx", "gy")
    down = [(i + 1, i) for i in range(ntm - 1)]
    up = [(i, i + 1) for i in range(ntm - 1)]
    edge = 10 * LEV

    fields = pltpu.VMEM((2,) + tile, F32)
    b_send, a_send, by_send, strips, z_send = call(
        pack_kernel,
        [(NBLOCKS, 8, CY)] * 2 + [(6, 8, CY), (6, CX, CY), (136, 8, CY)],
        [cells4, m4, l4, f4, mv4, v4, we4, wn4],
        [fields, fields, pltpu.VMEM(obs, jnp.int32), pltpu.VMEM(obs, F32)]
        + [fields] * 6
        + [pltpu.SemaphoreType.DMA((8,))],
        micros=2.5,
        fetched=range(8),
        limit=PACK_LIMIT,
    )
    got = lax.ppermute(strips, axes, plane(lambda i: i, True))
    bg = lax.ppermute(b_send, axes, plane(pair_b, False))
    ag = lax.ppermute(a_send, axes, plane(lambda i: i ^ 1, False))
    zt = lax.ppermute(z_send, "tm", down)
    ay_send = jnp.concatenate([got[:, :8], got[:, CX - 8 :]], 1)
    ay_send, by_send, late_cells = lax.optimization_barrier((ay_send, by_send, cells4))
    by = lax.ppermute(by_send, axes, plane(pair_b, True))
    ay = lax.ppermute(ay_send, axes, plane(lambda i: i ^ 1, False))

    lh, g1, own = call(
        local_kernel,
        [(2,) + tile, tile, strips.shape],
        [late_cells, m4, l4, f4, mv4, v4, strips],
        micros=1.0,
    )
    z_edges = jnp.concatenate(
        [
            bg[2 * LEV : 3 * LEV], bg[8 * LEV : 9 * LEV],
            ag[2 * LEV : 3 * LEV], ag[8 * LEV : 9 * LEV],
            bg[edge + 1 : edge + 2], by[1:2], ag[edge + 1 : edge + 2],
            ay[1].reshape(2, 8, CY), got[1].reshape(8, 8, CY),
        ],
        0,
    )
    zh = lax.ppermute(z_edges, "tm", down)
    scratch = [
        STATE, STATE, STRIP, STRIP, COEF, SCOEF, WIND, WSTRIP,
        pltpu.VMEM((2, LEV, BUF, CY), F32), pltpu.VMEM((2, BUF, CY), F32),
    ]
    ext, rv0, even_send, odd_send = call(
        first_kernel,
        [(3, LEV + 1, EXT, CY)] + [(2,) + tile] * 3,
        [counts, v4, l4, we4, wn4, mv4, lh, g1, own, got, bg, ag, by, ay],
        scratch,
        micros=5.0,
    )
    swap = lambda first: [(i, i + 1) for i in range(first, ntm - 1, 2)] + [
        (i + 1, i) for i in range(first, ntm - 1, 2)
    ]
    even = lax.ppermute(even_send, "tm", swap(0))
    odd = lax.ppermute(odd_send, "tm", swap(1))
    rv1, rl1, rl2, f21, b20, ql1, b21, dots = call(
        second_kernel,
        [tile] * 7 + [(2, 8, CY)],
        [counts, ext, we4, wn4, lh, own, got, bg, ag, by, ay, zt, zh, mv4],
        scratch,
        micros=9.0,
    )
    z_f2 = lax.ppermute(f21, "tm", up)
    rm, qm, h2 = call(
        obs_kernel, [obs, obs, (2,) + tile], [cells4, m4, v4, d4, ov4, rv0, rv1], micros=3.4
    )
    n = ntm * ngx * ngy
    keep, send = call(
        dots_kernel,
        [(7,) + tile, (n, CY)],
        [even, odd, rl2, f21, b20, z_send, h2, rv0, dots, rl1, rv1, b21, ql1, qm, rm, m4],
        micros=0.4,
    )
    sums = lax.all_to_all(send, ("tm", "gx", "gy"), 0, 0, tiled=True)
    return call(
        last_kernel,
        [l4.shape, obs, l4.shape, l4.shape, obs, l4.shape],
        [sums, l4, v4, rv0, z_f2, keep],
        micros=1.5,
    )


def solution(mesh):
    field = P("tm", None, "gx", "gy")
    obs = P("tm", "gx", "gy", None)
    sizes = tuple(mesh.shape[a] for a in ("tm", "gx", "gy"))
    return jax.shard_map(
        functools.partial(shards, sizes),
        mesh=mesh,
        in_specs=(field, obs, field, field, obs, field, obs, field, field, obs, P("tm")),
        out_specs=(field, obs, field, field, obs, field),
        check_vma=False,
    )
```

```python
import functools

import jax
import jax.numpy as jnp
from jax import lax
from jax.experimental import pallas as pl
from jax.experimental.pallas import tpu as pltpu
from jax.sharding import PartitionSpec as P

DIFFUSION = 0.18
VERTICAL = 0.1
CENTRE = 1.0 - 4.0 * DIFFUSION - 2.0 * VERTICAL

LEV, CX, CY = 8, 64, 128
HALO = 8
EXT = CX + 2 * HALO
TOP = 8
BUF = EXT + 2 * TOP
VMEM_LIMIT = 16 * 1024 * 1024
PACK_LIMIT = 60 * 1024 * 1024
NBLOCKS = 10 * LEV + 6
F32 = jnp.float32

VM = pl.BlockSpec(memory_space=pltpu.VMEM)
SM = pl.BlockSpec(memory_space=pltpu.SMEM)
FAR = pl.BlockSpec(memory_space=pltpu.HBM)


def call(body, outs, ins, scratch=(), micros=1.0, fetched=(), written=(), limit=VMEM_LIMIT):
    shapes = [jax.ShapeDtypeStruct(s, F32) for s in outs]
    nbytes = 4 * sum(int(a.size) for a in ins) + 4 * sum(
        functools.reduce(lambda a, b: a * b, s, 1) for s in outs
    )
    in_specs = [SM if (a.dtype == jnp.int32 and a.size < 64) else VM for a in ins]
    for i in fetched:
        in_specs[i] = FAR
    return pl.pallas_call(
        body,
        out_shape=shapes,
        in_specs=in_specs,
        out_specs=[FAR if i in written else VM for i in range(len(shapes))],
        scratch_shapes=list(scratch),
        compiler_params=pltpu.CompilerParams(vmem_limit_bytes=limit),
        cost_estimate=pl.CostEstimate(
            flops=int(1.1e9 * micros), bytes_accessed=nbytes, transcendentals=0
        ),
    )(*ins)


def iota(shape, dim):
    return lax.broadcasted_iota(jnp.int32, shape, dim)


def split(x):
    high = x.astype(jnp.bfloat16)
    low = (x - high.astype(F32)).astype(jnp.bfloat16)
    return high, low


def one_hots(cells):
    n = cells.shape[1]
    rows = (iota((LEV * CX, n), 0) == (cells >> 7)).astype(jnp.bfloat16)
    lanes = iota((CY, n), 0) == (cells & 127)
    return rows, lanes


def scatter(rows, lanes, values):
    high, low = split(values)
    zero = jnp.zeros((), jnp.bfloat16)
    parts = jnp.concatenate(
        [jnp.where(lanes, high.astype(F32), 0.0), jnp.where(lanes, low.astype(F32), 0.0)], 0
    ).astype(jnp.bfloat16)
    both = lax.dot_general(
        rows, parts, (((1,), (1,)), ((), ())), preferred_element_type=F32
    )
    return both[:, :CY] + both[:, CY:]


def gather(rows, lanes, field):
    high, low = split(field)
    both = lax.dot_general(
        jnp.concatenate([high, low], 1), rows, (((0,), (0,)), ((), ())),
        preferred_element_type=F32,
    )
    picked = both[:CY] + both[CY:]
    return jnp.sum(jnp.where(lanes, picked, 0.0), 0, keepdims=True)


def swap_halves(x):
    inner = (iota(x.shape, x.ndim - 1) & 15) < 8
    axis = x.ndim - 1
    return jnp.where(inner, pltpu.roll(x, CY - 8, axis), pltpu.roll(x, 8, axis))


def own_half(shape, gy):
    lane = iota(shape, len(shape) - 1) & 15
    return jnp.where(gy == 0, lane, lane ^ 8) < 8


def pack_kernel(
    cells_h, m_h, v_h, we_h, wn_h, l_h, f_h, mv_h,
    b_out, a_out, by_out, strip_out, z_out,
    lh_out, g_s, cells, m, v, we, wn, l, f, mv, sems,
):
    far = (cells_h, m_h, v_h, we_h, wn_h, l_h, f_h, mv_h)
    near = (cells, m, v, we, wn, l, f, mv)
    copies = [pltpu.make_async_copy(a, b, sems.at[i]) for i, (a, b) in enumerate(zip(far, near))]
    for copy in copies:
        copy.start()
    core = lax.axis_index("gx") % 2
    gy = lax.axis_index("gy")
    lane = iota((CX, CY), 1)

    def own(get):
        packed = jnp.zeros((CX, CY), F32)
        for z in range(LEV):
            rolled = pltpu.roll(get(z), (16 * z + 8) % CY, 1)
            packed = jnp.where((lane >> 4) == z, rolled, packed)
        return packed

    half = own_half((CX, CY), gy)

    def pack_strips(p, one, two):
        first = own(lambda z: one[0][one[1], z])
        second = own(lambda z: two[0][two[1], z])
        strip_out[p] = jnp.where(half, first, swap_halves(second))

    copies[0].wait()
    copies[1].wait()
    for s in range(2):
        rows, lanes = one_hots(cells[s, 0])
        lh_out[s] = scatter(rows, lanes, m[s, 0]).reshape(LEV, CX, CY)
    copies[2].wait()
    pack_strips(0, (v, 0), (v, 1))
    copies[3].wait()
    copies[4].wait()
    pack_strips(4, (we, 0), (wn, 0))
    pack_strips(5, (we, 1), (wn, 1))
    for copy in copies[5:]:
        copy.wait()
    for s in range(2):
        lh_out[s] += l[s]
        g_s[s] = f[s] - mv[s] * l[s] - v[s]
    for z in range(LEV):
        for i in range(CX // 8):
            z_out[z * 8 + i] = l[0, z, 8 * i : 8 * i + 8]
            z_out[64 + z * 8 + i] = g_s[0, z, 8 * i : 8 * i + 8]
    pack_strips(1, (l, 0), (g_s, 0))
    pack_strips(2, (l, 1), (g_s, 1))
    pack_strips(3, (lh_out, 0), (lh_out, 1))
    for i in range(CX // 8):
        z_out[128 + i] = strip_out[1, 8 * i : 8 * i + 8]

    sub = iota((8, CY), 0)
    for out, top in ((b_out, core == 0), (a_out, core != 0)):
        row = jnp.where(top, 0, CX - 8)
        row = pl.multiple_of(row, 8)
        edge = pl.ds(row, 8)
        for k, field in enumerate((v, l, we, wn)):
            for s in range(2):
                out[pl.ds((2 * k + s) * LEV, LEV)] = field[s, :, edge, :]
        keep = jnp.where(top, sub, 7 - sub) < 4
        for s in range(2):
            for z in range(LEV):
                lh_edge = lh_out[s, z, edge, :]
                g_edge = pltpu.roll(g_s[s, z, edge, :], 4, 0)
                out[(8 + s) * LEV + z] = jnp.where(keep, lh_edge, g_edge)
        out[pl.ds(10 * LEV, 6)] = strip_out[:, edge, :]
    by_out[...] = b_out[10 * LEV :]


def local_kernel(cells, m, l, f, mv, v, strips, lh_out, g1_out, own_out):
    for s in range(2):
        rows, lanes = one_hots(cells[s, 0])
        lh_out[s] = l[s] + scatter(rows, lanes, m[s, 0]).reshape(LEV, CX, CY)
    g1_out[...] = f[1] - mv[1] * l[1] - v[1]
    own_out[...] = strips[...]


def obs_kernel(cells, m, v, dep, ov, rv0, rv1, rm_out, qm_out, h2_out):
    for s in range(2):
        rows, lanes = one_hots(cells[s, 0])
        seen = gather(rows, lanes, v[s].reshape(LEV * CX, CY))
        rm = dep[s, 0] - (ov[s, 0] * m[s, 0] + seen)
        rm_out[s, 0] = rm
        h2_out[s] = scatter(rows, lanes, rm).reshape(LEV, CX, CY)
        rv = rv0[0] if s == 0 else rv1[...]
        qm_out[s, 0] = ov[s, 0] * rm + gather(rows, lanes, rv.reshape(LEV * CX, CY))


class Place:
    def __init__(self):
        gx = lax.axis_index("gx")
        self.gy = lax.axis_index("gy")
        core = gx % 2
        self.b_row = pl.multiple_of(jnp.where(core == 0, TOP, TOP + HALO + CX), 8)
        self.a_row = pl.multiple_of(jnp.where(core == 0, TOP + HALO + CX, TOP), 8)
        self.core = core
        self.ay_rows = pl.ds(pl.multiple_of(core * 8, 8), 8)
        self.low = jnp.where(gx == 0, 0.0, 1.0)
        self.high = jnp.where(gx == lax.axis_size("gx") - 1, 0.0, 1.0)


def clear(ref, guard_levels):
    lead = ref.shape[:-2]
    zero = jnp.zeros(lead + (TOP, CY), F32)
    ref[..., 0:TOP, :] = zero
    ref[..., BUF - TOP : BUF, :] = zero
    if guard_levels:
        full = jnp.zeros((BUF, CY), F32)
        for i in range(lead[0]):
            ref[i, 0] = full
            ref[i, LEV + 1] = full


def fill(dst, base, place, tile, b_block, a_block):
    for z in range(LEV):
        dst[base + z, TOP + HALO : TOP + HALO + CX] = tile(z)
        dst[base + z, pl.ds(place.b_row, 8)] = b_block(z)
        dst[base + z, pl.ds(place.a_row, 8)] = a_block(z)


def unpack(place, own, received):
    half = own_half(own.shape, place.gy)
    return jnp.where(half, own, received), swap_halves(jnp.where(half, received, own))


def fill_strips(first, second, place, own, got, own_b, got_b, own_a, got_a):
    mid = pl.ds(TOP + HALO, CX)
    for where, a, b in (
        (mid, own, got),
        (pl.ds(place.b_row, 8), own_b, got_b),
        (pl.ds(place.a_row, 8), own_a, got_a),
    ):
        one, two = unpack(place, a, b)
        first[where] = one
        second[where] = two


ROWS = slice(TOP, TOP + EXT)
UP = slice(TOP + 1, TOP + EXT + 1)
DOWN = slice(TOP - 1, TOP + EXT - 1)


def inject(place, state, strip):
    lane = iota((EXT, CY), 1)
    edge = jnp.where(place.gy == 0, lane, CY - 1 - lane) >= CY - 4
    for z in range(LEV):
        moved = pltpu.roll(strip[ROWS], (120 - 16 * z) % CY, 1)
        state[z + 1, ROWS] = jnp.where(edge, moved, state[z + 1, ROWS])


def extract(place, state, strip):
    lane = iota((EXT, CY), 1)
    half = own_half((EXT, CY), place.gy)
    group = jnp.where(half, lane >> 4, LEV)
    packed = strip[ROWS]
    for z in range(LEV):
        packed = jnp.where(
            group == z, pltpu.roll(state[z + 1, ROWS], (16 * z + 8) % CY, 1), packed
        )
    strip[ROWS] = packed


def coefficients(place, wind, strip, coef, scoef, adjoint):
    lane = iota((EXT, CY), 1)
    if not adjoint:
        for z in range(LEV):
            east, north = 0.5 * wind[0, z, ROWS], 0.5 * wind[1, z, ROWS]
            coef[0, z] = DIFFUSION - east
            coef[1, z] = DIFFUSION + east
            coef[2, z] = jnp.where(lane == CY - 1, 0.0, DIFFUSION - north)
            coef[3, z] = jnp.where(lane == 0, 0.0, DIFFUSION + north)
        east, north = 0.5 * strip[0, ROWS], 0.5 * strip[1, ROWS]
        scoef[0] = DIFFUSION - east
        scoef[1] = DIFFUSION + east
        scoef[2] = DIFFUSION - north
        scoef[3] = DIFFUSION + north
        return
    for z in range(LEV):
        north = wind[1, z, ROWS]
        after = pltpu.roll(north, CY - 1, 1)
        before = pltpu.roll(north, 1, 1)
        coef[0, z] = DIFFUSION + 0.5 * wind[0, z, UP]
        coef[1, z] = DIFFUSION - 0.5 * wind[0, z, DOWN]
        coef[2, z] = jnp.where(lane == CY - 1, 0.0, DIFFUSION + 0.5 * after)
        coef[3, z] = jnp.where(lane == 0, 0.0, DIFFUSION - 0.5 * before)
    scoef[0] = DIFFUSION + 0.5 * strip[0, UP]
    scoef[1] = DIFFUSION - 0.5 * strip[0, DOWN]
    scoef[2] = DIFFUSION + 0.5 * pltpu.roll(strip[1, ROWS], CY - 1, 1)
    scoef[3] = DIFFUSION - 0.5 * pltpu.roll(strip[1, ROWS], 1, 1)


def store(dst, z, out, place):
    dst[z, TOP : TOP + HALO] = out[:HALO] * place.low
    dst[z, TOP + HALO : TOP + HALO + CX] = out[HALO : HALO + CX]
    dst[z, TOP + HALO + CX : TOP + EXT] = out[HALO + CX :] * place.high


def first_slot(count):
    return count & 1


def one_step(place, src, dst, ssrc, sdst, coef, scoef):
    lane = iota((EXT, CY), 1)
    own = ssrc[ROWS]
    for z in range(LEV):
        mid = src[z + 1, ROWS]
        after = pltpu.roll(mid, CY - 1, 1)
        before = pltpu.roll(mid, 1, 1)
        out = (
            CENTRE * mid
            + coef[0, z] * src[z + 1, UP]
            + coef[1, z] * src[z + 1, DOWN]
            + coef[2, z] * after
            + coef[3, z] * before
            + VERTICAL * (src[z + 2, ROWS] + src[z, ROWS])
        )
        store(dst, z + 1, out, place)
    above = jnp.where(lane < CY - 16, pltpu.roll(own, CY - 16, 1), 0.0)
    below = jnp.where(lane >= 16, pltpu.roll(own, 16, 1), 0.0)
    out = (
        CENTRE * own
        + scoef[0] * ssrc[UP]
        + scoef[1] * ssrc[DOWN]
        + scoef[2] * pltpu.roll(own, CY - 1, 1)
        + scoef[3] * pltpu.roll(own, 1, 1)
        + VERTICAL * (above + below)
    )
    sdst[TOP : TOP + HALO] = out[:HALO] * place.low
    sdst[TOP + HALO : TOP + HALO + CX] = out[HALO : HALO + CX]
    sdst[TOP + HALO + CX : TOP + EXT] = out[HALO + CX :] * place.high


def sweep(place, state, strip, coef, scoef, count):
    def two(i, _):
        for j in range(2):

            @pl.when(2 * i + j >= 4 - count)
            def _():
                one_step(
                    place, state.at[j], state.at[1 - j], strip.at[j, 0], strip.at[1 - j, 0],
                    coef, scoef,
                )

        return 0

    lax.fori_loop(0, 2, two, 0)
    inject(place, state.at[0], strip.at[0, 0])


STATE = pltpu.VMEM((2, LEV + 2, BUF, CY), F32)
STRIP = pltpu.VMEM((2, 1, BUF, CY), F32)
COEF = pltpu.VMEM((4, LEV, EXT, CY), F32)
SCOEF = pltpu.VMEM((4, EXT, CY), F32)
WIND = pltpu.VMEM((2, LEV, BUF, CY), F32)
WSTRIP = pltpu.VMEM((2, BUF, CY), F32)


def fill_winds(place, s, we, wn, bg, ag, own, got, by, ay, wind, wstrip):
    for k, field in enumerate((we, wn)):
        fill(
            wind.at[k], 0, place, lambda z, field=field: field[s, z],
            lambda z, k=k: bg[(4 + 2 * k + s) * LEV + z],
            lambda z, k=k: ag[(4 + 2 * k + s) * LEV + z],
        )
    p = 4 + s
    fill_strips(
        wstrip.at[0], wstrip.at[1], place, own[p], got[p],
        bg[10 * LEV + p], by[p], ag[10 * LEV + p], ay[p, place.ay_rows],
    )


def first_kernel(
    counts, v, l, we, wn, mv, lh, g1, own, got, bg, ag, by, ay,
    ext_out, rv_out, even_out, odd_out,
    x_f, x_b, s_f, s_b, coef, scoef, wind, wstrip, extra, estrip,
):
    place = Place()
    clear(x_f, True)
    clear(x_b, True)
    for ref in (s_f, s_b, wind, wstrip, extra, estrip):
        clear(ref, False)

    def strips(p, first, second):
        fill_strips(
            first, second, place, own[p], got[p],
            bg[10 * LEV + p], by[p], ag[10 * LEV + p], ay[p, place.ay_rows],
        )

    fill_winds(place, 0, we, wn, bg, ag, own, got, by, ay, wind, wstrip)
    fill(
        x_b.at[first_slot(counts[0])], 1, place, lambda z: l[1, z],
        lambda z: bg[3 * LEV + z], lambda z: ag[3 * LEV + z],
    )
    strips(2, s_b.at[first_slot(counts[0]), 0], estrip.at[1])
    coefficients(place, wind, wstrip, coef, scoef, True)
    sweep(place, x_b, s_b, coef, scoef, counts[0])
    end = 0
    fill(
        extra.at[0], 0, place, lambda z: lh[0, z],
        lambda z: bg[8 * LEV + z], lambda z: ag[8 * LEV + z],
    )
    fill(
        extra.at[1], 0, place, lambda z: g1[z],
        lambda z: pltpu.roll(bg[9 * LEV + z], 4, 0),
        lambda z: pltpu.roll(ag[9 * LEV + z], 4, 0),
    )
    for z in range(LEV):
        rv = x_b[end, z + 1, ROWS] - extra[0, z, ROWS]
        ext_out[0, z] = rv
        rv_out[0, z] = rv[HALO : HALO + CX]
        rv_out[1, z] = mv[0, z]
    strips(3, estrip.at[0], s_f.at[0, 0])
    ext_out[0, LEV] = s_b[end, 0, ROWS] - estrip[0, ROWS]

    for s in range(2):
        if s == 1:
            fill_winds(place, 1, we, wn, bg, ag, own, got, by, ay, wind, wstrip)
        coefficients(place, wind, wstrip, coef, scoef, False)
        fill(
            x_f.at[first_slot(counts[s])], 1, place, lambda z, s=s: v[s, z],
            lambda z, s=s: bg[s * LEV + z], lambda z, s=s: ag[s * LEV + z],
        )
        if s == 0:
            strips(0, s_f.at[first_slot(counts[s]), 0], estrip.at[0])
        else:
            strips(0, estrip.at[0], s_f.at[first_slot(counts[s]), 0])
        sweep(place, x_f, s_f, coef, scoef, counts[s])
        for z in range(LEV):
            out = x_f[end, z + 1, ROWS]
            if s == 0:
                ext_out[1, z] = out + extra[1, z, ROWS]
            else:
                ext_out[2, z] = out
        out = s_f[end, 0, ROWS]
        ext_out[1 + s, LEV] = out + estrip[1, ROWS] if s == 0 else out

    tile = slice(HALO, HALO + CX)
    odd = lax.axis_index("tm") % 2

    @pl.when(odd == 0)
    def _():
        even_out[0] = ext_out[2, :LEV, tile]
        even_out[1] = rv_out[1]
        odd_out[...] = rv_out[...]

    @pl.when(odd == 1)
    def _():
        even_out[...] = rv_out[...]
        odd_out[0] = ext_out[2, :LEV, tile]
        odd_out[1] = rv_out[1]


def lane_sum(x):
    return functools.reduce(
        lambda a, b: a + b, [x[:, i : i + CY] for i in range(0, x.shape[1], CY)]
    )


def second_kernel(
    counts, ext, we, wn, lh, own, got, bg, ag, by, ay, zt, zh,
    mv,
    rv1_out, rl1_out, rl2_out, f21_out, b20_out, ql1_out, b21_out, dots_out,
    x_f, x_b, s_f, s_b, coef, scoef, wind, wstrip, extra, estrip,
):
    place = Place()
    clear(x_f, True)
    clear(x_b, True)
    for ref in (s_f, s_b, wind, wstrip, extra, estrip):
        clear(ref, False)
    tile = slice(HALO, HALO + CX)
    follows = jnp.where(lax.axis_index("tm") == lax.axis_size("tm") - 1, 0.0, 1.0)

    fill_winds(place, 1, we, wn, bg, ag, own, got, by, ay, wind, wstrip)
    coefficients(place, wind, wstrip, coef, scoef, True)

    def z_tile(base):
        return lambda z: zt[base + 8 * z : base + 8 * z + 8].reshape(CX, CY)

    fill(x_b.at[first_slot(counts[1])], 1, place, z_tile(0), lambda z: zh[z], lambda z: zh[16 + z])
    fill(
        extra.at[1], 0, place, z_tile(64),
        lambda z: pltpu.roll(zh[8 + z], 4, 0), lambda z: pltpu.roll(zh[24 + z], 4, 0),
    )
    fill_strips(
        s_b.at[first_slot(counts[1]), 0], estrip.at[1], place,
        zt[128:136].reshape(CX, CY), zh[37:45].reshape(CX, CY),
        zh[32], zh[33], zh[34], zh[35 + place.core],
    )
    sweep(place, x_b, s_b, coef, scoef, counts[1])
    end = 0
    slot = first_slot(counts[1])

    fill(
        extra.at[0], 0, place, lambda z: lh[1, z],
        lambda z: bg[9 * LEV + z], lambda z: ag[9 * LEV + z],
    )
    fill_strips(
        s_f.at[0, 0], estrip.at[0], place, own[3], got[3],
        bg[10 * LEV + 3], by[3], ag[10 * LEV + 3], ay[3, place.ay_rows],
    )
    for z in range(LEV):
        rv = x_b[end, z + 1, ROWS] - extra[0, z, ROWS]
        x_f[slot, z + 1, ROWS] = rv
        rv1_out[z] = rv[tile]
        rl = (extra[1, z, ROWS] + ext[2, z]) * follows
        x_b[slot, z + 1, ROWS] = rl
        rl2_out[z] = rl[tile]
    s_f[slot, 0, ROWS] = s_b[end, 0, ROWS] - estrip[0, ROWS]
    s_b[slot, 0, ROWS] = (estrip[1, ROWS] + ext[2, LEV]) * follows
    extract(place, x_f.at[slot], s_f.at[slot, 0])
    extract(place, x_b.at[slot], s_b.at[slot, 0])

    sweep(place, x_b, s_b, coef, scoef, counts[1])
    cross = jnp.zeros((8, CY), F32)
    square = jnp.zeros((8, CY), F32)

    def dots(r, q):
        return jnp.sum((r * q).reshape(-1, 8, CY), 0), jnp.sum((q * q).reshape(-1, 8, CY), 0)

    for z in range(LEV):
        rl1 = ext[1, z, tile]
        rl1_out[z] = rl1
        b21_out[z] = x_b[end, z + 1, TOP + HALO : TOP + HALO + CX]
    coefficients(place, wind, wstrip, coef, scoef, False)
    sweep(place, x_f, s_f, coef, scoef, counts[1])
    for z in range(LEV):
        f21_out[z] = x_f[end, z + 1, TOP + HALO : TOP + HALO + CX]

    slot = first_slot(counts[0])
    fill_winds(place, 0, we, wn, bg, ag, own, got, by, ay, wind, wstrip)
    coefficients(place, wind, wstrip, coef, scoef, False)
    for z in range(LEV):
        x_f[slot, z + 1, ROWS] = ext[0, z]
        x_b[slot, z + 1, ROWS] = ext[1, z]
    s_f[slot, 0, ROWS] = ext[0, LEV]
    s_b[slot, 0, ROWS] = ext[1, LEV]
    extract(place, x_f.at[slot], s_f.at[slot, 0])
    extract(place, x_b.at[slot], s_b.at[slot, 0])
    sweep(place, x_f, s_f, coef, scoef, counts[0])
    for z in range(LEV):
        rl1 = ext[1, z, tile]
        ql = mv[1, z] * rl1 + rv1_out[z] - x_f[end, z + 1, TOP + HALO : TOP + HALO + CX]
        ql1_out[z] = ql
        c, q = dots(rl1, ql)
        cross, square = cross + c, square + q
    coefficients(place, wind, wstrip, coef, scoef, True)
    sweep(place, x_b, s_b, coef, scoef, counts[0])
    for z in range(LEV):
        b20_out[z] = x_b[end, z + 1, TOP + HALO : TOP + HALO + CX]

    dots_out[0] = cross
    dots_out[1] = square


def dots_kernel(
    even, odd, rl2, f21, b20, z_own, h2, rv0, dots_in, rl1, rv1, b21, ql1, qm, rm, m,
    keep_out, send_out,
):
    follows = jnp.where(lax.axis_index("tm") == lax.axis_size("tm") - 1, 0.0, 1.0)
    starts = jnp.where(lax.axis_index("tm") == 0, 1.0, 0.0)
    for i, kept in enumerate((rm, qm, m)):
        for s in range(2):
            for k in range(m.shape[-1] // CY):
                keep_out[6, 2 * i + s, k : k + 1] = kept[s, 0, :, k * CY : (k + 1) * CY]
    rm_rows, qm_rows = keep_out[6, 0:2, 0:8], keep_out[6, 2:4, 0:8]
    cross = dots_in[0] + jnp.sum(rm_rows * qm_rows, 0)
    square = dots_in[1] + jnp.sum(qm_rows * qm_rows, 0)
    is_odd = lax.axis_index("tm") % 2 == 1

    def total(x):
        return jnp.sum(x.reshape(-1, 8, CY), 0)

    for z in range(LEV):
        rl0 = z_own[64 + 8 * z : 72 + 8 * z].reshape(CX, CY) + jnp.where(is_odd, even[0, z], odd[0, z])
        rv = rv0[0, z]
        qv = rl0 - b20[z] + h2[0, z]
        qv1 = rl1[z] - b21[z] + h2[1, z]
        for i, kept in enumerate((rl0, rl1[z], rv1[z], qv, qv1, ql1[z])):
            keep_out[i, z] = kept
        cross += total(rv1[z] * qv1)
        square += total(qv1 * qv1)
        ql = (rv0[1, z] * rl0 + rv) * starts
        rl2z = rl2[z]
        next_mv = jnp.where(is_odd, odd[1, z], even[1, z])
        next_rv = jnp.where(is_odd, odd[0, z], even[0, z])
        q2 = (next_mv * rl2z + next_rv - f21[z]) * follows
        cross += total(rv * qv) + total(rl0 * ql) + total(rl2z * q2)
        square += total(qv * qv) + total(ql * ql) + total(q2 * q2)
    cross = jnp.sum(jnp.sum(cross, 0, keepdims=True), 1, keepdims=True)
    square = jnp.sum(jnp.sum(square, 0, keepdims=True), 1, keepdims=True)
    n = send_out.shape[0]
    lane = iota((n, CY), 1)
    send_out[...] = jnp.where(lane == 0, cross, jnp.where(lane == 1, square, 0.0))


def last_kernel(
    sums, l, v, rv0, z_f2, keep,
    l_out, m_out, v_out, a_out, b_out, c_out,
):
    total = jnp.sum(sums[...], 0, keepdims=True)
    lane = iota((1, CY), 1)
    cross = jnp.sum(jnp.where(lane == 0, total, 0.0), 1, keepdims=True)
    square = jnp.sum(jnp.where(lane == 1, total, 0.0), 1, keepdims=True)
    alpha = cross / (square + 1e-06)
    for s in range(2):
        for k in range(m_out.shape[-1] // CY):
            rm, qm, m = (keep[6, 2 * i + s, k : k + 1] for i in range(3))
            m_out[s, 0, :, k * CY : (k + 1) * CY] = m + alpha * rm
            b_out[s, 0, :, k * CY : (k + 1) * CY] = rm - alpha * qm
    for z in range(LEV):
        rl0, rl1, rv1, qv0, qv1, ql1 = (keep[i, z] for i in range(6))
        ql0 = rv0[1, z] * rl0 + rv0[0, z] - z_f2[z]
        l_out[0, z] = l[0, z] + alpha * rl0
        l_out[1, z] = l[1, z] + alpha * rl1
        v_out[0, z] = v[0, z] + alpha * rv0[0, z]
        v_out[1, z] = v[1, z] + alpha * rv1
        a_out[0, z] = rl0 - alpha * ql0
        a_out[1, z] = rl1 - alpha * ql1
        c_out[0, z] = rv0[0, z] - alpha * qv0
        c_out[1, z] = rv1 - alpha * qv1


def shards(sizes, l4, m4, v4, f4, d4, mv4, ov4, we4, wn4, cells4, counts):
    ntm, ngx, ngy = sizes
    tile = (LEV, CX, CY)
    obs = m4.shape

    def pair_b(i):
        return i - 1 if i % 2 == 0 else i + 1

    def plane(move_x, move_y):
        pairs = []
        for x in range(ngx):
            for y in range(ngy):
                to = move_x(x)
                if 0 <= to < ngx:
                    pairs.append((x * ngy + y, to * ngy + (1 - y if move_y else y)))
        return pairs

    axes = ("gx", "gy")
    down = [(i + 1, i) for i in range(ntm - 1)]
    up = [(i, i + 1) for i in range(ntm - 1)]
    edge = 10 * LEV

    fields = pltpu.VMEM((2,) + tile, F32)
    b_send, a_send, by_send, strips, z_send = call(
        pack_kernel,
        [(NBLOCKS, 8, CY)] * 2 + [(6, 8, CY), (6, CX, CY), (136, 8, CY)],
        [cells4, m4, v4, we4, wn4, l4, f4, mv4],
        [fields, fields, pltpu.VMEM(obs, jnp.int32), pltpu.VMEM(obs, F32)]
        + [fields] * 6
        + [pltpu.SemaphoreType.DMA((8,))],
        micros=2.5,
        fetched=range(8),
        limit=PACK_LIMIT,
    )
    got = lax.ppermute(strips, axes, plane(lambda i: i, True))
    bg = lax.ppermute(b_send, axes, plane(pair_b, False))
    ag = lax.ppermute(a_send, axes, plane(lambda i: i ^ 1, False))
    zt = lax.ppermute(z_send, "tm", down)
    ay_send = jnp.concatenate([got[:, :8], got[:, CX - 8 :]], 1)
    ay_send, by_send, late_cells = lax.optimization_barrier((ay_send, by_send, cells4))
    by = lax.ppermute(by_send, axes, plane(pair_b, True))
    ay = lax.ppermute(ay_send, axes, plane(lambda i: i ^ 1, False))

    lh, g1, own = call(
        local_kernel,
        [(2,) + tile, tile, strips.shape],
        [late_cells, m4, l4, f4, mv4, v4, strips],
        micros=1.0,
    )
    z_edges = jnp.concatenate(
        [
            bg[2 * LEV : 3 * LEV], bg[8 * LEV : 9 * LEV],
            ag[2 * LEV : 3 * LEV], ag[8 * LEV : 9 * LEV],
            bg[edge + 1 : edge + 2], by[1:2], ag[edge + 1 : edge + 2],
            ay[1].reshape(2, 8, CY), got[1].reshape(8, 8, CY),
        ],
        0,
    )
    zh = lax.ppermute(z_edges, "tm", down)
    scratch = [
        STATE, STATE, STRIP, STRIP, COEF, SCOEF, WIND, WSTRIP,
        pltpu.VMEM((2, LEV, BUF, CY), F32), pltpu.VMEM((2, BUF, CY), F32),
    ]
    ext, rv0, even_send, odd_send = call(
        first_kernel,
        [(3, LEV + 1, EXT, CY)] + [(2,) + tile] * 3,
        [counts, v4, l4, we4, wn4, mv4, lh, g1, own, got, bg, ag, by, ay],
        scratch,
        micros=5.0,
    )
    swap = lambda first: [(i, i + 1) for i in range(first, ntm - 1, 2)] + [
        (i + 1, i) for i in range(first, ntm - 1, 2)
    ]
    even = lax.ppermute(even_send, "tm", swap(0))
    odd = lax.ppermute(odd_send, "tm", swap(1))
    rv1, rl1, rl2, f21, b20, ql1, b21, dots = call(
        second_kernel,
        [tile] * 7 + [(2, 8, CY)],
        [counts, ext, we4, wn4, lh, own, got, bg, ag, by, ay, zt, zh, mv4],
        scratch,
        micros=9.0,
    )
    z_f2 = lax.ppermute(f21, "tm", up)
    rm, qm, h2 = call(
        obs_kernel, [obs, obs, (2,) + tile], [cells4, m4, v4, d4, ov4, rv0, rv1], micros=3.4
    )
    n = ntm * ngx * ngy
    keep, send = call(
        dots_kernel,
        [(7,) + tile, (n, CY)],
        [even, odd, rl2, f21, b20, z_send, h2, rv0, dots, rl1, rv1, b21, ql1, qm, rm, m4],
        micros=0.4,
    )
    sums = lax.all_to_all(send, ("tm", "gx", "gy"), 0, 0, tiled=True)
    return call(
        last_kernel,
        [l4.shape, obs, l4.shape, l4.shape, obs, l4.shape],
        [sums, l4, v4, rv0, z_f2, keep],
        micros=1.5,
    )


def solution(mesh):
    field = P("tm", None, "gx", "gy")
    obs = P("tm", "gx", "gy", None)
    sizes = tuple(mesh.shape[a] for a in ("tm", "gx", "gy"))
    return jax.shard_map(
        functools.partial(shards, sizes),
        mesh=mesh,
        in_specs=(field, obs, field, field, obs, field, obs, field, field, obs, P("tm")),
        out_specs=(field, obs, field, field, obs, field),
        check_vma=False,
    )
```

```python
import functools

import jax
import jax.numpy as jnp
from jax import lax
from jax.experimental import pallas as pl
from jax.experimental.pallas import tpu as pltpu
from jax.sharding import PartitionSpec as P

DIFFUSION = 0.18
VERTICAL = 0.1
CENTRE = 1.0 - 4.0 * DIFFUSION - 2.0 * VERTICAL

LEV, CX, CY = 8, 64, 128
HALO = 8
EXT = CX + 2 * HALO
TOP = 8
BUF = EXT + 2 * TOP
VMEM_LIMIT = 16 * 1024 * 1024
PACK_LIMIT = 60 * 1024 * 1024
NBLOCKS = 10 * LEV + 6
F32 = jnp.float32

VM = pl.BlockSpec(memory_space=pltpu.VMEM)
SM = pl.BlockSpec(memory_space=pltpu.SMEM)
FAR = pl.BlockSpec(memory_space=pltpu.HBM)


def call(body, outs, ins, scratch=(), micros=1.0, fetched=(), written=(), limit=VMEM_LIMIT):
    shapes = [jax.ShapeDtypeStruct(s, F32) for s in outs]
    nbytes = 4 * sum(int(a.size) for a in ins) + 4 * sum(
        functools.reduce(lambda a, b: a * b, s, 1) for s in outs
    )
    in_specs = [SM if (a.dtype == jnp.int32 and a.size < 64) else VM for a in ins]
    for i in fetched:
        in_specs[i] = FAR
    return pl.pallas_call(
        body,
        out_shape=shapes,
        in_specs=in_specs,
        out_specs=[FAR if i in written else VM for i in range(len(shapes))],
        scratch_shapes=list(scratch),
        compiler_params=pltpu.CompilerParams(vmem_limit_bytes=limit),
        cost_estimate=pl.CostEstimate(
            flops=int(1.1e9 * micros), bytes_accessed=nbytes, transcendentals=0
        ),
    )(*ins)


def iota(shape, dim):
    return lax.broadcasted_iota(jnp.int32, shape, dim)


def split(x):
    high = x.astype(jnp.bfloat16)
    low = (x - high.astype(F32)).astype(jnp.bfloat16)
    return high, low


def one_hots(cells):
    n = cells.shape[1]
    rows = (iota((LEV * CX, n), 0) == (cells >> 7)).astype(jnp.bfloat16)
    lanes = iota((CY, n), 0) == (cells & 127)
    return rows, lanes


def scatter(rows, lanes, values):
    high, low = split(values)
    zero = jnp.zeros((), jnp.bfloat16)
    parts = jnp.concatenate(
        [jnp.where(lanes, high.astype(F32), 0.0), jnp.where(lanes, low.astype(F32), 0.0)], 0
    ).astype(jnp.bfloat16)
    both = lax.dot_general(
        rows, parts, (((1,), (1,)), ((), ())), preferred_element_type=F32
    )
    return both[:, :CY] + both[:, CY:]


def gather(rows, lanes, field):
    high, low = split(field)
    both = lax.dot_general(
        jnp.concatenate([high, low], 1), rows, (((0,), (0,)), ((), ())),
        preferred_element_type=F32,
    )
    picked = both[:CY] + both[CY:]
    return jnp.sum(jnp.where(lanes, picked, 0.0), 0, keepdims=True)


def swap_halves(x):
    inner = (iota(x.shape, x.ndim - 1) & 15) < 8
    axis = x.ndim - 1
    return jnp.where(inner, pltpu.roll(x, CY - 8, axis), pltpu.roll(x, 8, axis))


def own_half(shape, gy):
    lane = iota(shape, len(shape) - 1) & 15
    return jnp.where(gy == 0, lane, lane ^ 8) < 8


def pack_kernel(
    cells_h, m_h, v_h, we_h, wn_h, l_h, f_h, mv_h,
    b_out, a_out, by_out, strip_out, z_out,
    lh_out, g_s, cells, m, v, we, wn, l, f, mv, sems,
):
    far = (cells_h, m_h, v_h, we_h, wn_h, l_h, f_h, mv_h)
    near = (cells, m, v, we, wn, l, f, mv)
    copies = [pltpu.make_async_copy(a, b, sems.at[i]) for i, (a, b) in enumerate(zip(far, near))]
    for copy in copies:
        copy.start()
    core = lax.axis_index("gx") % 2
    gy = lax.axis_index("gy")
    lane = iota((CX, CY), 1)

    def own(get):
        packed = jnp.zeros((CX, CY), F32)
        for z in range(LEV):
            rolled = pltpu.roll(get(z), (16 * z + 8) % CY, 1)
            packed = jnp.where((lane >> 4) == z, rolled, packed)
        return packed

    half = own_half((CX, CY), gy)

    def pack_strips(p, one, two):
        first = own(lambda z: one[0][one[1], z])
        second = own(lambda z: two[0][two[1], z])
        strip_out[p] = jnp.where(half, first, swap_halves(second))

    copies[0].wait()
    copies[1].wait()
    for s in range(2):
        rows, lanes = one_hots(cells[s, 0])
        lh_out[s] = scatter(rows, lanes, m[s, 0]).reshape(LEV, CX, CY)
    copies[2].wait()
    pack_strips(0, (v, 0), (v, 1))
    copies[3].wait()
    copies[4].wait()
    pack_strips(4, (we, 0), (wn, 0))
    pack_strips(5, (we, 1), (wn, 1))
    for copy in copies[5:]:
        copy.wait()
    for s in range(2):
        lh_out[s] += l[s]
        g_s[s] = f[s] - mv[s] * l[s] - v[s]
    for z in range(LEV):
        for i in range(CX // 8):
            z_out[z * 8 + i] = l[0, z, 8 * i : 8 * i + 8]
            z_out[64 + z * 8 + i] = g_s[0, z, 8 * i : 8 * i + 8]
    pack_strips(1, (l, 0), (g_s, 0))
    pack_strips(2, (l, 1), (g_s, 1))
    pack_strips(3, (lh_out, 0), (lh_out, 1))
    for i in range(CX // 8):
        z_out[128 + i] = strip_out[1, 8 * i : 8 * i + 8]

    sub = iota((8, CY), 0)
    for out, top in ((b_out, core == 0), (a_out, core != 0)):
        row = jnp.where(top, 0, CX - 8)
        row = pl.multiple_of(row, 8)
        edge = pl.ds(row, 8)
        for k, field in enumerate((v, l, we, wn)):
            for s in range(2):
                out[pl.ds((2 * k + s) * LEV, LEV)] = field[s, :, edge, :]
        keep = jnp.where(top, sub, 7 - sub) < 4
        for s in range(2):
            for z in range(LEV):
                lh_edge = lh_out[s, z, edge, :]
                g_edge = pltpu.roll(g_s[s, z, edge, :], 4, 0)
                out[(8 + s) * LEV + z] = jnp.where(keep, lh_edge, g_edge)
        out[pl.ds(10 * LEV, 6)] = strip_out[:, edge, :]
    by_out[...] = b_out[10 * LEV :]


def local_kernel(cells, m, l, f, mv, v, strips, lh_out, g1_out, own_out):
    for s in range(2):
        rows, lanes = one_hots(cells[s, 0])
        lh_out[s] = l[s] + scatter(rows, lanes, m[s, 0]).reshape(LEV, CX, CY)
    g1_out[...] = f[1] - mv[1] * l[1] - v[1]
    own_out[...] = strips[...]


def obs_kernel(cells, m, v, dep, ov, rv0, rv1, rm_out, qm_out, h2_out):
    for s in range(2):
        rows, lanes = one_hots(cells[s, 0])
        seen = gather(rows, lanes, v[s].reshape(LEV * CX, CY))
        rm = dep[s, 0] - (ov[s, 0] * m[s, 0] + seen)
        rm_out[s, 0] = rm
        h2_out[s] = scatter(rows, lanes, rm).reshape(LEV, CX, CY)
        rv = rv0[0] if s == 0 else rv1[...]
        qm_out[s, 0] = ov[s, 0] * rm + gather(rows, lanes, rv.reshape(LEV * CX, CY))


class Place:
    def __init__(self):
        gx = lax.axis_index("gx")
        self.gy = lax.axis_index("gy")
        core = gx % 2
        self.b_row = pl.multiple_of(jnp.where(core == 0, TOP, TOP + HALO + CX), 8)
        self.a_row = pl.multiple_of(jnp.where(core == 0, TOP + HALO + CX, TOP), 8)
        self.core = core
        self.ay_rows = pl.ds(pl.multiple_of(core * 8, 8), 8)
        self.low = jnp.where(gx == 0, 0.0, 1.0)
        self.high = jnp.where(gx == lax.axis_size("gx") - 1, 0.0, 1.0)


def clear(ref, guard_levels):
    lead = ref.shape[:-2]
    zero = jnp.zeros(lead + (TOP, CY), F32)
    ref[..., 0:TOP, :] = zero
    ref[..., BUF - TOP : BUF, :] = zero
    if guard_levels:
        full = jnp.zeros((BUF, CY), F32)
        for i in range(lead[0]):
            ref[i, 0] = full
            ref[i, LEV + 1] = full


def fill(dst, base, place, tile, b_block, a_block):
    for z in range(LEV):
        dst[base + z, TOP + HALO : TOP + HALO + CX] = tile(z)
        dst[base + z, pl.ds(place.b_row, 8)] = b_block(z)
        dst[base + z, pl.ds(place.a_row, 8)] = a_block(z)


def unpack(place, own, received):
    half = own_half(own.shape, place.gy)
    return jnp.where(half, own, received), swap_halves(jnp.where(half, received, own))


def fill_strips(first, second, place, own, got, own_b, got_b, own_a, got_a):
    mid = pl.ds(TOP + HALO, CX)
    for where, a, b in (
        (mid, own, got),
        (pl.ds(place.b_row, 8), own_b, got_b),
        (pl.ds(place.a_row, 8), own_a, got_a),
    ):
        one, two = unpack(place, a, b)
        first[where] = one
        second[where] = two


ROWS = slice(TOP, TOP + EXT)
UP = slice(TOP + 1, TOP + EXT + 1)
DOWN = slice(TOP - 1, TOP + EXT - 1)


def inject(place, state, strip):
    lane = iota((EXT, CY), 1)
    edge = jnp.where(place.gy == 0, lane, CY - 1 - lane) >= CY - 4
    for z in range(LEV):
        moved = pltpu.roll(strip[ROWS], (120 - 16 * z) % CY, 1)
        state[z + 1, ROWS] = jnp.where(edge, moved, state[z + 1, ROWS])


def extract(place, state, strip):
    lane = iota((EXT, CY), 1)
    half = own_half((EXT, CY), place.gy)
    group = jnp.where(half, lane >> 4, LEV)
    packed = strip[ROWS]
    for z in range(LEV):
        packed = jnp.where(
            group == z, pltpu.roll(state[z + 1, ROWS], (16 * z + 8) % CY, 1), packed
        )
    strip[ROWS] = packed


def coefficients(place, wind, strip, coef, scoef, adjoint):
    lane = iota((EXT, CY), 1)
    if not adjoint:
        for z in range(LEV):
            east, north = 0.5 * wind[0, z, ROWS], 0.5 * wind[1, z, ROWS]
            coef[0, z] = DIFFUSION - east
            coef[1, z] = DIFFUSION + east
            coef[2, z] = jnp.where(lane == CY - 1, 0.0, DIFFUSION - north)
            coef[3, z] = jnp.where(lane == 0, 0.0, DIFFUSION + north)
        east, north = 0.5 * strip[0, ROWS], 0.5 * strip[1, ROWS]
        scoef[0] = DIFFUSION - east
        scoef[1] = DIFFUSION + east
        scoef[2] = DIFFUSION - north
        scoef[3] = DIFFUSION + north
        return
    for z in range(LEV):
        north = wind[1, z, ROWS]
        after = pltpu.roll(north, CY - 1, 1)
        before = pltpu.roll(north, 1, 1)
        coef[0, z] = DIFFUSION + 0.5 * wind[0, z, UP]
        coef[1, z] = DIFFUSION - 0.5 * wind[0, z, DOWN]
        coef[2, z] = jnp.where(lane == CY - 1, 0.0, DIFFUSION + 0.5 * after)
        coef[3, z] = jnp.where(lane == 0, 0.0, DIFFUSION - 0.5 * before)
    scoef[0] = DIFFUSION + 0.5 * strip[0, UP]
    scoef[1] = DIFFUSION - 0.5 * strip[0, DOWN]
    scoef[2] = DIFFUSION + 0.5 * pltpu.roll(strip[1, ROWS], CY - 1, 1)
    scoef[3] = DIFFUSION - 0.5 * pltpu.roll(strip[1, ROWS], 1, 1)


def store(dst, z, out, place):
    dst[z, TOP : TOP + HALO] = out[:HALO] * place.low
    dst[z, TOP + HALO : TOP + HALO + CX] = out[HALO : HALO + CX]
    dst[z, TOP + HALO + CX : TOP + EXT] = out[HALO + CX :] * place.high


def first_slot(count):
    return count & 1


def one_step(place, src, dst, ssrc, sdst, coef, scoef):
    lane = iota((EXT, CY), 1)
    own = ssrc[ROWS]
    for z in range(LEV):
        mid = src[z + 1, ROWS]
        after = pltpu.roll(mid, CY - 1, 1)
        before = pltpu.roll(mid, 1, 1)
        out = (
            CENTRE * mid
            + coef[0, z] * src[z + 1, UP]
            + coef[1, z] * src[z + 1, DOWN]
            + coef[2, z] * after
            + coef[3, z] * before
            + VERTICAL * (src[z + 2, ROWS] + src[z, ROWS])
        )
        store(dst, z + 1, out, place)
    above = jnp.where(lane < CY - 16, pltpu.roll(own, CY - 16, 1), 0.0)
    below = jnp.where(lane >= 16, pltpu.roll(own, 16, 1), 0.0)
    out = (
        CENTRE * own
        + scoef[0] * ssrc[UP]
        + scoef[1] * ssrc[DOWN]
        + scoef[2] * pltpu.roll(own, CY - 1, 1)
        + scoef[3] * pltpu.roll(own, 1, 1)
        + VERTICAL * (above + below)
    )
    sdst[TOP : TOP + HALO] = out[:HALO] * place.low
    sdst[TOP + HALO : TOP + HALO + CX] = out[HALO : HALO + CX]
    sdst[TOP + HALO + CX : TOP + EXT] = out[HALO + CX :] * place.high


def sweep(place, state, strip, coef, scoef, count):
    def two(i, _):
        for j in range(2):

            @pl.when(2 * i + j >= 4 - count)
            def _():
                one_step(
                    place, state.at[j], state.at[1 - j], strip.at[j, 0], strip.at[1 - j, 0],
                    coef, scoef,
                )

        return 0

    lax.fori_loop(0, 2, two, 0)
    inject(place, state.at[0], strip.at[0, 0])


STATE = pltpu.VMEM((2, LEV + 2, BUF, CY), F32)
STRIP = pltpu.VMEM((2, 1, BUF, CY), F32)
COEF = pltpu.VMEM((4, LEV, EXT, CY), F32)
SCOEF = pltpu.VMEM((4, EXT, CY), F32)
WIND = pltpu.VMEM((2, LEV, BUF, CY), F32)
WSTRIP = pltpu.VMEM((2, BUF, CY), F32)


def fill_winds(place, s, we, wn, bg, ag, own, got, by, ay, wind, wstrip):
    for k, field in enumerate((we, wn)):
        fill(
            wind.at[k], 0, place, lambda z, field=field: field[s, z],
            lambda z, k=k: bg[(4 + 2 * k + s) * LEV + z],
            lambda z, k=k: ag[(4 + 2 * k + s) * LEV + z],
        )
    p = 4 + s
    fill_strips(
        wstrip.at[0], wstrip.at[1], place, own[p], got[p],
        bg[10 * LEV + p], by[p], ag[10 * LEV + p], ay[p, place.ay_rows],
    )


def first_kernel(
    counts, v, l, we, wn, mv, lh, g1, own, got, bg, ag, by, ay,
    ext_out, rv_out, even_out, odd_out,
    x_f, x_b, s_f, s_b, coef, scoef, wind, wstrip, extra, estrip,
):
    place = Place()
    clear(x_f, True)
    clear(x_b, True)
    for ref in (s_f, s_b, wind, wstrip, extra, estrip):
        clear(ref, False)

    def strips(p, first, second):
        fill_strips(
            first, second, place, own[p], got[p],
            bg[10 * LEV + p], by[p], ag[10 * LEV + p], ay[p, place.ay_rows],
        )

    fill_winds(place, 0, we, wn, bg, ag, own, got, by, ay, wind, wstrip)
    fill(
        x_b.at[first_slot(counts[0])], 1, place, lambda z: l[1, z],
        lambda z: bg[3 * LEV + z], lambda z: ag[3 * LEV + z],
    )
    strips(2, s_b.at[first_slot(counts[0]), 0], estrip.at[1])
    coefficients(place, wind, wstrip, coef, scoef, True)
    sweep(place, x_b, s_b, coef, scoef, counts[0])
    end = 0
    fill(
        extra.at[0], 0, place, lambda z: lh[0, z],
        lambda z: bg[8 * LEV + z], lambda z: ag[8 * LEV + z],
    )
    fill(
        extra.at[1], 0, place, lambda z: g1[z],
        lambda z: pltpu.roll(bg[9 * LEV + z], 4, 0),
        lambda z: pltpu.roll(ag[9 * LEV + z], 4, 0),
    )
    for z in range(LEV):
        rv = x_b[end, z + 1, ROWS] - extra[0, z, ROWS]
        ext_out[0, z] = rv
        rv_out[0, z] = rv[HALO : HALO + CX]
        rv_out[1, z] = mv[0, z]
    strips(3, estrip.at[0], s_f.at[0, 0])
    ext_out[0, LEV] = s_b[end, 0, ROWS] - estrip[0, ROWS]

    for s in range(2):
        if s == 1:
            fill_winds(place, 1, we, wn, bg, ag, own, got, by, ay, wind, wstrip)
        coefficients(place, wind, wstrip, coef, scoef, False)
        fill(
            x_f.at[first_slot(counts[s])], 1, place, lambda z, s=s: v[s, z],
            lambda z, s=s: bg[s * LEV + z], lambda z, s=s: ag[s * LEV + z],
        )
        if s == 0:
            strips(0, s_f.at[first_slot(counts[s]), 0], estrip.at[0])
        else:
            strips(0, estrip.at[0], s_f.at[first_slot(counts[s]), 0])
        sweep(place, x_f, s_f, coef, scoef, counts[s])
        for z in range(LEV):
            out = x_f[end, z + 1, ROWS]
            if s == 0:
                ext_out[1, z] = out + extra[1, z, ROWS]
            else:
                ext_out[2, z] = out
        out = s_f[end, 0, ROWS]
        ext_out[1 + s, LEV] = out + estrip[1, ROWS] if s == 0 else out

    tile = slice(HALO, HALO + CX)
    odd = lax.axis_index("tm") % 2

    @pl.when(odd == 0)
    def _():
        even_out[0] = ext_out[2, :LEV, tile]
        even_out[1] = rv_out[1]
        odd_out[...] = rv_out[...]

    @pl.when(odd == 1)
    def _():
        even_out[...] = rv_out[...]
        odd_out[0] = ext_out[2, :LEV, tile]
        odd_out[1] = rv_out[1]


def lane_sum(x):
    return functools.reduce(
        lambda a, b: a + b, [x[:, i : i + CY] for i in range(0, x.shape[1], CY)]
    )


def second_kernel(
    counts, ext, we, wn, lh, own, got, bg, ag, by, ay, zt, zh,
    mv,
    rv1_out, rl1_out, rl2_out, f21_out, b20_out, ql1_out, b21_out, dots_out,
    x_f, x_b, s_f, s_b, coef, scoef, wind, wstrip, extra, estrip,
):
    place = Place()
    clear(x_f, True)
    clear(x_b, True)
    for ref in (s_f, s_b, wind, wstrip, extra, estrip):
        clear(ref, False)
    tile = slice(HALO, HALO + CX)
    follows = jnp.where(lax.axis_index("tm") == lax.axis_size("tm") - 1, 0.0, 1.0)

    fill_winds(place, 1, we, wn, bg, ag, own, got, by, ay, wind, wstrip)
    coefficients(place, wind, wstrip, coef, scoef, True)

    def z_tile(base):
        return lambda z: zt[base + 8 * z : base + 8 * z + 8].reshape(CX, CY)

    fill(x_b.at[first_slot(counts[1])], 1, place, z_tile(0), lambda z: zh[z], lambda z: zh[16 + z])
    fill(
        extra.at[1], 0, place, z_tile(64),
        lambda z: pltpu.roll(zh[8 + z], 4, 0), lambda z: pltpu.roll(zh[24 + z], 4, 0),
    )
    fill_strips(
        s_b.at[first_slot(counts[1]), 0], estrip.at[1], place,
        zt[128:136].reshape(CX, CY), zh[37:45].reshape(CX, CY),
        zh[32], zh[33], zh[34], zh[35 + place.core],
    )
    sweep(place, x_b, s_b, coef, scoef, counts[1])
    end = 0
    slot = first_slot(counts[1])

    fill(
        extra.at[0], 0, place, lambda z: lh[1, z],
        lambda z: bg[9 * LEV + z], lambda z: ag[9 * LEV + z],
    )
    fill_strips(
        s_f.at[0, 0], estrip.at[0], place, own[3], got[3],
        bg[10 * LEV + 3], by[3], ag[10 * LEV + 3], ay[3, place.ay_rows],
    )
    for z in range(LEV):
        rv = x_b[end, z + 1, ROWS] - extra[0, z, ROWS]
        x_f[slot, z + 1, ROWS] = rv
        rv1_out[z] = rv[tile]
        rl = (extra[1, z, ROWS] + ext[2, z]) * follows
        x_b[slot, z + 1, ROWS] = rl
        rl2_out[z] = rl[tile]
    s_f[slot, 0, ROWS] = s_b[end, 0, ROWS] - estrip[0, ROWS]
    s_b[slot, 0, ROWS] = (estrip[1, ROWS] + ext[2, LEV]) * follows
    extract(place, x_f.at[slot], s_f.at[slot, 0])
    extract(place, x_b.at[slot], s_b.at[slot, 0])

    sweep(place, x_b, s_b, coef, scoef, counts[1])
    cross = jnp.zeros((8, CY), F32)
    square = jnp.zeros((8, CY), F32)

    def dots(r, q):
        return jnp.sum((r * q).reshape(-1, 8, CY), 0), jnp.sum((q * q).reshape(-1, 8, CY), 0)

    for z in range(LEV):
        rl1 = ext[1, z, tile]
        rl1_out[z] = rl1
        b21_out[z] = x_b[end, z + 1, TOP + HALO : TOP + HALO + CX]
    coefficients(place, wind, wstrip, coef, scoef, False)
    sweep(place, x_f, s_f, coef, scoef, counts[1])
    for z in range(LEV):
        f21_out[z] = x_f[end, z + 1, TOP + HALO : TOP + HALO + CX]

    slot = first_slot(counts[0])
    fill_winds(place, 0, we, wn, bg, ag, own, got, by, ay, wind, wstrip)
    coefficients(place, wind, wstrip, coef, scoef, False)
    for z in range(LEV):
        x_f[slot, z + 1, ROWS] = ext[0, z]
        x_b[slot, z + 1, ROWS] = ext[1, z]
    s_f[slot, 0, ROWS] = ext[0, LEV]
    s_b[slot, 0, ROWS] = ext[1, LEV]
    extract(place, x_f.at[slot], s_f.at[slot, 0])
    extract(place, x_b.at[slot], s_b.at[slot, 0])
    sweep(place, x_f, s_f, coef, scoef, counts[0])
    for z in range(LEV):
        rl1 = ext[1, z, tile]
        ql = mv[1, z] * rl1 + rv1_out[z] - x_f[end, z + 1, TOP + HALO : TOP + HALO + CX]
        ql1_out[z] = ql
        c, q = dots(rl1, ql)
        cross, square = cross + c, square + q
    coefficients(place, wind, wstrip, coef, scoef, True)
    sweep(place, x_b, s_b, coef, scoef, counts[0])
    for z in range(LEV):
        b20_out[z] = x_b[end, z + 1, TOP + HALO : TOP + HALO + CX]

    dots_out[0] = cross
    dots_out[1] = square


def dots_kernel(
    even, odd, rl2, f21, b20, z_own, h2, rv0, dots_in, rl1, rv1, b21, ql1, qm, rm, m,
    keep_out, send_out,
):
    follows = jnp.where(lax.axis_index("tm") == lax.axis_size("tm") - 1, 0.0, 1.0)
    starts = jnp.where(lax.axis_index("tm") == 0, 1.0, 0.0)
    for i, kept in enumerate((rm, qm, m)):
        for s in range(2):
            for k in range(m.shape[-1] // CY):
                keep_out[6, 2 * i + s, k : k + 1] = kept[s, 0, :, k * CY : (k + 1) * CY]
    rm_rows, qm_rows = keep_out[6, 0:2, 0:8], keep_out[6, 2:4, 0:8]
    cross = dots_in[0] + jnp.sum(rm_rows * qm_rows, 0)
    square = dots_in[1] + jnp.sum(qm_rows * qm_rows, 0)
    is_odd = lax.axis_index("tm") % 2 == 1

    def total(x):
        return jnp.sum(x.reshape(-1, 8, CY), 0)

    for z in range(LEV):
        rl0 = z_own[64 + 8 * z : 72 + 8 * z].reshape(CX, CY) + jnp.where(is_odd, even[0, z], odd[0, z])
        rv = rv0[0, z]
        qv = rl0 - b20[z] + h2[0, z]
        qv1 = rl1[z] - b21[z] + h2[1, z]
        for i, kept in enumerate((rl0, rl1[z], rv1[z], qv, qv1, ql1[z])):
            keep_out[i, z] = kept
        cross += total(rv1[z] * qv1)
        square += total(qv1 * qv1)
        ql = (rv0[1, z] * rl0 + rv) * starts
        rl2z = rl2[z]
        next_mv = jnp.where(is_odd, odd[1, z], even[1, z])
        next_rv = jnp.where(is_odd, odd[0, z], even[0, z])
        q2 = (next_mv * rl2z + next_rv - f21[z]) * follows
        cross += total(rv * qv) + total(rl0 * ql) + total(rl2z * q2)
        square += total(qv * qv) + total(ql * ql) + total(q2 * q2)
    cross = jnp.sum(jnp.sum(cross, 0, keepdims=True), 1, keepdims=True)
    square = jnp.sum(jnp.sum(square, 0, keepdims=True), 1, keepdims=True)
    n = send_out.shape[0]
    lane = iota((n, CY), 1)
    send_out[...] = jnp.where(lane == 0, cross, jnp.where(lane == 1, square, 0.0))


def last_kernel(
    sums, l, v, rv0, z_f2, keep,
    l_out, m_out, v_out, a_out, b_out, c_out,
):
    total = jnp.sum(sums[...], 0, keepdims=True)
    lane = iota((1, CY), 1)
    cross = jnp.sum(jnp.where(lane == 0, total, 0.0), 1, keepdims=True)
    square = jnp.sum(jnp.where(lane == 1, total, 0.0), 1, keepdims=True)
    alpha = cross / (square + 1e-06)
    for s in range(2):
        for k in range(m_out.shape[-1] // CY):
            rm, qm, m = (keep[6, 2 * i + s, k : k + 1] for i in range(3))
            m_out[s, 0, :, k * CY : (k + 1) * CY] = m + alpha * rm
            b_out[s, 0, :, k * CY : (k + 1) * CY] = rm - alpha * qm
    for z in range(LEV):
        rl0, rl1, rv1, qv0, qv1, ql1 = (keep[i, z] for i in range(6))
        ql0 = rv0[1, z] * rl0 + rv0[0, z] - z_f2[z]
        l_out[0, z] = l[0, z] + alpha * rl0
        l_out[1, z] = l[1, z] + alpha * rl1
        v_out[0, z] = v[0, z] + alpha * rv0[0, z]
        v_out[1, z] = v[1, z] + alpha * rv1
        a_out[0, z] = rl0 - alpha * ql0
        a_out[1, z] = rl1 - alpha * ql1
        c_out[0, z] = rv0[0, z] - alpha * qv0
        c_out[1, z] = rv1 - alpha * qv1


def shards(sizes, l4, m4, v4, f4, d4, mv4, ov4, we4, wn4, cells4, counts):
    ntm, ngx, ngy = sizes
    tile = (LEV, CX, CY)
    obs = m4.shape

    def pair_b(i):
        return i - 1 if i % 2 == 0 else i + 1

    def plane(move_x, move_y):
        pairs = []
        for x in range(ngx):
            for y in range(ngy):
                to = move_x(x)
                if 0 <= to < ngx:
                    pairs.append((x * ngy + y, to * ngy + (1 - y if move_y else y)))
        return pairs

    axes = ("gx", "gy")
    down = [(i + 1, i) for i in range(ntm - 1)]
    up = [(i, i + 1) for i in range(ntm - 1)]
    edge = 10 * LEV

    fields = pltpu.VMEM((2,) + tile, F32)
    b_send, a_send, by_send, strips, z_send = call(
        pack_kernel,
        [(NBLOCKS, 8, CY)] * 2 + [(6, 8, CY), (6, CX, CY), (136, 8, CY)],
        [cells4, m4, v4, we4, wn4, l4, f4, mv4],
        [fields, fields, pltpu.VMEM(obs, jnp.int32), pltpu.VMEM(obs, F32)]
        + [fields] * 6
        + [pltpu.SemaphoreType.DMA((8,))],
        micros=2.5,
        fetched=range(8),
        limit=PACK_LIMIT,
    )
    got = lax.ppermute(strips, axes, plane(lambda i: i, True))
    bg = lax.ppermute(b_send, axes, plane(pair_b, False))
    ag = lax.ppermute(a_send, axes, plane(lambda i: i ^ 1, False))
    zt = lax.ppermute(z_send, "tm", down)
    ay_send = jnp.concatenate([got[:, :8], got[:, CX - 8 :]], 1)
    ay_send, by_send = lax.optimization_barrier((ay_send, by_send))
    by = lax.ppermute(by_send, axes, plane(pair_b, True))
    ay = lax.ppermute(ay_send, axes, plane(lambda i: i ^ 1, False))

    lh, g1, own = call(
        local_kernel,
        [(2,) + tile, tile, strips.shape],
        [cells4, m4, l4, f4, mv4, v4, strips],
        micros=1.0,
    )
    z_edges = jnp.concatenate(
        [
            bg[2 * LEV : 3 * LEV], bg[8 * LEV : 9 * LEV],
            ag[2 * LEV : 3 * LEV], ag[8 * LEV : 9 * LEV],
            bg[edge + 1 : edge + 2], by[1:2], ag[edge + 1 : edge + 2],
            ay[1].reshape(2, 8, CY), got[1].reshape(8, 8, CY),
        ],
        0,
    )
    zh = lax.ppermute(z_edges, "tm", down)
    scratch = [
        STATE, STATE, STRIP, STRIP, COEF, SCOEF, WIND, WSTRIP,
        pltpu.VMEM((2, LEV, BUF, CY), F32), pltpu.VMEM((2, BUF, CY), F32),
    ]
    ext, rv0, even_send, odd_send = call(
        first_kernel,
        [(3, LEV + 1, EXT, CY)] + [(2,) + tile] * 3,
        [counts, v4, l4, we4, wn4, mv4, lh, g1, own, got, bg, ag, by, ay],
        scratch,
        micros=5.0,
    )
    swap = lambda first: [(i, i + 1) for i in range(first, ntm - 1, 2)] + [
        (i + 1, i) for i in range(first, ntm - 1, 2)
    ]
    even = lax.ppermute(even_send, "tm", swap(0))
    odd = lax.ppermute(odd_send, "tm", swap(1))
    rv1, rl1, rl2, f21, b20, ql1, b21, dots = call(
        second_kernel,
        [tile] * 7 + [(2, 8, CY)],
        [counts, ext, we4, wn4, lh, own, got, bg, ag, by, ay, zt, zh, mv4],
        scratch,
        micros=9.0,
    )
    z_f2 = lax.ppermute(f21, "tm", up)
    rm, qm, h2 = call(
        obs_kernel, [obs, obs, (2,) + tile], [cells4, m4, v4, d4, ov4, rv0, rv1], micros=3.4
    )
    n = ntm * ngx * ngy
    keep, send = call(
        dots_kernel,
        [(7,) + tile, (n, CY)],
        [even, odd, rl2, f21, b20, z_send, h2, rv0, dots, rl1, rv1, b21, ql1, qm, rm, m4],
        micros=0.4,
    )
    sums = lax.all_to_all(send, ("tm", "gx", "gy"), 0, 0, tiled=True)
    return call(
        last_kernel,
        [l4.shape, obs, l4.shape, l4.shape, obs, l4.shape],
        [sums, l4, v4, rv0, z_f2, keep],
        micros=1.5,
    )


def solution(mesh):
    field = P("tm", None, "gx", "gy")
    obs = P("tm", "gx", "gy", None)
    sizes = tuple(mesh.shape[a] for a in ("tm", "gx", "gy"))
    return jax.shard_map(
        functools.partial(shards, sizes),
        mesh=mesh,
        in_specs=(field, obs, field, field, obs, field, obs, field, field, obs, P("tm")),
        out_specs=(field, obs, field, field, obs, field),
        check_vma=False,
    )
```
